32 devices in a mesh: dp: 16 (over z, y, x), tensor: 2 (over core).
Axes of the slice: x: 2, y: 2, z: 4, core: 2. Of those that a mesh axis runs over, the one named last changes fastest.
Arguments:
- square_grad: float32 [8, 2359296], P(None, ('dp', 'tensor')), may hold values from -80 to 80
- square_state: float32 [8, 2359296], P(None, ('dp', 'tensor')), may hold values from -6 to 6
- swiglu_grad: float32 [6, 6291456], P(None, ('dp', 'tensor')), may hold values from -80 to 80
- swiglu_state: float32 [6, 6291456], P(None, ('dp', 'tensor')), may hold values from -6 to 6
- square_order: int32 [8], replicated, may hold values from 0 to 7, each once
- swiglu_order: int32 [6], replicated, may hold values from 0 to 5, each once
- owners: int32 [14], replicated, may hold values from 0 to 15, as said below
- vector_values: float32 [43008], P(('dp', 'tensor')), may hold values from -6 to 6
- vector_grad: float32 [43008], P(('dp', 'tensor')), may hold values from -6 to 6
- vector_first: float32 [43008], P(('dp', 'tensor')), may hold values from -4 to 4
- vector_second: float32 [43008], P(('dp', 'tensor')), may hold values from 0.01 to 1
- embed_values: float32 [2048, 1536], P('dp', 'tensor'), may hold values from -6 to 6
- embed_grad: float32 [2048, 1536], P('dp', 'tensor'), may hold values from -6 to 6
- embed_first: float32 [2048, 1536], P('dp', 'tensor'), may hold values from -4 to 4
- embed_second: float32 [2048, 1536], P('dp', 'tensor'), may hold values from 0.01 to 1
- embed_ranges: int32 [16, 2], replicated, may hold values from 0 to 2048, as said below
Outputs:
- square_next: float32 [8, 2359296], P(None, ('dp', 'tensor'))
- swiglu_next: float32 [6, 6291456], P(None, ('dp', 'tensor'))
- square_update: bfloat16 [8, 1536, 1536], P(None, 'dp', 'tensor')
- swiglu_update: bfloat16 [6, 1536, 4096], P(None, 'dp', 'tensor')
- owner_norms: float32 [16], P('dp')
- vector_step: float32 [43008], P(('dp', 'tensor'))
- first_vector: float32 [43008], P(('dp', 'tensor'))
- second_vector: float32 [43008], P(('dp', 'tensor'))
- embed_step: float32 [2048, 1536], P('dp', 'tensor')
- first_embed: float32 [2048, 1536], P('dp', 'tensor')
- second_embed: float32 [2048, 1536], P('dp', 'tensor')
The draws below stay inside these ranges and needn't reach their ends.
Inputs may be any that keep to these rules, and one draw needn't show every extreme that they name: Different matrices have different owners. `square_order`: each matrix once. `swiglu_order`: each matrix once. `embed_ranges`: start < end in every row.
All inputs are finite; a program needn't handle non-finite values.
Results may differ from the reference program's by a relative error of at most 0.0065.
Values may be sent and summed in bfloat16 or wider, within the bound.
No kernel may reach another device: no remote copies, remote signals or barrier semaphores. Data moves between devices by JAX's collectives and lax.ppermute only.
A program may use at most 128 MiB of HBM per device.

```python
import math
import jax
import jax.numpy as jnp
from jax import lax

D = 1536
FF = 4096
NS_STEPS = 2
NRANGE = 16
SQ = 8
ML = 6
MATS = 14
OWNERS = 16
EMB_ROWS = 2048
VEC = 43008


def matrix_grads(key, count, rows, width):
    keys = jax.random.split(key, 3)
    row_scale = jnp.exp(jax.random.uniform(keys[0], (count, rows, 1), jnp.float32, 0.0, math.log(10.0)))
    row_scale = row_scale * jnp.exp(math.log(3.0) * jnp.arange(rows, dtype=jnp.float32) / rows)[None, :, None]
    col_scale = jnp.exp(jax.random.uniform(keys[1], (count, 1, width), jnp.float32, 0.0, math.log(10.0)))
    base = jnp.clip(jax.random.normal(keys[2], (count, rows, width), jnp.float32), -5.0, 5.0)
    values = base * row_scale * col_scale / 30.0
    return values.reshape(count, rows * width)


def draw_square_grad(key, part):
    return matrix_grads(jax.random.fold_in(key, 11), SQ, D, D)


def draw_swiglu_grad(key, part):
    return matrix_grads(jax.random.fold_in(key, 23), ML, D, FF)


def draw_owners(key, part):
    keys = jax.random.split(jax.random.fold_in(key, 37), 2)
    middle = jax.random.permutation(keys[0], jnp.arange(1, OWNERS - 1, dtype=jnp.int32))
    listed = jnp.concatenate([jnp.array([0, OWNERS - 1], jnp.int32), middle])[:MATS]
    return jax.random.permutation(keys[1], listed).astype(jnp.int32)


def draw_embed_ranges(key, part):
    keys = jax.random.split(jax.random.fold_in(key, 53), 2)
    lengths = jax.random.randint(keys[0], (NRANGE,), 1, EMB_ROWS // 8 + 1)
    starts = jax.random.randint(keys[1], (NRANGE,), 0, EMB_ROWS - lengths + 1)
    starts = starts.at[0].set(0)
    starts = starts.at[1].set(EMB_ROWS - lengths[1])
    return jnp.stack([starts, starts + lengths], axis=1).astype(jnp.int32)


def level_of(own_key, dims, cuts, smallest, top_value):
    loudness = 1.0
    for axis_at, parts in cuts:
        steps = jax.random.uniform(jax.random.fold_in(jax.random.fold_in(own_key, 6), axis_at), (parts,), jnp.float32, smallest / len(cuts), top_value / len(cuts))
        loudness = loudness * jnp.repeat(jnp.exp(steps), dims[axis_at] // parts).reshape((-1,) + (1,) * (len(dims) - 1 - axis_at))
    return loudness


def noise(stream_key, extent, deviation, reach, cuts=(), kind=jnp.bfloat16):
    result = jax.random.normal(stream_key, extent, jnp.float32) * deviation
    if len(cuts) > 0:
        result = level_of(stream_key, extent, cuts, -0.22, 0.18) * result
    return jnp.clip(result, min=-reach, max=reach).astype(kind)


def setup_inputs(seed: int = 0) -> dict:
    seeds = jax.random.split(jax.random.key(seed), 17)
    square_grad = draw_square_grad(jax.random.fold_in(seeds[16], 71), 0)
    square_state = noise(seeds[1], (SQ, D * D), 1.0, 6.0, ((1, 32),), jnp.float32)
    swiglu_grad = draw_swiglu_grad(jax.random.fold_in(seeds[16], 71), 0)
    swiglu_state = noise(seeds[3], (ML, D * FF), 1.0, 6.0, ((1, 32),), jnp.float32)
    square_order = jax.random.permutation(seeds[4], SQ).astype(jnp.int32)
    swiglu_order = jax.random.permutation(seeds[5], ML).astype(jnp.int32)
    owners = draw_owners(jax.random.fold_in(seeds[16], 71), 0)
    vector_values = noise(seeds[7], (VEC,), 1.0, 6.0, ((0, 32),), jnp.float32)
    vector_grad = noise(seeds[8], (VEC,), 1.0, 6.0, ((0, 32),), jnp.float32)
    vector_first = noise(seeds[9], (VEC,), 0.3, 4.0, ((0, 32),), jnp.float32)
    vector_second = jnp.clip(jnp.exp(math.log(1.0) - 4.6051702 * jax.random.uniform(seeds[10], (VEC,), jnp.float32) ** level_of(seeds[10], (VEC,), ((0, 32),), -0.2, 0.2)), 0.01, 1.0)
    embed_values = noise(seeds[11], (EMB_ROWS, D), 1.0, 6.0, ((0, 16), (1, 2)), jnp.float32)
    embed_grad = noise(seeds[12], (EMB_ROWS, D), 1.0, 6.0, ((0, 16), (1, 2)), jnp.float32)
    embed_first = noise(seeds[13], (EMB_ROWS, D), 0.3, 4.0, ((0, 16), (1, 2)), jnp.float32)
    embed_second = jnp.clip(jnp.exp(math.log(1.0) - 4.6051702 * jax.random.uniform(seeds[14], (EMB_ROWS, D), jnp.float32) ** level_of(seeds[14], (EMB_ROWS, D), ((0, 16), (1, 2)), -0.2, 0.2)), 0.01, 1.0)
    embed_ranges = draw_embed_ranges(jax.random.fold_in(seeds[16], 71), 0)
    return {"square_grad": square_grad, "square_state": square_state, "swiglu_grad": swiglu_grad, "swiglu_state": swiglu_state, "square_order": square_order, "swiglu_order": swiglu_order, "owners": owners, "vector_values": vector_values, "vector_grad": vector_grad, "vector_first": vector_first, "vector_second": vector_second, "embed_values": embed_values, "embed_grad": embed_grad, "embed_first": embed_first, "embed_second": embed_second, "embed_ranges": embed_ranges}


QUINTIC_LINEAR = 3.4445
QUINTIC_CUBIC = -4.775
QUINTIC_FIFTH = 2.0315
MOMENTUM = 0.95
BIAS_FIRST = 1.0 - 0.9 ** 10
BIAS_SECOND = 1.0 - 0.95 ** 10

def orthogonalize(slot_matrix, factor):
    iterate = slot_matrix
    first_scale = jnp.float32(1.0)
    for round_index in range(NS_STEPS):
        gram = jnp.dot(iterate, iterate.T, preferred_element_type=jnp.float32)
        if round_index == 0:
            gram_scale = jnp.sqrt(jnp.sum(gram * gram)) + 1e-06
            first_scale = gram_scale
        else:
            gram_scale = jnp.float32(1.0)
        normed = (gram / gram_scale).astype(jnp.bfloat16)
        squared = jnp.dot(normed, normed, preferred_element_type=jnp.float32)
        polynomial = (QUINTIC_CUBIC * normed.astype(jnp.float32) + QUINTIC_FIFTH * squared).astype(jnp.bfloat16)
        product = jnp.dot(polynomial, iterate, preferred_element_type=jnp.float32)
        mixed = (QUINTIC_LINEAR * iterate.astype(jnp.float32) + product) / jnp.sqrt(gram_scale)
        if round_index == NS_STEPS - 1:
            iterate = (factor * mixed).astype(jnp.bfloat16)
        else:
            iterate = mixed.astype(jnp.bfloat16)
    return (iterate, first_scale)

def square_run(matrix):
    return orthogonalize(matrix, math.sqrt(D))

def swiglu_run(matrix):
    return orthogonalize(matrix, math.sqrt(FF))

def momentum_terms(gradient, state):
    state_next = MOMENTUM * state + gradient
    return (state_next, (gradient + MOMENTUM * state_next).astype(jnp.bfloat16))

def canonical(slots, order, count):
    inverse = jnp.zeros((count,), jnp.int32).at[order].set(jnp.arange(count, dtype=jnp.int32))
    return slots[inverse]

def adamw_terms(values, gradient, first, second):
    first_next = 0.9 * first + 0.1 * gradient
    second_next = 0.95 * second + 0.05 * gradient * gradient
    direction = first_next / BIAS_FIRST / (jnp.sqrt(second_next / BIAS_SECOND) + 1e-08) + 0.1 * values
    return (direction, first_next, second_next)

def reference(square_grad, square_state, swiglu_grad, swiglu_state, square_order, swiglu_order, owners, vector_values, vector_grad, vector_first, vector_second, embed_values, embed_grad, embed_first, embed_second, embed_ranges):
    square_next, square_send = momentum_terms(square_grad, square_state)
    swiglu_next, swiglu_send = momentum_terms(swiglu_grad, swiglu_state)
    square_mats = canonical(square_send, square_order, SQ).reshape(SQ, D, D)
    swiglu_mats = canonical(swiglu_send, swiglu_order, ML).reshape(ML, D, FF)
    square_update, square_scale = lax.map(square_run, square_mats)
    swiglu_update, swiglu_scale = lax.map(swiglu_run, swiglu_mats)
    all_scales = jnp.concatenate([square_scale, swiglu_scale])
    owner_norms = jnp.zeros((OWNERS,), jnp.float32).at[owners].set(0.5 * jnp.log(all_scales))
    vector_step, first_vector, second_vector = adamw_terms(vector_values, vector_grad, vector_first, vector_second)
    row_numbers = jnp.arange(EMB_ROWS, dtype=jnp.int32)[:, None]
    inside = (row_numbers >= embed_ranges[None, :, 0]) & (row_numbers < embed_ranges[None, :, 1])
    row_live = lax.optimization_barrier(jnp.sum(inside.astype(jnp.int32), axis=1)) > 0
    direction, first_next, second_next = adamw_terms(embed_values, embed_grad, embed_first, embed_second)
    embed_step = jnp.where(row_live[:, None], direction, 0.0)
    first_embed = jnp.where(row_live[:, None], first_next, embed_first)
    second_embed = jnp.where(row_live[:, None], second_next, embed_second)
    return (square_next, swiglu_next, square_update, swiglu_update, owner_norms, vector_step, first_vector, second_vector, embed_step, first_embed, second_embed)
```

```python
import math

import jax
import jax.numpy as jnp
import numpy as np
from jax import lax
from jax.sharding import PartitionSpec as P

D = 1536
FF = 4096
NS_STEPS = 2


QUINTIC_LINEAR = 3.4445
QUINTIC_CUBIC = -4.775
QUINTIC_FIFTH = 2.0315
MOMENTUM = 0.95
BIAS_FIRST = 1.0 - 0.9**10
BIAS_SECOND = 1.0 - 0.95**10


def momentum_terms(gradient, state):
    state_next = MOMENTUM * state + gradient
    return (state_next, (gradient + MOMENTUM * state_next).astype(jnp.bfloat16))


def adamw_terms(values, gradient, first, second):
    first_next = 0.9 * first + 0.1 * gradient
    second_next = 0.95 * second + 0.05 * gradient * gradient
    direction = (
        first_next / BIAS_FIRST / (jnp.sqrt(second_next / BIAS_SECOND) + 1e-08) + 0.1 * values
    )
    return (direction, first_next, second_next)


def placement(chips, heavy_count, light_count):
    planes = 4
    per = chips // planes
    order = []
    for inner in range(planes // 2 - 1, -1, -1):
        for k in range(per):
            order += [inner * per + k, (planes - 1 - inner) * per + k]
    heavy = order[:heavy_count]
    light = order[heavy_count : heavy_count + light_count]
    return heavy, light


def exchange(blocks, pairs):
    return lax.ppermute(blocks, "dp", pairs)


def other_core(x):
    return lax.ppermute(x, "tensor", [(0, 1), (1, 0)])


def inverse_of(order):
    count = order.shape[0]
    match = order[None, :] == jnp.arange(count, dtype=jnp.int32)[:, None]
    return jnp.sum(jnp.where(match, jnp.arange(count, dtype=jnp.int32)[None, :], 0), axis=1)


def local(
    square_grad,
    square_state,
    swiglu_grad,
    swiglu_state,
    square_order,
    swiglu_order,
    owners,
    vector_values,
    vector_grad,
    vector_first,
    vector_second,
    embed_values,
    embed_grad,
    embed_first,
    embed_second,
    embed_ranges,
):
    chips = lax.axis_size("dp")
    cores = lax.axis_size("tensor")
    chip = lax.axis_index("dp")
    square_count = square_grad.shape[0]
    swiglu_count = swiglu_grad.shape[0]
    flat_rows = D // (chips * cores)
    chip_rows = D // chips
    narrow = D // cores
    wide = FF // cores
    heavy, light = placement(chips, swiglu_count, square_count)
    is_heavy = np.zeros((chips,), np.bool_)
    is_heavy[heavy] = True
    is_light = np.zeros((chips,), np.bool_)
    is_light[light] = True
    is_owner = is_heavy | is_light
    slot_of = np.zeros((chips,), np.int32)
    for j, o in enumerate(heavy):
        slot_of[o] = j
    for j, o in enumerate(light):
        slot_of[o] = swiglu_count + j

    square_next, square_send = momentum_terms(square_grad, square_state)
    swiglu_next, swiglu_send = momentum_terms(swiglu_grad, swiglu_state)
    square_rows = lax.all_to_all(
        square_send.reshape(square_count, flat_rows, D), "tensor", split_axis=2, concat_axis=1, tiled=True
    )
    swiglu_rows = lax.all_to_all(
        swiglu_send.reshape(swiglu_count, flat_rows, FF), "tensor", split_axis=2, concat_axis=1, tiled=True
    )
    first_part = jnp.concatenate([swiglu_rows[:, :, :narrow], square_rows], axis=0)
    second_part = swiglu_rows[:, :, narrow:]

    partner = chip ^ jnp.arange(chips, dtype=jnp.int32)
    slot_table = jnp.asarray(slot_of)[partner]
    heavy_table = jnp.minimum(slot_table, swiglu_count - 1)
    first_blocks = []
    second_blocks = []
    for r in range(chips):
        block = lax.dynamic_index_in_dim(first_part, slot_table[r], 0, keepdims=False)
        if r:
            block = exchange(block, [(s, s ^ r) for s in range(chips) if is_owner[s ^ r]])
        first_blocks.append(block)
        block = lax.dynamic_index_in_dim(second_part, heavy_table[r], 0, keepdims=False)
        if r:
            block = exchange(block, [(s, s ^ r) for s in range(chips) if is_heavy[s ^ r]])
        else:
            block = jnp.where(jnp.asarray(is_heavy)[chip], block, jnp.zeros((), jnp.bfloat16))
        second_blocks.append(block)
    matrix = jnp.concatenate(
        [jnp.concatenate(first_blocks, axis=0), jnp.concatenate(second_blocks, axis=0)], axis=1
    )

    heavy_here = jnp.asarray(is_heavy)[chip]
    factor = jnp.where(heavy_here, jnp.float32(math.sqrt(FF)), jnp.float32(math.sqrt(D)))
    iterate = matrix
    first_scale = jnp.float32(1.0)
    for round_index in range(NS_STEPS):
        gram_part = jnp.einsum("rc,sc->rs", iterate, iterate, preferred_element_type=jnp.float32)
        gram = gram_part + other_core(gram_part)
        if round_index == 0:
            gram_scale = jnp.sqrt(jnp.sum(gram * gram)) + 1e-06
            first_scale = gram_scale
        else:
            gram_scale = jnp.float32(1.0)
        normed = (gram / gram_scale).astype(jnp.bfloat16)
        squared = jnp.dot(normed, normed, preferred_element_type=jnp.float32)
        polynomial = (
            QUINTIC_CUBIC * normed.astype(jnp.float32) + QUINTIC_FIFTH * squared
        ).astype(jnp.bfloat16)
        if round_index < NS_STEPS - 1:
            product = jnp.dot(polynomial, iterate, preferred_element_type=jnp.float32)
            mixed = (QUINTIC_LINEAR * iterate.astype(jnp.float32) + product) / jnp.sqrt(gram_scale)
            iterate = mixed.astype(jnp.bfloat16)
    first_back = []
    second_back = []
    group = max(1, chips // 4)
    for g in range(0, chips, group):
        rows = slice(g * chip_rows, (g + group) * chip_rows)
        product = jnp.dot(polynomial[rows], iterate, preferred_element_type=jnp.float32)
        mixed = QUINTIC_LINEAR * iterate[rows].astype(jnp.float32) + product
        final = (factor * mixed).astype(jnp.bfloat16)
        for r in range(g, g + group):
            part = final[(r - g) * chip_rows : (r - g + 1) * chip_rows]
            block = part[:, :narrow]
            if r:
                block = exchange(block, [(s, s ^ r) for s in range(chips) if is_owner[s]])
            first_back.append(block)
            block = part[:, narrow:]
            if r:
                block = exchange(block, [(s, s ^ r) for s in range(chips) if is_heavy[s]])
            second_back.append(block)

    chip_of_square = jnp.asarray(np.array(light, np.int32))[inverse_of(square_order)]
    chip_of_swiglu = jnp.asarray(np.array(heavy, np.int32))[inverse_of(swiglu_order)]
    first_all = jnp.stack(first_back)
    second_all = jnp.stack(second_back)
    square_update = first_all[chip_of_square ^ chip]
    swiglu_update = jnp.concatenate(
        [first_all[chip_of_swiglu ^ chip], second_all[chip_of_swiglu ^ chip]], axis=2
    )

    logs = lax.all_gather(0.5 * jnp.log(first_scale), "dp")
    matrix_chip = jnp.concatenate([chip_of_square, chip_of_swiglu])
    owner_norms = jnp.sum(jnp.where(owners == chip, logs[matrix_chip], 0.0)).reshape(1)

    vector_step, first_vector, second_vector = adamw_terms(
        vector_values, vector_grad, vector_first, vector_second
    )
    embed_rows = embed_values.shape[0]
    row_numbers = chip * embed_rows + jnp.arange(embed_rows, dtype=jnp.int32)
    inside = (row_numbers[:, None] >= embed_ranges[None, :, 0]) & (
        row_numbers[:, None] < embed_ranges[None, :, 1]
    )
    row_live = jnp.sum(inside.astype(jnp.int32), axis=1) > 0
    direction, first_next, second_next = adamw_terms(
        embed_values, embed_grad, embed_first, embed_second
    )
    embed_step = jnp.where(row_live[:, None], direction, 0.0)
    first_embed = jnp.where(row_live[:, None], first_next, embed_first)
    second_embed = jnp.where(row_live[:, None], second_next, embed_second)
    return (
        square_next,
        swiglu_next,
        square_update,
        swiglu_update,
        owner_norms,
        vector_step,
        first_vector,
        second_vector,
        embed_step,
        first_embed,
        second_embed,
    )


def solution(mesh):
    flat = P(None, ("dp", "tensor"))
    vector = P(("dp", "tensor"))
    tile = P("dp", "tensor")
    update = P(None, "dp", "tensor")
    return jax.shard_map(
        local,
        mesh=mesh,
        in_specs=(flat,) * 4 + (P(),) * 3 + (vector,) * 4 + (tile,) * 4 + (P(),),
        out_specs=(flat, flat, update, update, P("dp")) + (vector,) * 3 + (tile,) * 3,
        check_vma=False,
    )
```

```python
import math

import jax
import jax.numpy as jnp
import numpy as np
from jax import lax
from jax.experimental import pallas as pl
from jax.experimental.pallas import tpu as pltpu
from jax.sharding import PartitionSpec as P

D = 1536
FF = 4096
NS_STEPS = 2


QUINTIC_LINEAR = 3.4445
QUINTIC_CUBIC = -4.775
QUINTIC_FIFTH = 2.0315
MOMENTUM = 0.95
BIAS_FIRST = 1.0 - 0.9**10
BIAS_SECOND = 1.0 - 0.95**10


def momentum_terms(gradient, state):
    state_next = MOMENTUM * state + gradient
    return (state_next, (gradient + MOMENTUM * state_next).astype(jnp.bfloat16))


def adamw_terms(values, gradient, first, second):
    first_next = 0.9 * first + 0.1 * gradient
    second_next = 0.95 * second + 0.05 * gradient * gradient
    direction = (
        first_next / BIAS_FIRST / (jnp.sqrt(second_next / BIAS_SECOND) + 1e-08) + 0.1 * values
    )
    return (direction, first_next, second_next)


LANE = 128
GRANULE = 256


class Plan:
    def __init__(self, chips, cores, square_count, swiglu_count):
        planes = 4
        per = chips // planes
        side = max(1, int(round(math.sqrt(per))))

        def coords(i):
            return (i % side, (i // side) % max(1, per // side), i // per)

        def hops(a, b):
            return sum(abs(p - q) for p, q in zip(coords(a), coords(b)))

        low = [i for i in range(chips) if coords(i)[2] < planes // 2]
        low.sort(key=lambda i: (-(sum(coords(i)) % 2), -coords(i)[2], i))
        high = [i for i in range(chips) if coords(i)[2] >= planes // 2]
        high.sort(key=lambda i: (-(sum(coords(i)) % 2), coords(i)[2], i))
        order = [c for pair in zip(low, high) for c in pair]
        self.heavy = order[:swiglu_count]
        rest = order[swiglu_count:]
        self.light = rest[:square_count]
        helpers = rest
        narrow = D // cores
        wide = FF // cores
        self.granules = (wide - narrow) // GRANULE
        self.passes = self.granules - 2
        count = len(helpers)
        take = [
            [helpers[(k + p * swiglu_count) % count] for k in range(swiglu_count)]
            for p in range(self.passes)
        ]
        cost = lambda p, k, h: hops(h, self.heavy[k]) ** 2
        better = True
        while better:
            better = False
            places = [(p, k) for p in range(self.passes) for k in range(swiglu_count)]
            for p, k in places:
                for h in helpers:
                    used = sum(row.count(h) for row in take)
                    if used < 2 and h not in take[p] and cost(p, k, h) < cost(p, k, take[p][k]):
                        take[p][k] = h
                        better = True
                for q, m in places:
                    a, b = take[p][k], take[q][m]
                    if a == b or (q != p and (b in take[p] or a in take[q])):
                        continue
                    if cost(p, k, b) + cost(q, m, a) < cost(p, k, a) + cost(q, m, b):
                        take[p][k], take[q][m] = b, a
                        better = True
        self.take = take
        self.held = {o: [(j, 0), (j, 1)] for j, o in enumerate(self.heavy)}
        self.place = {}
        for p in range(self.passes):
            for k in range(swiglu_count):
                h = take[p][k]
                self.held.setdefault(h, []).append((k, 2 + p))
        for chip, list_of in self.held.items():
            for where, item in enumerate(list_of):
                self.place[item] = (chip, where)
        self.is_heavy = np.array([c in self.heavy for c in range(chips)])
        self.slot_in_pass = np.zeros((max(1, self.passes), chips), np.bool_)
        for p in range(self.passes):
            for k in range(swiglu_count):
                self.slot_in_pass[p, take[p][k]] = self.place[(k, 2 + p)][1] == 1
        self.idle = [c for c in range(chips) if c not in self.heavy and c not in self.light]


def prepare_kernel(plan, cores, sg, ss, wg, ws, sn, wn, first, second):
    narrow_tiles = D // cores // LANE
    wide_tiles = FF // cores // LANE
    square_next = MOMENTUM * ss[...] + sg[...]
    sn[...] = square_next
    swiglu_next = MOMENTUM * ws[...] + wg[...]
    wn[...] = swiglu_next

    def piece(grad, state, row_tile, slot):
        g = grad[:, row_tile, slot, :]
        return (g + MOMENTUM * (MOMENTUM * state[:, row_tile, slot, :] + g)).astype(jnp.bfloat16)

    for j, owner in enumerate(plan.heavy):
        for core in range(cores):
            for t in range(wide_tiles):
                value = piece(wg, ws, core * wide_tiles + t, j)
                if t < narrow_tiles:
                    first[owner * cores + core, :, t * LANE : (t + 1) * LANE] = value
                else:
                    b, part = divmod(t - narrow_tiles, GRANULE // LANE)
                    chip, where = plan.place[(j, b)]
                    at = where * GRANULE + part * LANE
                    second[chip * cores + core, :, at : at + LANE] = value
    for j, owner in enumerate(plan.light):
        for core in range(cores):
            for t in range(narrow_tiles):
                value = piece(sg, ss, core * narrow_tiles + t, j)
                first[owner * cores + core, :, t * LANE : (t + 1) * LANE] = value
    for chip in range(len(plan.is_heavy)):
        for core in range(cores):
            if chip in plan.idle:
                first[chip * cores + core] = jnp.zeros(first.shape[1:], first.dtype)
            for where in range(len(plan.held.get(chip, [])), 2):
                second[chip * cores + core, :, where * GRANULE : (where + 1) * GRANULE] = jnp.zeros(
                    (first.shape[1], GRANULE), first.dtype
                )


def prepare(plan, chips, cores, square_grad, square_state, swiglu_grad, swiglu_state):
    rows = D // (chips * cores)
    chunk = 16 if rows % 16 == 0 else rows
    square_count, swiglu_count = square_grad.shape[0], swiglu_grad.shape[0]

    def tiles(x, width):
        count = x.shape[0]
        return x.reshape(count, rows, width // LANE, LANE).transpose(1, 2, 0, 3)

    def flat(x, width):
        return x.transpose(2, 0, 1, 3).reshape(x.shape[2], rows * width)

    narrow = D // cores
    square_block = pl.BlockSpec((chunk, D // LANE, square_count, LANE), lambda i: (i, 0, 0, 0))
    swiglu_block = pl.BlockSpec((chunk, FF // LANE, swiglu_count, LANE), lambda i: (i, 0, 0, 0))
    devices = chips * cores
    out = pl.pallas_call(
        lambda *refs: prepare_kernel(plan, cores, *refs),
        grid=(rows // chunk,),
        in_specs=[square_block, square_block, swiglu_block, swiglu_block],
        out_specs=[
            square_block,
            swiglu_block,
            pl.BlockSpec((devices, chunk, narrow), lambda i: (0, i, 0)),
            pl.BlockSpec((devices, chunk, 2 * GRANULE), lambda i: (0, i, 0)),
        ],
        out_shape=[
            jax.ShapeDtypeStruct((rows, D // LANE, square_count, LANE), jnp.float32),
            jax.ShapeDtypeStruct((rows, FF // LANE, swiglu_count, LANE), jnp.float32),
            jax.ShapeDtypeStruct((devices, rows, narrow), jnp.bfloat16),
            jax.ShapeDtypeStruct((devices, rows, 2 * GRANULE), jnp.bfloat16),
        ],
        compiler_params=pltpu.CompilerParams(vmem_limit_bytes=56 * 1024 * 1024),
        name="prepare",
    )(tiles(square_grad, D), tiles(square_state, D), tiles(swiglu_grad, FF), tiles(swiglu_state, FF))
    return flat(out[0], D), flat(out[1], FF), out[2], out[3]


def other_core(x):
    return lax.ppermute(x, "tensor", [(0, 1), (1, 0)])


def inverse_of(order):
    count = order.shape[0]
    match = order[None, :] == jnp.arange(count, dtype=jnp.int32)[:, None]
    return jnp.sum(jnp.where(match, jnp.arange(count, dtype=jnp.int32)[None, :], 0), axis=1)


def local(
    square_grad,
    square_state,
    swiglu_grad,
    swiglu_state,
    square_order,
    swiglu_order,
    owners,
    vector_values,
    vector_grad,
    vector_first,
    vector_second,
    embed_values,
    embed_grad,
    embed_first,
    embed_second,
    embed_ranges,
):
    chips = lax.axis_size("dp")
    cores = lax.axis_size("tensor")
    chip = lax.axis_index("dp")
    square_count = square_grad.shape[0]
    swiglu_count = swiglu_grad.shape[0]
    chip_rows = D // chips
    narrow = D // cores
    plan = Plan(chips, cores, square_count, swiglu_count)

    square_next, swiglu_next, first_send, second_send = prepare(
        plan, chips, cores, square_grad, square_state, swiglu_grad, swiglu_state
    )
    both = ("dp", "tensor")
    second_got = lax.all_to_all(
        second_send.reshape(D, 2 * GRANULE), both, split_axis=0, concat_axis=0, tiled=True
    )
    first_got = lax.all_to_all(
        first_send.reshape(D, narrow), both, split_axis=0, concat_axis=0, tiled=True
    )
    heavy_here = jnp.asarray(plan.is_heavy)[chip]
    pieces = [second_got[:, :GRANULE], second_got[:, GRANULE:]]
    relayed = []
    for p in range(plan.passes):
        pick = jnp.asarray(plan.slot_in_pass[p])[chip]
        pairs = [(plan.take[p][k], plan.heavy[k]) for k in range(swiglu_count)]
        relayed.append(lax.ppermute(jnp.where(pick, pieces[1], pieces[0]), "dp", pairs))
    kept = jnp.where(heavy_here, second_got, jnp.zeros((), jnp.bfloat16))
    matrix = jnp.concatenate([first_got, kept] + relayed, axis=1)

    factor = jnp.where(heavy_here, jnp.float32(math.sqrt(FF)), jnp.float32(math.sqrt(D)))
    iterate = matrix
    first_scale = jnp.float32(1.0)
    for round_index in range(NS_STEPS):
        gram_part = jnp.einsum("rc,sc->rs", iterate, iterate, preferred_element_type=jnp.float32)
        gram = gram_part + other_core(gram_part)
        if round_index == 0:
            gram_scale = jnp.sqrt(jnp.sum(gram * gram)) + 1e-06
            first_scale = gram_scale
        else:
            gram_scale = jnp.float32(1.0)
        normed = (gram / gram_scale).astype(jnp.bfloat16)
        squared = jnp.dot(normed, normed, preferred_element_type=jnp.float32)
        polynomial = (
            QUINTIC_CUBIC * normed.astype(jnp.float32) + QUINTIC_FIFTH * squared
        ).astype(jnp.bfloat16)
        if round_index < NS_STEPS - 1:
            product = jnp.dot(polynomial, iterate, preferred_element_type=jnp.float32)
            mixed = (QUINTIC_LINEAR * iterate.astype(jnp.float32) + product) / jnp.sqrt(gram_scale)
            iterate = mixed.astype(jnp.bfloat16)

    def finish(columns):
        part = iterate[:, columns]
        product = jnp.dot(polynomial, part, preferred_element_type=jnp.float32)
        return (factor * (QUINTIC_LINEAR * part.astype(jnp.float32) + product)).astype(jnp.bfloat16)

    def send_back(x):
        return lax.all_to_all(
            x.reshape(chips, chip_rows, -1), "dp", split_axis=0, concat_axis=0, tiled=True
        )

    first_back = send_back(finish(slice(0, narrow)))
    rest = finish(slice(narrow, None))
    handed = []
    for p in range(plan.passes):
        pairs = [(plan.heavy[k], plan.take[p][k]) for k in range(swiglu_count)]
        at = (2 + p) * GRANULE
        handed.append(lax.ppermute(rest[:, at : at + GRANULE], "dp", pairs))
    halves = []
    for where in range(2):
        value = rest[:, where * GRANULE : (where + 1) * GRANULE]
        for p in range(plan.passes):
            mine = np.zeros((chips,), np.bool_)
            for k in range(swiglu_count):
                if plan.place[(k, 2 + p)][1] == where:
                    mine[plan.take[p][k]] = True
            value = jnp.where(jnp.asarray(mine)[chip], handed[p], value)
        halves.append(value)
    second_back = send_back(jnp.concatenate(halves, axis=1))

    slot_of_square = inverse_of(square_order)
    slot_of_swiglu = inverse_of(swiglu_order)
    chip_of_square = jnp.asarray(np.array(plan.light, np.int32))[slot_of_square]
    chip_of_swiglu = jnp.asarray(np.array(plan.heavy, np.int32))[slot_of_swiglu]
    square_update = first_back[chip_of_square]
    parts = [first_back[np.array(plan.heavy, np.int32)]]
    for b in range(plan.granules):
        parts.append(
            jnp.stack(
                [
                    second_back[plan.place[(j, b)][0], :, plan.place[(j, b)][1] * GRANULE :][:, :GRANULE]
                    for j in range(swiglu_count)
                ]
            )
        )
    swiglu_update = jnp.concatenate(parts, axis=2)[slot_of_swiglu]

    logs = lax.all_gather(0.5 * jnp.log(first_scale), "dp")
    matrix_chip = jnp.concatenate([chip_of_square, chip_of_swiglu])
    owner_norms = jnp.sum(jnp.where(owners == chip, logs[matrix_chip], 0.0)).reshape(1)

    vector_step, first_vector, second_vector = adamw_terms(
        vector_values, vector_grad, vector_first, vector_second
    )
    embed_rows = embed_values.shape[0]
    row_numbers = chip * embed_rows + jnp.arange(embed_rows, dtype=jnp.int32)
    inside = (row_numbers[:, None] >= embed_ranges[None, :, 0]) & (
        row_numbers[:, None] < embed_ranges[None, :, 1]
    )
    row_live = jnp.sum(inside.astype(jnp.int32), axis=1) > 0
    direction, first_next, second_next = adamw_terms(
        embed_values, embed_grad, embed_first, embed_second
    )
    embed_step = jnp.where(row_live[:, None], direction, 0.0)
    first_embed = jnp.where(row_live[:, None], first_next, embed_first)
    second_embed = jnp.where(row_live[:, None], second_next, embed_second)
    return (
        square_next,
        swiglu_next,
        square_update,
        swiglu_update,
        owner_norms,
        vector_step,
        first_vector,
        second_vector,
        embed_step,
        first_embed,
        second_embed,
    )


def solution(mesh):
    flat = P(None, ("dp", "tensor"))
    vector = P(("dp", "tensor"))
    tile = P("dp", "tensor")
    update = P(None, "dp", "tensor")
    return jax.shard_map(
        local,
        mesh=mesh,
        in_specs=(flat,) * 4 + (P(),) * 3 + (vector,) * 4 + (tile,) * 4 + (P(),),
        out_specs=(flat, flat, update, update, P("dp")) + (vector,) * 3 + (tile,) * 3,
        check_vma=False,
    )
```

```python
import math

import jax
import jax.numpy as jnp
import numpy as np
from jax import lax
from jax.experimental import pallas as pl
from jax.experimental.pallas import tpu as pltpu
from jax.sharding import PartitionSpec as P

D = 1536
FF = 4096
NS_STEPS = 2


QUINTIC_LINEAR = 3.4445
QUINTIC_CUBIC = -4.775
QUINTIC_FIFTH = 2.0315
MOMENTUM = 0.95
BIAS_FIRST = 1.0 - 0.9**10
BIAS_SECOND = 1.0 - 0.95**10


def momentum_terms(gradient, state):
    state_next = MOMENTUM * state + gradient
    return (state_next, (gradient + MOMENTUM * state_next).astype(jnp.bfloat16))


def adamw_terms(values, gradient, first, second):
    first_next = 0.9 * first + 0.1 * gradient
    second_next = 0.95 * second + 0.05 * gradient * gradient
    direction = (
        first_next / BIAS_FIRST / (jnp.sqrt(second_next / BIAS_SECOND) + 1e-08) + 0.1 * values
    )
    return (direction, first_next, second_next)


LANE = 128
GRANULE = 256


class Plan:
    def __init__(self, chips, cores, square_count, swiglu_count):
        planes = 4
        per = chips // planes
        side = max(1, int(round(math.sqrt(per))))

        def coords(i):
            return (i % side, (i // side) % max(1, per // side), i // per)

        def hops(a, b):
            return sum(abs(p - q) for p, q in zip(coords(a), coords(b)))

        low = [i for i in range(chips) if coords(i)[2] < planes // 2]
        low.sort(key=lambda i: (-(sum(coords(i)) % 2), -coords(i)[2], i))
        high = [i for i in range(chips) if coords(i)[2] >= planes // 2]
        high.sort(key=lambda i: (-(sum(coords(i)) % 2), coords(i)[2], i))
        order = [c for pair in zip(low, high) for c in pair]
        self.heavy = order[:swiglu_count]
        rest = order[swiglu_count:]
        self.light = rest[:square_count]
        helpers = rest
        narrow = D // cores
        wide = FF // cores
        self.granules = (wide - narrow) // GRANULE
        self.passes = self.granules - 2
        count = len(helpers)
        take = [
            [helpers[(k + p * swiglu_count) % count] for k in range(swiglu_count)]
            for p in range(self.passes)
        ]
        cost = lambda p, k, h: hops(h, self.heavy[k]) ** 2
        better = True
        while better:
            better = False
            places = [(p, k) for p in range(self.passes) for k in range(swiglu_count)]
            for p, k in places:
                for h in helpers:
                    used = sum(row.count(h) for row in take)
                    if used < 2 and h not in take[p] and cost(p, k, h) < cost(p, k, take[p][k]):
                        take[p][k] = h
                        better = True
                for q, m in places:
                    a, b = take[p][k], take[q][m]
                    if a == b or (q != p and (b in take[p] or a in take[q])):
                        continue
                    if cost(p, k, b) + cost(q, m, a) < cost(p, k, a) + cost(q, m, b):
                        take[p][k], take[q][m] = b, a
                        better = True
        self.take = take
        self.held = {o: [(j, 0), (j, 1)] for j, o in enumerate(self.heavy)}
        self.place = {}
        for p in range(self.passes):
            for k in range(swiglu_count):
                h = take[p][k]
                self.held.setdefault(h, []).append((k, 2 + p))
        for chip, list_of in self.held.items():
            for where, item in enumerate(list_of):
                self.place[item] = (chip, where)
        self.is_heavy = np.array([c in self.heavy for c in range(chips)])
        self.slot_in_pass = np.zeros((max(1, self.passes), chips), np.bool_)
        for p in range(self.passes):
            for k in range(swiglu_count):
                self.slot_in_pass[p, take[p][k]] = self.place[(k, 2 + p)][1] == 1
        self.idle = [c for c in range(chips) if c not in self.heavy and c not in self.light]


def prepare_kernel(plan, cores, sg, ss, wg, ws, sn, wn, first, second):
    narrow_tiles = D // cores // LANE
    wide_tiles = FF // cores // LANE
    square_next = MOMENTUM * ss[...] + sg[...]
    sn[...] = square_next
    swiglu_next = MOMENTUM * ws[...] + wg[...]
    wn[...] = swiglu_next

    def piece(grad, state, row_tile, slot):
        g = grad[:, row_tile, slot, :]
        return (g + MOMENTUM * (MOMENTUM * state[:, row_tile, slot, :] + g)).astype(jnp.bfloat16)

    for j, owner in enumerate(plan.heavy):
        for core in range(cores):
            for t in range(wide_tiles):
                value = piece(wg, ws, core * wide_tiles + t, j)
                if t < narrow_tiles:
                    first[owner * cores + core, :, t * LANE : (t + 1) * LANE] = value
                else:
                    b, part = divmod(t - narrow_tiles, GRANULE // LANE)
                    chip, where = plan.place[(j, b)]
                    at = where * GRANULE + part * LANE
                    second[chip * cores + core, :, at : at + LANE] = value
    for j, owner in enumerate(plan.light):
        for core in range(cores):
            for t in range(narrow_tiles):
                value = piece(sg, ss, core * narrow_tiles + t, j)
                first[owner * cores + core, :, t * LANE : (t + 1) * LANE] = value
    for chip in range(len(plan.is_heavy)):
        for core in range(cores):
            if chip in plan.idle:
                first[chip * cores + core] = jnp.zeros(first.shape[1:], first.dtype)
            for where in range(len(plan.held.get(chip, [])), 2):
                second[chip * cores + core, :, where * GRANULE : (where + 1) * GRANULE] = jnp.zeros(
                    (first.shape[1], GRANULE), first.dtype
                )


def prepare(plan, chips, cores, square_grad, square_state, swiglu_grad, swiglu_state):
    rows = D // (chips * cores)
    chunk = 16 if rows % 16 == 0 else rows
    square_count, swiglu_count = square_grad.shape[0], swiglu_grad.shape[0]

    def tiles(x, width):
        count = x.shape[0]
        return x.reshape(count, rows, width // LANE, LANE).transpose(1, 2, 0, 3)

    def flat(x, width):
        return x.transpose(2, 0, 1, 3).reshape(x.shape[2], rows * width)

    narrow = D // cores
    square_block = pl.BlockSpec((chunk, D // LANE, square_count, LANE), lambda i: (i, 0, 0, 0))
    swiglu_block = pl.BlockSpec((chunk, FF // LANE, swiglu_count, LANE), lambda i: (i, 0, 0, 0))
    devices = chips * cores
    out = pl.pallas_call(
        lambda *refs: prepare_kernel(plan, cores, *refs),
        grid=(rows // chunk,),
        in_specs=[square_block, square_block, swiglu_block, swiglu_block],
        out_specs=[
            square_block,
            swiglu_block,
            pl.BlockSpec((devices, chunk, narrow), lambda i: (0, i, 0)),
            pl.BlockSpec((devices, chunk, 2 * GRANULE), lambda i: (0, i, 0)),
        ],
        out_shape=[
            jax.ShapeDtypeStruct((rows, D // LANE, square_count, LANE), jnp.float32),
            jax.ShapeDtypeStruct((rows, FF // LANE, swiglu_count, LANE), jnp.float32),
            jax.ShapeDtypeStruct((devices, rows, narrow), jnp.bfloat16),
            jax.ShapeDtypeStruct((devices, rows, 2 * GRANULE), jnp.bfloat16),
        ],
        compiler_params=pltpu.CompilerParams(vmem_limit_bytes=56 * 1024 * 1024),
        name="prepare",
    )(tiles(square_grad, D), tiles(square_state, D), tiles(swiglu_grad, FF), tiles(swiglu_state, FF))
    return flat(out[0], D), flat(out[1], FF), out[2], out[3]


def other_core(x):
    return lax.ppermute(x, "tensor", [(0, 1), (1, 0)])


BLOCK = 256
EDGE = D // BLOCK
NEAR = EDGE // 2
PACKED = EDGE * NEAR + NEAR
VMEM_LIMIT = 58 * 1024 * 1024


def each_pair(body):
    def row(i, carry):
        for d in range(NEAR):
            j = lax.rem(i + d, EDGE)
            body(i * NEAR + d, i, j, d == 0)
        return carry

    lax.fori_loop(0, EDGE, row, 0)

    def far(i, carry):
        body(EDGE * NEAR + i, i, i + NEAR, False)
        return carry

    lax.fori_loop(0, NEAR, far, 0)


def span(i):
    return pl.ds(pl.multiple_of(i * BLOCK, BLOCK), BLOCK)


def nt(a, b):
    return lax.dot_general(a, b, (((1,), (1,)), ((), ())), preferred_element_type=jnp.float32)


def gram_blocks(parts, out):
    def body(slot, i, j, diagonal):
        total = nt(parts[0][span(i), :], parts[0][span(j), :])
        for part in parts[1:]:
            total += nt(part[span(i), :], part[span(j), :])
        out[slot] = total

    each_pair(body)


def mirror(out, i, j, diagonal, value):
    out[span(i), span(j)] = value.astype(out.dtype)
    if not diagonal:
        out[span(j), span(i)] = value.T.astype(out.dtype)


def polynomial_blocks(normed, out):
    def body(slot, i, j, diagonal):
        squared = jnp.dot(normed[span(i), :], normed[:, span(j)], preferred_element_type=jnp.float32)
        value = QUINTIC_CUBIC * normed[span(i), span(j)].astype(jnp.float32) + QUINTIC_FIFTH * squared
        mirror(out, i, j, diagonal, value)

    each_pair(body)


def mixed_rows(polynomial, part, scale, targets):
    def row(i, carry):
        at = 0
        for target in targets:
            for c in range(0, target.shape[1], BLOCK):
                columns = slice(at, at + BLOCK)
                product = jnp.dot(
                    polynomial[span(i), :], part[:, columns], preferred_element_type=jnp.float32
                )
                mixed = QUINTIC_LINEAR * part[span(i), columns].astype(jnp.float32) + product
                target[span(i), c : c + BLOCK] = (mixed * scale).astype(target.dtype)
                at += BLOCK
        return carry

    lax.fori_loop(0, EDGE, row, 0)


def gram_kernel(flag, first, second, *rest):
    relayed, out = rest[:-1], rest[-1]
    heavy = flag[0] > 0

    @pl.when(heavy)
    def _():
        gram_blocks([first, second, *relayed], out)

    @pl.when(jnp.logical_not(heavy))
    def _():
        gram_blocks([first], out)


def middle_kernel(flag, own, other, first, second, *rest):
    count = len(rest) - 6
    relayed = rest[:count]
    first_out, second_out, packed, scale_out, normed, polynomial = rest[count:]
    heavy = flag[0] > 0

    def add(slot, total):
        gram = own[slot] + other[slot]
        packed[slot] = gram
        return total + jnp.sum(gram * gram)

    def row(i, carry):
        once, twice = carry
        once = add(i * NEAR, once)
        for d in range(1, NEAR):
            twice = add(i * NEAR + d, twice)
        return once, twice

    once, twice = lax.fori_loop(0, EDGE, row, (jnp.float32(0.0), jnp.float32(0.0)))
    twice = lax.fori_loop(0, NEAR, lambda i, t: add(EDGE * NEAR + i, t), twice)
    total = jnp.full((8, LANE), once + 2.0 * twice, jnp.float32)
    scale = jnp.sqrt(total) + 1e-06
    scale_out[...] = scale
    inverse = (1.0 / scale)[0:1, 0:1]
    root = (1.0 / jnp.sqrt(scale))[0:1, 0:1]

    def norm(slot, i, j, diagonal):
        mirror(normed, i, j, diagonal, packed[slot] * inverse)

    each_pair(norm)
    polynomial_blocks(normed, polynomial)
    mixed_rows(polynomial, first, root, [first_out])

    @pl.when(heavy)
    def _():
        at = 0
        for part in (second, *relayed):
            width = part.shape[1]
            mixed_rows(polynomial, part, root, [second_out.at[:, at : at + width]])
            at += width
        gram_blocks([first_out, second_out], packed)

    @pl.when(jnp.logical_not(heavy))
    def _():
        gram_blocks([first_out], packed)


def last_kernel(factor, own, other, first, polynomial, out, normed):
    def norm(slot, i, j, diagonal):
        mirror(normed, i, j, diagonal, own[slot] + other[slot])

    each_pair(norm)
    polynomial_blocks(normed, polynomial)
    mixed_rows(polynomial, first, factor[0], [out])


def rest_kernel(flag, factor, polynomial, second, *outs):
    @pl.when(flag[0] > 0)
    def _():
        mixed_rows(polynomial, second, factor[0], outs)


def call(kernel, name, scalars, arrays, outs, scratch=(), flops=0):
    moved = sum(x.size * x.dtype.itemsize for x in arrays)
    moved += sum(math.prod(o.shape) * o.dtype.itemsize for o in outs)
    smem = pl.BlockSpec(memory_space=pltpu.SMEM)
    return pl.pallas_call(
        kernel,
        in_specs=[smem] * len(scalars) + [pl.BlockSpec(memory_space=pltpu.VMEM)] * len(arrays),
        out_specs=[pl.BlockSpec(memory_space=pltpu.VMEM)] * len(outs),
        out_shape=list(outs),
        scratch_shapes=list(scratch),
        compiler_params=pltpu.CompilerParams(vmem_limit_bytes=VMEM_LIMIT),
        cost_estimate=pl.CostEstimate(flops=flops, bytes_accessed=moved, transcendentals=0),
        name=name,
    )(*scalars, *arrays)


def assemble_squares(plan, square_order, first_back):
    count = square_order.shape[0]

    def kernel(order, source, out, sems):
        copies = [
            pltpu.make_async_copy(source.at[plan.light[j]], out.at[order[j]], sems.at[j])
            for j in range(count)
        ]
        for copy in copies:
            copy.start()
        for copy in copies:
            copy.wait()

    return pl.pallas_call(
        kernel,
        in_specs=[pl.BlockSpec(memory_space=pltpu.SMEM), pl.BlockSpec(memory_space=pl.ANY)],
        out_specs=pl.BlockSpec(memory_space=pl.ANY),
        out_shape=jax.ShapeDtypeStruct((count,) + first_back.shape[1:], jnp.bfloat16),
        scratch_shapes=[pltpu.SemaphoreType.DMA((count,))],
        name="assemble_squares",
    )(square_order, first_back)


def assemble_swiglu(plan, swiglu_order, first_back, second_back):
    count = swiglu_order.shape[0]
    narrow = first_back.shape[2]
    rows = first_back.shape[1]
    wide = narrow + plan.granules * GRANULE

    def kernel(order, first, second, out, sems):
        copies = []

        def move(source, j, at, width):
            copies.append(
                pltpu.make_async_copy(
                    source, out.at[order[j], :, pl.ds(at, width)], sems.at[len(copies)]
                )
            )

        for j in range(count):
            owner = plan.heavy[j]
            move(first.at[owner], j, 0, narrow)
            move(second.at[owner], j, narrow, 2 * GRANULE)
            for b in range(2, plan.granules):
                chip, where = plan.place[(j, b)]
                source = second.at[chip, :, pl.ds(where * GRANULE, GRANULE)]
                move(source, j, narrow + b * GRANULE, GRANULE)
        for copy in copies:
            copy.start()
        for copy in copies:
            copy.wait()

    return pl.pallas_call(
        kernel,
        in_specs=[pl.BlockSpec(memory_space=pltpu.SMEM)] + [pl.BlockSpec(memory_space=pl.ANY)] * 2,
        out_specs=pl.BlockSpec(memory_space=pl.ANY),
        out_shape=jax.ShapeDtypeStruct((count, rows, wide), jnp.bfloat16),
        scratch_shapes=[pltpu.SemaphoreType.DMA((count * plan.granules,))],
        name="assemble_swiglu",
    )(swiglu_order, first_back, second_back)


def lookup(table, positions):
    matches = positions[:, None] == jnp.arange(table.shape[0], dtype=jnp.int32)[None, :]
    return jnp.sum(jnp.where(matches, table[None, :], 0), axis=1)


def local(
    square_grad,
    square_state,
    swiglu_grad,
    swiglu_state,
    square_order,
    swiglu_order,
    owners,
    vector_values,
    vector_grad,
    vector_first,
    vector_second,
    embed_values,
    embed_grad,
    embed_first,
    embed_second,
    embed_ranges,
):
    chips = lax.axis_size("dp")
    cores = lax.axis_size("tensor")
    chip = lax.axis_index("dp")
    square_count = square_grad.shape[0]
    swiglu_count = swiglu_grad.shape[0]
    chip_rows = D // chips
    narrow = D // cores
    plan = Plan(chips, cores, square_count, swiglu_count)

    square_next, swiglu_next, first_send, second_send = prepare(
        plan, chips, cores, square_grad, square_state, swiglu_grad, swiglu_state
    )
    both = ("dp", "tensor")
    second_got = lax.all_to_all(
        second_send.reshape(D, 2 * GRANULE), both, split_axis=0, concat_axis=0, tiled=True
    )
    first_got = lax.all_to_all(
        first_send.reshape(D, narrow), both, split_axis=0, concat_axis=0, tiled=True
    )
    heavy_here = jnp.asarray(plan.is_heavy)[chip]
    pieces = [second_got[:, :GRANULE], second_got[:, GRANULE:]]
    relayed = []
    for p in range(plan.passes):
        pick = jnp.asarray(plan.slot_in_pass[p])[chip]
        pairs = [(plan.take[p][k], plan.heavy[k]) for k in range(swiglu_count)]
        relayed.append(lax.ppermute(jnp.where(pick, pieces[1], pieces[0]), "dp", pairs))
    flag = heavy_here.astype(jnp.int32).reshape(1)
    factor = jnp.where(heavy_here, jnp.float32(math.sqrt(FF)), jnp.float32(math.sqrt(D))).reshape(1)
    packed = jax.ShapeDtypeStruct((PACKED, BLOCK, BLOCK), jnp.float32)
    whole_square = jax.ShapeDtypeStruct((D, D), jnp.bfloat16)
    first_shape = jax.ShapeDtypeStruct((D, narrow), jnp.bfloat16)
    extra = plan.granules * GRANULE
    second_shape = jax.ShapeDtypeStruct((D, extra), jnp.bfloat16)
    square_buffer = pltpu.VMEM((D, D), jnp.bfloat16)
    half = D * D * (narrow + extra)
    (own,) = call(
        gram_kernel, "gram", [flag], [first_got, second_got, *relayed], [packed], flops=half
    )
    first_mid, second_mid, own_mid, scale = call(
        middle_kernel,
        "middle",
        [flag],
        [own, other_core(own), first_got, second_got, *relayed],
        [first_shape, second_shape, packed, jax.ShapeDtypeStruct((8, LANE), jnp.float32)],
        [square_buffer, square_buffer],
        flops=3 * half + D * D * D,
    )
    logs = lax.all_gather(scale, "dp")
    polynomial, first_done = call(
        last_kernel,
        "last",
        [factor],
        [own_mid, other_core(own_mid), first_mid],
        [whole_square, first_shape],
        [square_buffer],
        flops=D * D * D + 2 * D * D * narrow,
    )
    piece_shape = jax.ShapeDtypeStruct((D, GRANULE), jnp.bfloat16)
    rest = call(
        rest_kernel,
        "rest",
        [flag, factor],
        [polynomial, second_mid],
        [jax.ShapeDtypeStruct((D, 2 * GRANULE), jnp.bfloat16)] + [piece_shape] * plan.passes,
        flops=2 * D * D * extra,
    )

    def send_back(x):
        return lax.all_to_all(
            x.reshape(chips, chip_rows, -1), "dp", split_axis=0, concat_axis=0, tiled=True
        )

    first_back = send_back(first_done)
    handed = []
    for p in range(plan.passes):
        pairs = [(plan.heavy[k], plan.take[p][k]) for k in range(swiglu_count)]
        handed.append(lax.ppermute(rest[1 + p], "dp", pairs))
    halves = []
    for where in range(2):
        value = rest[0][:, where * GRANULE : (where + 1) * GRANULE]
        for p in range(plan.passes):
            mine = np.zeros((chips,), np.bool_)
            for k in range(swiglu_count):
                if plan.place[(k, 2 + p)][1] == where:
                    mine[plan.take[p][k]] = True
            value = jnp.where(jnp.asarray(mine)[chip], handed[p], value)
        halves.append(value)
    second_out, first_back = lax.optimization_barrier((jnp.concatenate(halves, axis=1), first_back))
    second_back = send_back(second_out)

    square_update = assemble_squares(plan, square_order, first_back)
    swiglu_update = assemble_swiglu(plan, swiglu_order, first_back, second_back)

    slot_chips = np.array(plan.light + plan.heavy, np.int32)
    slot_owner = jnp.concatenate(
        [lookup(owners[:square_count], square_order), lookup(owners[square_count:], swiglu_order)]
    )
    slot_logs = 0.5 * jnp.log(logs[:, 0, 0])[slot_chips]
    owner_norms = jnp.sum(jnp.where(slot_owner == chip, slot_logs, 0.0)).reshape(1)

    vector_step, first_vector, second_vector = adamw_terms(
        vector_values, vector_grad, vector_first, vector_second
    )
    embed_rows = embed_values.shape[0]
    row_numbers = chip * embed_rows + jnp.arange(embed_rows, dtype=jnp.int32)
    inside = (row_numbers[:, None] >= embed_ranges[None, :, 0]) & (
        row_numbers[:, None] < embed_ranges[None, :, 1]
    )
    row_live = jnp.sum(inside.astype(jnp.int32), axis=1) > 0
    direction, first_next, second_next = adamw_terms(
        embed_values, embed_grad, embed_first, embed_second
    )
    embed_step = jnp.where(row_live[:, None], direction, 0.0)
    first_embed = jnp.where(row_live[:, None], first_next, embed_first)
    second_embed = jnp.where(row_live[:, None], second_next, embed_second)
    return (
        square_next,
        swiglu_next,
        square_update,
        swiglu_update,
        owner_norms,
        vector_step,
        first_vector,
        second_vector,
        embed_step,
        first_embed,
        second_embed,
    )


def solution(mesh):
    flat = P(None, ("dp", "tensor"))
    vector = P(("dp", "tensor"))
    tile = P("dp", "tensor")
    update = P(None, "dp", "tensor")
    return jax.shard_map(
        local,
        mesh=mesh,
        in_specs=(flat,) * 4 + (P(),) * 3 + (vector,) * 4 + (tile,) * 4 + (P(),),
        out_specs=(flat, flat, update, update, P("dp")) + (vector,) * 3 + (tile,) * 3,
        check_vma=False,
    )
```

```python
import math

import jax
import jax.numpy as jnp
import numpy as np
from jax import lax
from jax.experimental import pallas as pl
from jax.experimental.pallas import tpu as pltpu
from jax.sharding import PartitionSpec as P

D = 1536
FF = 4096
NS_STEPS = 2


QUINTIC_LINEAR = 3.4445
QUINTIC_CUBIC = -4.775
QUINTIC_FIFTH = 2.0315
MOMENTUM = 0.95
BIAS_FIRST = 1.0 - 0.9**10
BIAS_SECOND = 1.0 - 0.95**10


def momentum_terms(gradient, state):
    state_next = MOMENTUM * state + gradient
    return (state_next, (gradient + MOMENTUM * state_next).astype(jnp.bfloat16))


def adamw_terms(values, gradient, first, second):
    first_next = 0.9 * first + 0.1 * gradient
    second_next = 0.95 * second + 0.05 * gradient * gradient
    direction = (
        first_next / BIAS_FIRST / (jnp.sqrt(second_next / BIAS_SECOND) + 1e-08) + 0.1 * values
    )
    return (direction, first_next, second_next)


LANE = 128
GRANULE = 256


class Plan:
    def __init__(self, chips, cores, square_count, swiglu_count):
        planes = 4
        per = chips // planes
        side = max(1, int(round(math.sqrt(per))))

        def coords(i):
            return (i % side, (i // side) % max(1, per // side), i // per)

        def hops(a, b):
            return sum(abs(p - q) for p, q in zip(coords(a), coords(b)))

        low = [i for i in range(chips) if coords(i)[2] < planes // 2]
        low.sort(key=lambda i: (-(sum(coords(i)) % 2), -coords(i)[2], i))
        high = [i for i in range(chips) if coords(i)[2] >= planes // 2]
        high.sort(key=lambda i: (-(sum(coords(i)) % 2), coords(i)[2], i))
        order = [c for pair in zip(low, high) for c in pair]
        self.heavy = order[:swiglu_count]
        rest = order[swiglu_count:]
        self.light = rest[:square_count]
        helpers = rest
        narrow = D // cores
        wide = FF // cores
        self.granules = (wide - narrow) // GRANULE
        self.passes = self.granules - 2
        count = len(helpers)
        take = [
            [helpers[(k + p * swiglu_count) % count] for k in range(swiglu_count)]
            for p in range(self.passes)
        ]
        cost = lambda p, k, h: hops(h, self.heavy[k]) ** 2
        better = True
        while better:
            better = False
            places = [(p, k) for p in range(self.passes) for k in range(swiglu_count)]
            for p, k in places:
                for h in helpers:
                    used = sum(row.count(h) for row in take)
                    if used < 2 and h not in take[p] and cost(p, k, h) < cost(p, k, take[p][k]):
                        take[p][k] = h
                        better = True
                for q, m in places:
                    a, b = take[p][k], take[q][m]
                    if a == b or (q != p and (b in take[p] or a in take[q])):
                        continue
                    if cost(p, k, b) + cost(q, m, a) < cost(p, k, a) + cost(q, m, b):
                        take[p][k], take[q][m] = b, a
                        better = True
        self.take = take
        self.held = {o: [(j, 0), (j, 1)] for j, o in enumerate(self.heavy)}
        self.place = {}
        for p in range(self.passes):
            for k in range(swiglu_count):
                h = take[p][k]
                self.held.setdefault(h, []).append((k, 2 + p))
        for chip, list_of in self.held.items():
            for where, item in enumerate(list_of):
                self.place[item] = (chip, where)
        self.is_heavy = np.array([c in self.heavy for c in range(chips)])
        self.slot_in_pass = np.zeros((max(1, self.passes), chips), np.bool_)
        for p in range(self.passes):
            for k in range(swiglu_count):
                self.slot_in_pass[p, take[p][k]] = self.place[(k, 2 + p)][1] == 1
        self.idle = [c for c in range(chips) if c not in self.heavy and c not in self.light]


def prepare_kernel(plan, cores, sg, ss, wg, ws, sn, wn, first, second, sv, wv):
    narrow_tiles = D // cores // LANE
    wide_tiles = FF // cores // LANE
    for grad, state, following, sent in ((wg, ws, wn, wv), (sg, ss, sn, sv)):

        def row(r, carry):
            after = MOMENTUM * state[r] + grad[r]
            following[r] = after
            sent[r] = grad[r] + MOMENTUM * after
            return carry

        lax.fori_loop(0, grad.shape[0], row, 0)

    def piece(sent, row_tile, slot):
        return sent[:, row_tile, slot, :].astype(jnp.bfloat16)

    for j, owner in enumerate(plan.heavy):
        for core in range(cores):
            for t in range(wide_tiles):
                value = piece(wv, core * wide_tiles + t, j)
                if t < narrow_tiles:
                    first[owner * cores + core, :, t * LANE : (t + 1) * LANE] = value
                else:
                    b, part = divmod(t - narrow_tiles, GRANULE // LANE)
                    chip, where = plan.place[(j, b)]
                    at = where * GRANULE + part * LANE
                    second[chip * cores + core, :, at : at + LANE] = value
    for j, owner in enumerate(plan.light):
        for core in range(cores):
            for t in range(narrow_tiles):
                value = piece(sv, core * narrow_tiles + t, j)
                first[owner * cores + core, :, t * LANE : (t + 1) * LANE] = value
    for chip in range(len(plan.is_heavy)):
        for core in range(cores):
            if chip in plan.idle:
                first[chip * cores + core] = jnp.zeros(first.shape[1:], first.dtype)
            for where in range(len(plan.held.get(chip, [])), 2):
                second[chip * cores + core, :, where * GRANULE : (where + 1) * GRANULE] = jnp.zeros(
                    (first.shape[1], GRANULE), first.dtype
                )


def prepare(plan, chips, cores, square_grad, square_state, swiglu_grad, swiglu_state):
    rows = D // (chips * cores)
    chunk = 16 if rows % 16 == 0 else rows
    square_count, swiglu_count = square_grad.shape[0], swiglu_grad.shape[0]

    def tiles(x, width):
        count = x.shape[0]
        return x.reshape(count, rows, width // LANE, LANE).transpose(1, 2, 0, 3)

    def flat(x, width):
        return x.transpose(2, 0, 1, 3).reshape(x.shape[2], rows * width)

    narrow = D // cores
    square_block = pl.BlockSpec((chunk, D // LANE, square_count, LANE), lambda i: (i, 0, 0, 0))
    swiglu_block = pl.BlockSpec((chunk, FF // LANE, swiglu_count, LANE), lambda i: (i, 0, 0, 0))
    devices = chips * cores
    out = pl.pallas_call(
        lambda *refs: prepare_kernel(plan, cores, *refs),
        grid=(rows // chunk,),
        in_specs=[square_block, square_block, swiglu_block, swiglu_block],
        out_specs=[
            square_block,
            swiglu_block,
            pl.BlockSpec((devices, chunk, narrow), lambda i: (0, i, 0)),
            pl.BlockSpec((devices, chunk, 2 * GRANULE), lambda i: (0, i, 0)),
        ],
        out_shape=[
            jax.ShapeDtypeStruct((rows, D // LANE, square_count, LANE), jnp.float32),
            jax.ShapeDtypeStruct((rows, FF // LANE, swiglu_count, LANE), jnp.float32),
            jax.ShapeDtypeStruct((devices, rows, narrow), jnp.bfloat16),
            jax.ShapeDtypeStruct((devices, rows, 2 * GRANULE), jnp.bfloat16),
        ],
        scratch_shapes=[
            pltpu.VMEM((chunk, D // LANE, square_count, LANE), jnp.float32),
            pltpu.VMEM((chunk, FF // LANE, swiglu_count, LANE), jnp.float32),
        ],
        compiler_params=pltpu.CompilerParams(vmem_limit_bytes=56 * 1024 * 1024),
        name="prepare",
    )(tiles(square_grad, D), tiles(square_state, D), tiles(swiglu_grad, FF), tiles(swiglu_state, FF))
    return flat(out[0], D), flat(out[1], FF), out[2], out[3]


def other_core(x):
    return lax.ppermute(x, "tensor", [(0, 1), (1, 0)])


BLOCK = 256
EDGE = D // BLOCK
NEAR = EDGE // 2
PACKED = EDGE * NEAR + NEAR
GROUPS = EDGE + 1
MIB = 1024 * 1024


def each_pair(body, after=None):
    def row(i, carry):
        for d in range(NEAR):
            j = lax.rem(i + d, EDGE)
            body(i * NEAR + d, i, j, d == 0)
        if after is not None:
            after(i)
        return carry

    lax.fori_loop(0, EDGE, row, 0)
    for i in range(NEAR):
        body(EDGE * NEAR + i, i, i + NEAR, False)
    if after is not None:
        after(EDGE)


def span(i):
    if isinstance(i, int):
        return pl.ds(i * BLOCK, BLOCK)
    return pl.ds(pl.multiple_of(i * BLOCK, BLOCK), BLOCK)


def group(ref, g):
    return ref.at[pl.ds(g * NEAR, NEAR)]


def rows_of(ref, i):
    return ref.at[span(i), :]


def columns_of(ref, at, width):
    return ref.at[:, pl.ds(at, width)]


def gram_blocks(x, width, out, after):
    def body(slot, i, j, diagonal):
        out[slot] = lax.dot_general(
            x[span(i), :width],
            x[span(j), :width],
            (((1,), (1,)), ((), ())),
            preferred_element_type=jnp.float32,
        )

    each_pair(body, after)


def mirror(out, i, j, diagonal, value):
    rounded = value.astype(out.dtype)
    out[span(i), span(j)] = rounded
    if not diagonal:
        out[span(j), span(i)] = rounded.T


def polynomial_blocks(normed, out):
    def body(slot, i, j, diagonal):
        squared = jnp.dot(normed[span(i), :], normed[:, span(j)], preferred_element_type=jnp.float32)
        value = QUINTIC_CUBIC * normed[span(i), span(j)].astype(jnp.float32) + QUINTIC_FIFTH * squared
        mirror(out, i, j, diagonal, value)

    each_pair(body)


def mixed_rows(polynomial, x, width, scale, out, before=None, after=None):
    def row(i, carry):
        if before is not None:
            before(i)
        for c in range(0, width, BLOCK):
            product = jnp.dot(
                polynomial[span(i), :], x[:, c : c + BLOCK], preferred_element_type=jnp.float32
            )
            mixed = QUINTIC_LINEAR * x[span(i), c : c + BLOCK].astype(jnp.float32) + product
            out[span(i), c : c + BLOCK] = (mixed * scale).astype(out.dtype)
        if after is not None:
            after(i)
        return carry

    lax.fori_loop(0, EDGE, row, 0)


def column_copies(sources, x, sems):
    copies, at = [], 0
    for k, source in enumerate(sources):
        width = source.shape[1]
        copies.append(pltpu.make_async_copy(source, columns_of(x, at, width), sems.at[k]))
        at += width
    return copies


def start_all(copies):
    for copy in copies:
        copy.start()


def wait_all(copies):
    for copy in copies:
        copy.wait()


def by_kind(flag, narrow, wide, body):
    @pl.when(flag[0] > 0)
    def _():
        body(wide)

    @pl.when(flag[0] <= 0)
    def _():
        body(narrow)


def gram_kernel(flag, *refs):
    parts, (out, x, blocks, in_sems, out_sems) = refs[:-5], refs[-5:]
    copies = column_copies(parts, x, in_sems)

    def send(g):
        pltpu.make_async_copy(group(blocks, g), group(out, g), out_sems.at[g]).start()

    def run(width):
        used = copies[: 1 if width < x.shape[1] else len(copies)]
        start_all(used)
        wait_all(used)
        gram_blocks(x, width, blocks, send)

    by_kind(flag, parts[0].shape[1], x.shape[1], run)
    wait_all(
        [
            pltpu.make_async_copy(group(blocks, g), group(out, g), out_sems.at[g])
            for g in range(GROUPS)
        ]
    )


def group_copies(source, target, sems):
    return [
        pltpu.make_async_copy(group(source, g), group(target, g), sems.at[g]) for g in range(GROUPS)
    ]


def middle_kernel(flag, own_in, other_in, *refs):
    parts, refs = refs[:-15], refs[-15:]
    first_out, second_out, packed_out, scale_out = refs[:4]
    own, other, x, mixed, normed, polynomial = refs[4:10]
    own_sems, other_sems, x_sems, mixed_sems, packed_sems = refs[10:]
    narrow, wide = first_out.shape[1], x.shape[1]
    own_copies = group_copies(own_in, own, own_sems)
    other_copies = group_copies(other_in, other, other_sems)
    x_copies = column_copies(parts, x, x_sems)
    for a, b in zip(own_copies, other_copies):
        a.start()
        b.start()
    by_kind(flag, 1, len(x_copies), lambda used: start_all(x_copies[:used]))

    once = jnp.zeros((8, BLOCK), jnp.float32)
    twice = jnp.zeros((8, BLOCK), jnp.float32)
    for g in range(GROUPS):
        own_copies[g].wait()
        other_copies[g].wait()
        for d in range(NEAR):
            slot = g * NEAR + d
            gram = own[slot] + other[slot]
            own[slot] = gram
            squares = jnp.sum((gram * gram).reshape(BLOCK // 8, 8, BLOCK), axis=0)
            if d == 0 and g < EDGE:
                once += squares
            else:
                twice += squares
    total = jnp.full((8, LANE), jnp.sum(once + 2.0 * twice), jnp.float32)
    scale = jnp.sqrt(total) + 1e-06
    scale_out[...] = scale
    inverse = (1.0 / scale)[0:1, 0:1]
    root = (1.0 / jnp.sqrt(scale))[0:1, 0:1]
    each_pair(lambda slot, i, j, diagonal: mirror(normed, i, j, diagonal, own[slot] * inverse))
    polynomial_blocks(normed, polynomial)

    def send(g):
        pltpu.make_async_copy(group(other, g), group(packed_out, g), packed_sems.at[g]).start()

    def run(width):
        used = x_copies[: 1 if width < wide else len(x_copies)]
        wait_all(used)
        mixed_rows(polynomial, x, width, root, mixed)
        sends = [pltpu.make_async_copy(columns_of(mixed, 0, narrow), first_out, mixed_sems.at[0])]
        if width == wide:
            rest = columns_of(mixed, narrow, wide - narrow)
            sends.append(pltpu.make_async_copy(rest, second_out, mixed_sems.at[1]))
        start_all(sends)
        gram_blocks(mixed, width, other, send)
        wait_all(sends)

    by_kind(flag, narrow, wide, run)
    wait_all(group_copies(other, packed_out, packed_sems))


def last_kernel(factor, own_in, other_in, x_in, polynomial_out, out, *refs):
    own, other, x, mixed, normed, polynomial = refs[:6]
    own_sems, other_sems, x_sem, polynomial_sem, out_sems = refs[6:]
    own_copies = group_copies(own_in, own, own_sems)
    other_copies = group_copies(other_in, other, other_sems)
    for a, b in zip(own_copies, other_copies):
        a.start()
        b.start()
    x_copy = pltpu.make_async_copy(x_in, x, x_sem)
    x_copy.start()
    for g in range(GROUPS):
        own_copies[g].wait()
        other_copies[g].wait()
        for d in range(NEAR):
            slot = g * NEAR + d
            i, j = (g, (g + d) % EDGE) if g < EDGE else (d, d + NEAR)
            mirror(normed, i, j, i == j, own[slot] + other[slot])
    polynomial_blocks(normed, polynomial)
    polynomial_copy = pltpu.make_async_copy(polynomial, polynomial_out, polynomial_sem)
    polynomial_copy.start()
    x_copy.wait()

    def out_copy(i):
        return pltpu.make_async_copy(rows_of(mixed, i), rows_of(out, i), out_sems.at[i])

    mixed_rows(
        polynomial, x, x.shape[1], factor[0], mixed, after=lambda i: out_copy(i).start()
    )
    wait_all([out_copy(i) for i in range(EDGE)])
    polynomial_copy.wait()


def rest_kernel(flag, factor, polynomial_in, x_in, *refs):
    outs, (x, mixed, polynomial, x_sem, polynomial_sems, out_sems) = refs[:-6], refs[-6:]
    x_copy = pltpu.make_async_copy(x_in, x, x_sem)

    def polynomial_copy(i):
        return pltpu.make_async_copy(
            rows_of(polynomial_in, i), rows_of(polynomial, i), polynomial_sems.at[i]
        )

    def out_copies(i):
        copies, at = [], 0
        for k, out in enumerate(outs):
            width = out.shape[1]
            source = mixed.at[span(i), pl.ds(at, width)]
            copies.append(pltpu.make_async_copy(source, rows_of(out, i), out_sems.at[k, i]))
            at += width
        return copies

    @pl.when(flag[0] > 0)
    def _():
        x_copy.start()
        start_all([polynomial_copy(i) for i in range(EDGE)])
        x_copy.wait()
        mixed_rows(
            polynomial,
            x,
            x.shape[1],
            factor[0],
            mixed,
            before=lambda i: polynomial_copy(i).wait(),
            after=lambda i: start_all(out_copies(i)),
        )
        for i in range(EDGE):
            wait_all(out_copies(i))


def call(kernel, name, scalars, arrays, outs, scratch, limit, flops, small_outs=0):
    moved = sum(x.size * x.dtype.itemsize for x in arrays)
    moved += sum(math.prod(o.shape) * o.dtype.itemsize for o in outs)
    smem = pl.BlockSpec(memory_space=pltpu.SMEM)
    anywhere = pl.BlockSpec(memory_space=pl.ANY)
    vmem = pl.BlockSpec(memory_space=pltpu.VMEM)
    return pl.pallas_call(
        kernel,
        in_specs=[smem] * len(scalars) + [anywhere] * len(arrays),
        out_specs=[anywhere] * (len(outs) - small_outs) + [vmem] * small_outs,
        out_shape=list(outs),
        scratch_shapes=list(scratch),
        compiler_params=pltpu.CompilerParams(vmem_limit_bytes=limit * MIB),
        cost_estimate=pl.CostEstimate(flops=flops, bytes_accessed=moved, transcendentals=0),
        name=name,
    )(*scalars, *arrays)


def assemble_squares(plan, square_order, first_back):
    count = square_order.shape[0]
    shape = first_back.shape[1:]

    def kernel(order, chip_of, source, out):
        out[...] = source[...]

    return pl.pallas_call(
        kernel,
        grid_spec=pltpu.PrefetchScalarGridSpec(
            num_scalar_prefetch=2,
            grid=(count,),
            in_specs=[pl.BlockSpec((1,) + shape, lambda j, order, chip_of: (chip_of[j], 0, 0))],
            out_specs=pl.BlockSpec((1,) + shape, lambda j, order, chip_of: (order[j], 0, 0)),
        ),
        out_shape=jax.ShapeDtypeStruct((count,) + shape, jnp.bfloat16),
        name="assemble_squares",
    )(square_order, jnp.asarray(plan.light, jnp.int32), first_back)


def assemble_swiglu(plan, swiglu_order, first_back, second_back):
    count = swiglu_order.shape[0]
    rows, narrow = first_back.shape[1:]
    wide = narrow + plan.granules * GRANULE
    extra = range(2, plan.granules)
    chips = [plan.heavy[j] for j in range(count)]
    places = [plan.place[(j, b)] for b in extra for j in range(count)]
    table = np.array(chips + [c for c, _ in places] + [w for _, w in places], np.int32)

    def kernel(order, where, first, own, *refs):
        out = refs[-1]
        out[0, :, :narrow] = first[0]
        out[0, :, narrow : narrow + 2 * GRANULE] = own[0]
        for k, ref in enumerate(refs[:-1]):
            at = narrow + (2 + k) * GRANULE
            out[0, :, at : at + GRANULE] = ref[0]

    def granule(k):
        def index(j, order, where):
            at = (1 + k) * count + j
            return where[at], 0, where[len(extra) * count + at]

        return pl.BlockSpec((1, rows, GRANULE), index)

    return pl.pallas_call(
        kernel,
        grid_spec=pltpu.PrefetchScalarGridSpec(
            num_scalar_prefetch=2,
            grid=(count,),
            in_specs=[
                pl.BlockSpec((1, rows, narrow), lambda j, order, where: (where[j], 0, 0)),
                pl.BlockSpec((1, rows, 2 * GRANULE), lambda j, order, where: (where[j], 0, 0)),
            ]
            + [granule(k) for k in range(len(extra))],
            out_specs=pl.BlockSpec((1, rows, wide), lambda j, order, where: (order[j], 0, 0)),
        ),
        out_shape=jax.ShapeDtypeStruct((count, rows, wide), jnp.bfloat16),
        name="assemble_swiglu",
    )(swiglu_order, jnp.asarray(table), first_back, *([second_back] * (1 + len(extra))))


def spread(value, chips, chip):
    known = jnp.where(jnp.arange(chips, dtype=jnp.int32) == chip, value, 0.0)
    step = 1
    while step < chips:
        known = known + lax.ppermute(known, "dp", [(s, s ^ step) for s in range(chips)])
        step *= 2
    return known


def lookup(table, positions):
    matches = positions[:, None] == jnp.arange(table.shape[0], dtype=jnp.int32)[None, :]
    return jnp.sum(jnp.where(matches, table[None, :], 0), axis=1)


def local(
    square_grad,
    square_state,
    swiglu_grad,
    swiglu_state,
    square_order,
    swiglu_order,
    owners,
    vector_values,
    vector_grad,
    vector_first,
    vector_second,
    embed_values,
    embed_grad,
    embed_first,
    embed_second,
    embed_ranges,
):
    chips = lax.axis_size("dp")
    cores = lax.axis_size("tensor")
    chip = lax.axis_index("dp")
    square_count = square_grad.shape[0]
    swiglu_count = swiglu_grad.shape[0]
    chip_rows = D // chips
    narrow = D // cores
    plan = Plan(chips, cores, square_count, swiglu_count)

    square_next, swiglu_next, first_send, second_send = prepare(
        plan, chips, cores, square_grad, square_state, swiglu_grad, swiglu_state
    )
    both = ("dp", "tensor")
    second_got = lax.all_to_all(
        second_send.reshape(D, 2 * GRANULE), both, split_axis=0, concat_axis=0, tiled=True
    )
    first_got = lax.all_to_all(
        first_send.reshape(D, narrow), both, split_axis=0, concat_axis=0, tiled=True
    )
    heavy_here = jnp.asarray(plan.is_heavy)[chip]
    pieces = [second_got[:, :GRANULE], second_got[:, GRANULE:]]
    relayed = []
    for p in range(plan.passes):
        pick = jnp.asarray(plan.slot_in_pass[p])[chip]
        pairs = [(plan.take[p][k], plan.heavy[k]) for k in range(swiglu_count)]
        relayed.append(lax.ppermute(jnp.where(pick, pieces[1], pieces[0]), "dp", pairs))
    flag = heavy_here.astype(jnp.int32).reshape(1)
    factor = jnp.where(heavy_here, jnp.float32(math.sqrt(FF)), jnp.float32(math.sqrt(D))).reshape(1)
    packed = jax.ShapeDtypeStruct((PACKED, BLOCK, BLOCK), jnp.float32)
    whole_square = jax.ShapeDtypeStruct((D, D), jnp.bfloat16)
    first_shape = jax.ShapeDtypeStruct((D, narrow), jnp.bfloat16)
    extra = plan.granules * GRANULE
    second_shape = jax.ShapeDtypeStruct((D, extra), jnp.bfloat16)
    square_buffer = pltpu.VMEM((D, D), jnp.bfloat16)
    packed_buffer = pltpu.VMEM(packed.shape, jnp.float32)
    matrix_buffer = pltpu.VMEM((D, narrow + extra), jnp.bfloat16)
    first_buffer = pltpu.VMEM((D, narrow), jnp.bfloat16)
    second_buffer = pltpu.VMEM((D, extra), jnp.bfloat16)
    sems = lambda *shape: pltpu.SemaphoreType.DMA(shape)
    half = D * D * (narrow + extra)
    parts = [first_got, second_got, *relayed]
    (own,) = call(
        gram_kernel,
        "gram",
        [flag],
        parts,
        [packed],
        [matrix_buffer, packed_buffer, sems(len(parts)), sems(GROUPS)],
        18,
        half,
    )
    first_mid, second_mid, own_mid, scale = call(
        middle_kernel,
        "middle",
        [flag],
        [own, other_core(own), *parts],
        [first_shape, second_shape, packed, jax.ShapeDtypeStruct((8, LANE), jnp.float32)],
        [packed_buffer] * 2
        + [matrix_buffer] * 2
        + [square_buffer] * 2
        + [sems(GROUPS), sems(GROUPS), sems(len(parts)), sems(2), sems(GROUPS)],
        44,
        3 * half + D * D * D,
        small_outs=1,
    )
    polynomial, first_done = call(
        last_kernel,
        "last",
        [factor],
        [own_mid, other_core(own_mid), first_mid],
        [whole_square, first_shape],
        [packed_buffer] * 2
        + [first_buffer] * 2
        + [square_buffer] * 2
        + [sems(GROUPS), sems(GROUPS), sems(), sems(), sems(EDGE)],
        34,
        D * D * D + 2 * D * D * narrow,
    )
    piece_shape = jax.ShapeDtypeStruct((D, GRANULE), jnp.bfloat16)
    rest = call(
        rest_kernel,
        "rest",
        [flag, factor],
        [polynomial, second_mid],
        [jax.ShapeDtypeStruct((D, 2 * GRANULE), jnp.bfloat16)] + [piece_shape] * plan.passes,
        [second_buffer] * 2 + [square_buffer, sems(), sems(EDGE), sems(1 + plan.passes, EDGE)],
        20,
        2 * D * D * extra,
    )
    logs = spread(0.5 * jnp.log(scale[0, 0]), chips, chip)

    def send_back(x):
        return lax.all_to_all(
            x.reshape(chips, chip_rows, -1), "dp", split_axis=0, concat_axis=0, tiled=True
        )

    first_back = send_back(first_done)
    handed = []
    for p in range(plan.passes):
        pairs = [(plan.heavy[k], plan.take[p][k]) for k in range(swiglu_count)]
        handed.append(lax.ppermute(rest[1 + p], "dp", pairs))
    halves = []
    for where in range(2):
        value = rest[0][:, where * GRANULE : (where + 1) * GRANULE]
        for p in range(plan.passes):
            mine = np.zeros((chips,), np.bool_)
            for k in range(swiglu_count):
                if plan.place[(k, 2 + p)][1] == where:
                    mine[plan.take[p][k]] = True
            value = jnp.where(jnp.asarray(mine)[chip], handed[p], value)
        halves.append(value)
    second_out, first_back = lax.optimization_barrier((jnp.concatenate(halves, axis=1), first_back))
    second_back = send_back(second_out)

    square_update = assemble_squares(plan, square_order, first_back)
    swiglu_update = assemble_swiglu(plan, swiglu_order, first_back, second_back)

    slot_chips = np.array(plan.light + plan.heavy, np.int32)
    slot_owner = jnp.concatenate(
        [lookup(owners[:square_count], square_order), lookup(owners[square_count:], swiglu_order)]
    )
    slot_logs = logs[slot_chips]
    owner_norms = jnp.sum(jnp.where(slot_owner == chip, slot_logs, 0.0)).reshape(1)

    vector_step, first_vector, second_vector = adamw_terms(
        vector_values, vector_grad, vector_first, vector_second
    )
    embed_rows = embed_values.shape[0]
    row_numbers = chip * embed_rows + jnp.arange(embed_rows, dtype=jnp.int32)
    inside = (row_numbers[:, None] >= embed_ranges[None, :, 0]) & (
        row_numbers[:, None] < embed_ranges[None, :, 1]
    )
    row_live = jnp.sum(inside.astype(jnp.int32), axis=1) > 0
    direction, first_next, second_next = adamw_terms(
        embed_values, embed_grad, embed_first, embed_second
    )
    embed_step = jnp.where(row_live[:, None], direction, 0.0)
    first_embed = jnp.where(row_live[:, None], first_next, embed_first)
    second_embed = jnp.where(row_live[:, None], second_next, embed_second)
    return (
        square_next,
        swiglu_next,
        square_update,
        swiglu_update,
        owner_norms,
        vector_step,
        first_vector,
        second_vector,
        embed_step,
        first_embed,
        second_embed,
    )


def solution(mesh):
    flat = P(None, ("dp", "tensor"))
    vector = P(("dp", "tensor"))
    tile = P("dp", "tensor")
    update = P(None, "dp", "tensor")
    return jax.shard_map(
        local,
        mesh=mesh,
        in_specs=(flat,) * 4 + (P(),) * 3 + (vector,) * 4 + (tile,) * 4 + (P(),),
        out_specs=(flat, flat, update, update, P("dp")) + (vector,) * 3 + (tile,) * 3,
        check_vma=False,
    )
```

```python
import math

import jax
import jax.numpy as jnp
import numpy as np
from jax import lax
from jax.experimental import pallas as pl
from jax.experimental.pallas import tpu as pltpu
from jax.sharding import PartitionSpec as P

D = 1536
FF = 4096
NS_STEPS = 2


QUINTIC_LINEAR = 3.4445
QUINTIC_CUBIC = -4.775
QUINTIC_FIFTH = 2.0315
MOMENTUM = 0.95
BIAS_FIRST = 1.0 - 0.9**10
BIAS_SECOND = 1.0 - 0.95**10


def momentum_terms(gradient, state):
    state_next = MOMENTUM * state + gradient
    return (state_next, (gradient + MOMENTUM * state_next).astype(jnp.bfloat16))


def adamw_terms(values, gradient, first, second):
    first_next = 0.9 * first + 0.1 * gradient
    second_next = 0.95 * second + 0.05 * gradient * gradient
    direction = (
        first_next / BIAS_FIRST / (jnp.sqrt(second_next / BIAS_SECOND) + 1e-08) + 0.1 * values
    )
    return (direction, first_next, second_next)


LANE = 128
GRANULE = 256


class Plan:
    def __init__(self, chips, cores, square_count, swiglu_count):
        planes = 4
        per = chips // planes
        side = max(1, int(round(math.sqrt(per))))

        def coords(i):
            return (i % side, (i // side) % max(1, per // side), i // per)

        def hops(a, b):
            return sum(abs(p - q) for p, q in zip(coords(a), coords(b)))

        low = [i for i in range(chips) if coords(i)[2] < planes // 2]
        low.sort(key=lambda i: (-(sum(coords(i)) % 2), -coords(i)[2], i))
        high = [i for i in range(chips) if coords(i)[2] >= planes // 2]
        high.sort(key=lambda i: (-(sum(coords(i)) % 2), coords(i)[2], i))
        order = [c for pair in zip(low, high) for c in pair]
        self.heavy = order[:swiglu_count]
        rest = order[swiglu_count:]
        self.light = rest[:square_count]
        helpers = rest
        narrow = D // cores
        wide = FF // cores
        self.granules = (wide - narrow) // GRANULE
        self.passes = self.granules - 2
        count = len(helpers)
        take = [
            [helpers[(k + p * swiglu_count) % count] for k in range(swiglu_count)]
            for p in range(self.passes)
        ]
        cost = lambda p, k, h: hops(h, self.heavy[k]) ** 2
        better = True
        while better:
            better = False
            places = [(p, k) for p in range(self.passes) for k in range(swiglu_count)]
            for p, k in places:
                for h in helpers:
                    used = sum(row.count(h) for row in take)
                    if used < 2 and h not in take[p] and cost(p, k, h) < cost(p, k, take[p][k]):
                        take[p][k] = h
                        better = True
                for q, m in places:
                    a, b = take[p][k], take[q][m]
                    if a == b or (q != p and (b in take[p] or a in take[q])):
                        continue
                    if cost(p, k, b) + cost(q, m, a) < cost(p, k, a) + cost(q, m, b):
                        take[p][k], take[q][m] = b, a
                        better = True
        self.take = take
        self.held = {o: [(j, 0), (j, 1)] for j, o in enumerate(self.heavy)}
        self.place = {}
        for p in range(self.passes):
            for k in range(swiglu_count):
                h = take[p][k]
                self.held.setdefault(h, []).append((k, 2 + p))
        for chip, list_of in self.held.items():
            for where, item in enumerate(list_of):
                self.place[item] = (chip, where)
        self.is_heavy = np.array([c in self.heavy for c in range(chips)])
        self.slot_in_pass = np.zeros((max(1, self.passes), chips), np.bool_)
        for p in range(self.passes):
            for k in range(swiglu_count):
                self.slot_in_pass[p, take[p][k]] = self.place[(k, 2 + p)][1] == 1
        self.idle = [c for c in range(chips) if c not in self.heavy and c not in self.light]


def momentum_rows(grad, state, following, sent):
    def row(r, carry):
        after = MOMENTUM * state[r] + grad[r]
        following[r] = after
        sent[r] = grad[r] + MOMENTUM * after
        return carry

    lax.fori_loop(0, grad.shape[0], row, 0)


def wide_kernel(plan, cores, grad, state, following, first, second, sent):
    narrow_tiles = D // cores // LANE
    wide_tiles = FF // cores // LANE
    momentum_rows(grad, state, following, sent)
    for j, owner in enumerate(plan.heavy):
        for core in range(cores):
            for t in range(wide_tiles):
                value = sent[:, core * wide_tiles + t, j, :].astype(jnp.bfloat16)
                if t < narrow_tiles:
                    first[owner * cores + core, :, t * LANE : (t + 1) * LANE] = value
                else:
                    b, part = divmod(t - narrow_tiles, GRANULE // LANE)
                    chip, where = plan.place[(j, b)]
                    at = where * GRANULE + part * LANE
                    second[chip * cores + core, :, at : at + LANE] = value
    for chip in range(len(plan.is_heavy)):
        for core in range(cores):
            if chip in plan.idle:
                first[chip * cores + core] = jnp.zeros(first.shape[1:], first.dtype)
            for where in range(len(plan.held.get(chip, [])), 2):
                second[chip * cores + core, :, where * GRANULE : (where + 1) * GRANULE] = jnp.zeros(
                    (first.shape[1], GRANULE), first.dtype
                )


def narrow_kernel(plan, cores, grad, state, given, following, first, sent, stage, sems):
    narrow_tiles = D // cores // LANE
    momentum_rows(grad, state, following, sent)
    copies = []
    for j, owner in enumerate(plan.light):
        for core in range(cores):
            for t in range(narrow_tiles):
                value = sent[:, core * narrow_tiles + t, j, :].astype(jnp.bfloat16)
                stage[j * cores + core, :, t * LANE : (t + 1) * LANE] = value
        copies.append(
            pltpu.make_async_copy(
                stage.at[pl.ds(j * cores, cores)], first.at[pl.ds(owner * cores, cores)], sems.at[j]
            )
        )
        copies[-1].start()
    for copy in copies:
        copy.wait()


def tiles_of(x, rows, width):
    return x.reshape(x.shape[0], rows, width // LANE, LANE).transpose(1, 2, 0, 3)


def flat_of(x):
    return x.transpose(2, 0, 1, 3).reshape(x.shape[2], -1)


def prepare_wide(plan, chips, cores, grad, state):
    rows = D // (chips * cores)
    chunk = 16 if rows % 16 == 0 else rows
    count = grad.shape[0]
    narrow = D // cores
    devices = chips * cores
    block = (chunk, FF // LANE, count, LANE)
    spec = pl.BlockSpec(block, lambda i: (i, 0, 0, 0))
    following, first, second = pl.pallas_call(
        lambda *refs: wide_kernel(plan, cores, *refs),
        grid=(rows // chunk,),
        in_specs=[spec, spec],
        out_specs=[
            spec,
            pl.BlockSpec((devices, chunk, narrow), lambda i: (0, i, 0)),
            pl.BlockSpec((devices, chunk, 2 * GRANULE), lambda i: (0, i, 0)),
        ],
        out_shape=[
            jax.ShapeDtypeStruct((rows,) + block[1:], jnp.float32),
            jax.ShapeDtypeStruct((devices, rows, narrow), jnp.bfloat16),
            jax.ShapeDtypeStruct((devices, rows, 2 * GRANULE), jnp.bfloat16),
        ],
        scratch_shapes=[pltpu.VMEM(block, jnp.float32)],
        compiler_params=pltpu.CompilerParams(vmem_limit_bytes=48 * 1024 * 1024),
        name="prepare_wide",
    )(tiles_of(grad, rows, FF), tiles_of(state, rows, FF))
    return flat_of(following), first, second


def prepare_narrow(plan, chips, cores, grad, state, first):
    rows = D // (chips * cores)
    count = grad.shape[0]
    block = (rows, D // LANE, count, LANE)
    vmem = pl.BlockSpec(memory_space=pltpu.VMEM)
    anywhere = pl.BlockSpec(memory_space=pl.ANY)
    following, first = pl.pallas_call(
        lambda *refs: narrow_kernel(plan, cores, *refs),
        in_specs=[vmem, vmem, anywhere],
        out_specs=[vmem, anywhere],
        out_shape=[
            jax.ShapeDtypeStruct(block, jnp.float32),
            jax.ShapeDtypeStruct(first.shape, first.dtype),
        ],
        input_output_aliases={2: 1},
        scratch_shapes=[
            pltpu.VMEM(block, jnp.float32),
            pltpu.VMEM((count * cores, rows, D // cores), jnp.bfloat16),
            pltpu.SemaphoreType.DMA((count,)),
        ],
        compiler_params=pltpu.CompilerParams(vmem_limit_bytes=32 * 1024 * 1024),
        cost_estimate=pl.CostEstimate(
            flops=0, bytes_accessed=3 * grad.size * 4 + grad.size * 2, transcendentals=0
        ),
        name="prepare_narrow",
    )(tiles_of(grad, rows, D), tiles_of(state, rows, D), first)
    return flat_of(following), first


def other_core(x):
    return lax.ppermute(x, "tensor", [(0, 1), (1, 0)])


BLOCK = 256
EDGE = D // BLOCK
NEAR = EDGE // 2
PACKED = EDGE * NEAR + NEAR
GROUPS = EDGE + 1
MIB = 1024 * 1024


def each_pair(body, after=None):
    def row(i, carry):
        for d in range(NEAR):
            j = lax.rem(i + d, EDGE)
            body(i * NEAR + d, i, j, d == 0)
        if after is not None:
            after(i)
        return carry

    lax.fori_loop(0, EDGE, row, 0)
    for i in range(NEAR):
        body(EDGE * NEAR + i, i, i + NEAR, False)
    if after is not None:
        after(EDGE)


def span(i):
    if isinstance(i, int):
        return pl.ds(i * BLOCK, BLOCK)
    return pl.ds(pl.multiple_of(i * BLOCK, BLOCK), BLOCK)


def group(ref, g):
    return ref.at[pl.ds(g * NEAR, NEAR)]


def rows_of(ref, i):
    return ref.at[span(i), :]


def columns_of(ref, at, width):
    return ref.at[:, pl.ds(at, width)]


def gram_blocks(x, width, out, after):
    def body(slot, i, j, diagonal):
        out[slot] = lax.dot_general(
            x[span(i), :width],
            x[span(j), :width],
            (((1,), (1,)), ((), ())),
            preferred_element_type=jnp.float32,
        )

    each_pair(body, after)


def mirror(out, i, j, diagonal, value):
    rounded = value.astype(out.dtype)
    out[span(i), span(j)] = rounded
    if not diagonal:
        out[span(j), span(i)] = rounded.T


def polynomial_blocks(normed, out):
    def body(slot, i, j, diagonal):
        squared = jnp.dot(normed[span(i), :], normed[:, span(j)], preferred_element_type=jnp.float32)
        value = QUINTIC_CUBIC * normed[span(i), span(j)].astype(jnp.float32) + QUINTIC_FIFTH * squared
        mirror(out, i, j, diagonal, value)

    each_pair(body)


def mixed_rows(polynomial, x, width, scale, out, before=None, after=None):
    def row(i, carry):
        if before is not None:
            before(i)
        for c in range(0, width, BLOCK):
            product = jnp.dot(
                polynomial[span(i), :], x[:, c : c + BLOCK], preferred_element_type=jnp.float32
            )
            mixed = QUINTIC_LINEAR * x[span(i), c : c + BLOCK].astype(jnp.float32) + product
            out[span(i), c : c + BLOCK] = (mixed * scale).astype(out.dtype)
        if after is not None:
            after(i)
        return carry

    lax.fori_loop(0, EDGE, row, 0)


def column_copies(sources, x, sems):
    copies, at = [], 0
    for k, source in enumerate(sources):
        width = source.shape[1]
        copies.append(pltpu.make_async_copy(source, columns_of(x, at, width), sems.at[k]))
        at += width
    return copies


def start_all(copies):
    for copy in copies:
        copy.start()


def wait_all(copies):
    for copy in copies:
        copy.wait()


def by_kind(flag, narrow, wide, body):
    @pl.when(flag[0] > 0)
    def _():
        body(wide)

    @pl.when(flag[0] <= 0)
    def _():
        body(narrow)


def gram_kernel(flag, *refs):
    parts, (out, x, blocks, in_sems, out_sems) = refs[:-5], refs[-5:]
    copies = column_copies(parts, x, in_sems)

    def send(g):
        pltpu.make_async_copy(group(blocks, g), group(out, g), out_sems.at[g]).start()

    def run(width):
        used = copies[: 1 if width < x.shape[1] else len(copies)]
        start_all(used)
        wait_all(used)
        gram_blocks(x, width, blocks, send)

    by_kind(flag, parts[0].shape[1], x.shape[1], run)
    wait_all(
        [
            pltpu.make_async_copy(group(blocks, g), group(out, g), out_sems.at[g])
            for g in range(GROUPS)
        ]
    )


def group_copies(source, target, sems):
    return [
        pltpu.make_async_copy(group(source, g), group(target, g), sems.at[g]) for g in range(GROUPS)
    ]


def middle_kernel(flag, own_in, other_in, *refs):
    parts, refs = refs[:-15], refs[-15:]
    first_out, second_out, packed_out, scale_out = refs[:4]
    own, other, x, mixed, normed, polynomial = refs[4:10]
    own_sems, other_sems, x_sems, mixed_sems, packed_sems = refs[10:]
    narrow, wide = first_out.shape[1], x.shape[1]
    own_copies = group_copies(own_in, own, own_sems)
    other_copies = group_copies(other_in, other, other_sems)
    x_copies = column_copies(parts, x, x_sems)
    for a, b in zip(own_copies, other_copies):
        a.start()
        b.start()
    by_kind(flag, 1, len(x_copies), lambda used: start_all(x_copies[:used]))

    once = jnp.zeros((8, BLOCK), jnp.float32)
    twice = jnp.zeros((8, BLOCK), jnp.float32)
    for g in range(GROUPS):
        own_copies[g].wait()
        other_copies[g].wait()
        for d in range(NEAR):
            slot = g * NEAR + d
            gram = own[slot] + other[slot]
            own[slot] = gram
            squares = jnp.sum((gram * gram).reshape(BLOCK // 8, 8, BLOCK), axis=0)
            if d == 0 and g < EDGE:
                once += squares
            else:
                twice += squares
    total = jnp.full((8, LANE), jnp.sum(once + 2.0 * twice), jnp.float32)
    scale = jnp.sqrt(total) + 1e-06
    scale_out[...] = scale
    inverse = (1.0 / scale)[0:1, 0:1]
    root = (1.0 / jnp.sqrt(scale))[0:1, 0:1]
    each_pair(lambda slot, i, j, diagonal: mirror(normed, i, j, diagonal, own[slot] * inverse))
    polynomial_blocks(normed, polynomial)

    def send(g):
        pltpu.make_async_copy(group(other, g), group(packed_out, g), packed_sems.at[g]).start()

    def run(width):
        used = x_copies[: 1 if width < wide else len(x_copies)]
        wait_all(used)
        mixed_rows(polynomial, x, width, root, mixed)
        sends = [pltpu.make_async_copy(columns_of(mixed, 0, narrow), first_out, mixed_sems.at[0])]
        if width == wide:
            rest = columns_of(mixed, narrow, wide - narrow)
            sends.append(pltpu.make_async_copy(rest, second_out, mixed_sems.at[1]))
        start_all(sends)
        gram_blocks(mixed, width, other, send)
        wait_all(sends)

    by_kind(flag, narrow, wide, run)
    wait_all(group_copies(other, packed_out, packed_sems))


def last_kernel(flag, factor, own_in, other_in, x_in, *refs):
    count = len(refs) - 11
    polynomial_out, outs = refs[0], refs[1:count]
    own, other, x, mixed, normed, polynomial = refs[count : count + 6]
    own_sems, other_sems, x_sem, polynomial_sem, out_sems = refs[count + 6 :]
    own_copies = group_copies(own_in, own, own_sems)
    other_copies = group_copies(other_in, other, other_sems)
    for a, b in zip(own_copies, other_copies):
        a.start()
        b.start()
    x_copy = pltpu.make_async_copy(x_in, x, x_sem)
    heavy = flag[0] > 0

    @pl.when(heavy)
    def _():
        x_copy.start()

    for g in range(GROUPS):
        own_copies[g].wait()
        other_copies[g].wait()
        for d in range(NEAR):
            slot = g * NEAR + d
            i, j = (g, (g + d) % EDGE) if g < EDGE else (d, d + NEAR)
            mirror(normed, i, j, i == j, own[slot] + other[slot])
    polynomial_blocks(normed, polynomial)
    polynomial_copy = pltpu.make_async_copy(polynomial, polynomial_out, polynomial_sem)
    polynomial_copy.start()

    def out_copies(i):
        copies, at = [], 0
        for k, out in enumerate(outs):
            width = out.shape[1]
            source = mixed.at[span(i), pl.ds(at, width)]
            copies.append(pltpu.make_async_copy(source, rows_of(out, i), out_sems.at[k, i]))
            at += width
        return copies

    @pl.when(heavy)
    def _():
        x_copy.wait()
        mixed_rows(
            polynomial,
            x,
            x.shape[1],
            factor[0],
            mixed,
            after=lambda i: start_all(out_copies(i)),
        )
        for i in range(EDGE):
            wait_all(out_copies(i))

    polynomial_copy.wait()


def finish_kernel(factor, polynomial_in, x_in, out, x, mixed, polynomial, x_sem, in_sems, out_sems):
    x_copy = pltpu.make_async_copy(x_in, x, x_sem)
    x_copy.start()

    def in_copy(i):
        return pltpu.make_async_copy(rows_of(polynomial_in, i), rows_of(polynomial, i), in_sems.at[i])

    def out_copy(i):
        return pltpu.make_async_copy(rows_of(mixed, i), rows_of(out, i), out_sems.at[i])

    start_all([in_copy(i) for i in range(EDGE)])
    x_copy.wait()
    mixed_rows(
        polynomial,
        x,
        x.shape[1],
        factor[0],
        mixed,
        before=lambda i: in_copy(i).wait(),
        after=lambda i: out_copy(i).start(),
    )
    wait_all([out_copy(i) for i in range(EDGE)])


def join_kernel(pick, own, *refs):
    handed, (out, stage, in_sems, out_sem) = refs[:-4], refs[-4:]
    for where in range(2):
        target = columns_of(stage, where * GRANULE, GRANULE)
        for k in range(1 + len(handed)):
            source = columns_of(own, where * GRANULE, GRANULE) if k == 0 else handed[k - 1]

            @pl.when(pick[where] == k)
            def _():
                pltpu.make_async_copy(source, target, in_sems.at[where]).start()

    for where in range(2):
        target = columns_of(stage, where * GRANULE, GRANULE)
        pltpu.make_async_copy(columns_of(own, 0, GRANULE), target, in_sems.at[where]).wait()
    copy = pltpu.make_async_copy(stage, out, out_sem)
    copy.start()
    copy.wait()


def call(kernel, name, scalars, arrays, outs, scratch, limit, flops, small_outs=0):
    moved = sum(x.size * x.dtype.itemsize for x in arrays)
    moved += sum(math.prod(o.shape) * o.dtype.itemsize for o in outs)
    smem = pl.BlockSpec(memory_space=pltpu.SMEM)
    anywhere = pl.BlockSpec(memory_space=pl.ANY)
    vmem = pl.BlockSpec(memory_space=pltpu.VMEM)
    return pl.pallas_call(
        kernel,
        in_specs=[smem] * len(scalars) + [anywhere] * len(arrays),
        out_specs=[anywhere] * (len(outs) - small_outs) + [vmem] * small_outs,
        out_shape=list(outs),
        scratch_shapes=list(scratch),
        compiler_params=pltpu.CompilerParams(vmem_limit_bytes=limit * MIB),
        cost_estimate=pl.CostEstimate(flops=flops, bytes_accessed=moved, transcendentals=0),
        name=name,
    )(*scalars, *arrays)


def assemble(kernel, name, order, arrays, shape, copies):
    anywhere = pl.BlockSpec(memory_space=pl.ANY)
    return pl.pallas_call(
        kernel,
        in_specs=[pl.BlockSpec(memory_space=pltpu.SMEM)] + [anywhere] * len(arrays),
        out_specs=anywhere,
        out_shape=jax.ShapeDtypeStruct(shape, jnp.bfloat16),
        scratch_shapes=[
            pltpu.VMEM(shape, jnp.bfloat16),
            pltpu.SemaphoreType.DMA((copies,)),
            pltpu.SemaphoreType.DMA((shape[0],)),
        ],
        compiler_params=pltpu.CompilerParams(vmem_limit_bytes=8 * MIB),
        name=name,
    )(order, *arrays)


def place_slots(order, stage, out, copies, out_sems):
    for slot in copies:
        start_all(slot)
    outs = []
    for j, slot in enumerate(copies):
        wait_all(slot)
        outs.append(pltpu.make_async_copy(stage.at[j], out.at[order[j]], out_sems.at[j]))
        outs[-1].start()
    wait_all(outs)


def assemble_squares(plan, square_order, first_back):
    count = square_order.shape[0]

    def kernel(order, source, out, stage, in_sems, out_sems):
        copies = [
            [pltpu.make_async_copy(source.at[plan.light[j]], stage.at[j], in_sems.at[j])]
            for j in range(count)
        ]
        place_slots(order, stage, out, copies, out_sems)

    shape = (count,) + first_back.shape[1:]
    return assemble(kernel, "assemble_squares", square_order, [first_back], shape, count)


def assemble_swiglu(plan, swiglu_order, first_back, second_back):
    count = swiglu_order.shape[0]
    rows, narrow = first_back.shape[1:]
    wide = narrow + plan.granules * GRANULE

    def kernel(order, first, second, out, stage, in_sems, out_sems):
        copies = []
        for j in range(count):
            moves = [
                (first.at[plan.heavy[j]], 0, narrow),
                (second.at[plan.heavy[j]], narrow, 2 * GRANULE),
            ]
            for b in range(2, plan.granules):
                chip, where = plan.place[(j, b)]
                source = second.at[chip, :, pl.ds(where * GRANULE, GRANULE)]
                moves.append((source, narrow + b * GRANULE, GRANULE))
            copies.append(
                [
                    pltpu.make_async_copy(
                        source, stage.at[j, :, pl.ds(at, width)], in_sems.at[j * len(moves) + k]
                    )
                    for k, (source, at, width) in enumerate(moves)
                ]
            )
        place_slots(order, stage, out, copies, out_sems)

    arrays = [first_back, second_back]
    shape = (count, rows, wide)
    return assemble(kernel, "assemble_swiglu", swiglu_order, arrays, shape, count * plan.granules)


def spread(value, chips, chip):
    known = jnp.where(jnp.arange(chips, dtype=jnp.int32) == chip, value, 0.0)
    step = 1
    while step < chips:
        known = known + lax.ppermute(known, "dp", [(s, s ^ step) for s in range(chips)])
        step *= 2
    return known


def lookup(table, positions):
    matches = positions[:, None] == jnp.arange(table.shape[0], dtype=jnp.int32)[None, :]
    return jnp.sum(jnp.where(matches, table[None, :], 0), axis=1)


def local(
    square_grad,
    square_state,
    swiglu_grad,
    swiglu_state,
    square_order,
    swiglu_order,
    owners,
    vector_values,
    vector_grad,
    vector_first,
    vector_second,
    embed_values,
    embed_grad,
    embed_first,
    embed_second,
    embed_ranges,
):
    chips = lax.axis_size("dp")
    cores = lax.axis_size("tensor")
    chip = lax.axis_index("dp")
    square_count = square_grad.shape[0]
    swiglu_count = swiglu_grad.shape[0]
    chip_rows = D // chips
    narrow = D // cores
    plan = Plan(chips, cores, square_count, swiglu_count)

    swiglu_next, first_send, second_send = prepare_wide(
        plan, chips, cores, swiglu_grad, swiglu_state
    )
    square_next, first_send = prepare_narrow(
        plan, chips, cores, square_grad, square_state, first_send
    )
    both = ("dp", "tensor")
    second_got = lax.all_to_all(
        second_send.reshape(D, 2 * GRANULE), both, split_axis=0, concat_axis=0, tiled=True
    )
    first_got = lax.all_to_all(
        first_send.reshape(D, narrow), both, split_axis=0, concat_axis=0, tiled=True
    )
    heavy_here = jnp.asarray(plan.is_heavy)[chip]
    pieces = [second_got[:, :GRANULE], second_got[:, GRANULE:]]
    relayed = []
    for p in range(plan.passes):
        pick = jnp.asarray(plan.slot_in_pass[p])[chip]
        pairs = [(plan.take[p][k], plan.heavy[k]) for k in range(swiglu_count)]
        relayed.append(lax.ppermute(jnp.where(pick, pieces[1], pieces[0]), "dp", pairs))
    flag = heavy_here.astype(jnp.int32).reshape(1)
    factor = jnp.where(heavy_here, jnp.float32(math.sqrt(FF)), jnp.float32(math.sqrt(D))).reshape(1)
    packed = jax.ShapeDtypeStruct((PACKED, BLOCK, BLOCK), jnp.float32)
    whole_square = jax.ShapeDtypeStruct((D, D), jnp.bfloat16)
    first_shape = jax.ShapeDtypeStruct((D, narrow), jnp.bfloat16)
    extra = plan.granules * GRANULE
    second_shape = jax.ShapeDtypeStruct((D, extra), jnp.bfloat16)
    square_buffer = pltpu.VMEM((D, D), jnp.bfloat16)
    packed_buffer = pltpu.VMEM(packed.shape, jnp.float32)
    matrix_buffer = pltpu.VMEM((D, narrow + extra), jnp.bfloat16)
    first_buffer = pltpu.VMEM((D, narrow), jnp.bfloat16)
    second_buffer = pltpu.VMEM((D, extra), jnp.bfloat16)
    sems = lambda *shape: pltpu.SemaphoreType.DMA(shape)
    half = D * D * (narrow + extra)
    parts = [first_got, second_got, *relayed]
    (own,) = call(
        gram_kernel,
        "gram",
        [flag],
        parts,
        [packed],
        [matrix_buffer, packed_buffer, sems(len(parts)), sems(GROUPS)],
        15,
        half,
    )
    first_mid, second_mid, own_mid, scale = call(
        middle_kernel,
        "middle",
        [flag],
        [own, other_core(own), *parts],
        [first_shape, second_shape, packed, jax.ShapeDtypeStruct((8, LANE), jnp.float32)],
        [packed_buffer] * 2
        + [matrix_buffer] * 2
        + [square_buffer] * 2
        + [sems(GROUPS), sems(GROUPS), sems(len(parts)), sems(2), sems(GROUPS)],
        37,
        3 * half + D * D * D,
        small_outs=1,
    )
    piece_shape = jax.ShapeDtypeStruct((D, GRANULE), jnp.bfloat16)
    pair_shape = jax.ShapeDtypeStruct((D, 2 * GRANULE), jnp.bfloat16)
    polynomial, kept, *rest = call(
        last_kernel,
        "last",
        [flag, factor],
        [own_mid, other_core(own_mid), second_mid],
        [whole_square, pair_shape] + [piece_shape] * plan.passes,
        [packed_buffer] * 2
        + [second_buffer] * 2
        + [square_buffer] * 2
        + [sems(GROUPS), sems(GROUPS), sems(), sems(), sems(1 + plan.passes, EDGE)],
        32,
        D * D * D + 2 * D * D * extra,
    )
    handed = []
    for p in range(plan.passes):
        pairs = [(plan.heavy[k], plan.take[p][k]) for k in range(swiglu_count)]
        handed.append(lax.ppermute(rest[p], "dp", pairs))
    (first_done,) = call(
        finish_kernel,
        "finish",
        [factor],
        [polynomial, first_mid],
        [first_shape],
        [first_buffer] * 2 + [square_buffer, sems(), sems(EDGE), sems(EDGE)],
        14,
        2 * D * D * narrow,
    )
    scale, _ = lax.optimization_barrier((scale, first_done))
    logs = spread(0.5 * jnp.log(scale[0, 0]), chips, chip)

    def send_back(x):
        return lax.all_to_all(
            x.reshape(chips, chip_rows, -1), "dp", split_axis=0, concat_axis=0, tiled=True
        )

    first_back = send_back(first_done)
    choice = np.zeros((chips, 2), np.int32)
    for p in range(plan.passes):
        for k in range(swiglu_count):
            choice[plan.take[p][k], plan.place[(k, 2 + p)][1]] = 1 + p
    (second_out,) = call(
        join_kernel,
        "join",
        [jnp.asarray(choice)[chip]],
        [kept, *handed],
        [pair_shape],
        [pltpu.VMEM(pair_shape.shape, jnp.bfloat16), sems(2), sems()],
        4,
        0,
    )
    second_out, first_back, logs = lax.optimization_barrier((second_out, first_back, logs))
    second_back = send_back(second_out)

    square_update = assemble_squares(plan, square_order, first_back)
    swiglu_update = assemble_swiglu(plan, swiglu_order, first_back, second_back)

    slot_chips = np.array(plan.light + plan.heavy, np.int32)
    slot_owner = jnp.concatenate(
        [lookup(owners[:square_count], square_order), lookup(owners[square_count:], swiglu_order)]
    )
    slot_logs = logs[slot_chips]
    owner_norms = jnp.sum(jnp.where(slot_owner == chip, slot_logs, 0.0)).reshape(1)

    vector_step, first_vector, second_vector = adamw_terms(
        vector_values, vector_grad, vector_first, vector_second
    )
    embed_rows = embed_values.shape[0]
    row_numbers = chip * embed_rows + jnp.arange(embed_rows, dtype=jnp.int32)
    inside = (row_numbers[:, None] >= embed_ranges[None, :, 0]) & (
        row_numbers[:, None] < embed_ranges[None, :, 1]
    )
    row_live = jnp.sum(inside.astype(jnp.int32), axis=1) > 0
    direction, first_next, second_next = adamw_terms(
        embed_values, embed_grad, embed_first, embed_second
    )
    embed_step = jnp.where(row_live[:, None], direction, 0.0)
    first_embed = jnp.where(row_live[:, None], first_next, embed_first)
    second_embed = jnp.where(row_live[:, None], second_next, embed_second)
    return (
        square_next,
        swiglu_next,
        square_update,
        swiglu_update,
        owner_norms,
        vector_step,
        first_vector,
        second_vector,
        embed_step,
        first_embed,
        second_embed,
    )


def solution(mesh):
    flat = P(None, ("dp", "tensor"))
    vector = P(("dp", "tensor"))
    tile = P("dp", "tensor")
    update = P(None, "dp", "tensor")
    return jax.shard_map(
        local,
        mesh=mesh,
        in_specs=(flat,) * 4 + (P(),) * 3 + (vector,) * 4 + (tile,) * 4 + (P(),),
        out_specs=(flat, flat, update, update, P("dp")) + (vector,) * 3 + (tile,) * 3,
        check_vma=False,
    )
```

```python
import math

import jax
import jax.numpy as jnp
import numpy as np
from jax import lax
from jax.experimental import pallas as pl
from jax.experimental.pallas import tpu as pltpu
from jax.sharding import PartitionSpec as P

D = 1536
FF = 4096
NS_STEPS = 2


QUINTIC_LINEAR = 3.4445
QUINTIC_CUBIC = -4.775
QUINTIC_FIFTH = 2.0315
MOMENTUM = 0.95
BIAS_FIRST = 1.0 - 0.9**10
BIAS_SECOND = 1.0 - 0.95**10


def momentum_terms(gradient, state):
    state_next = MOMENTUM * state + gradient
    return (state_next, (gradient + MOMENTUM * state_next).astype(jnp.bfloat16))


def adamw_terms(values, gradient, first, second):
    first_next = 0.9 * first + 0.1 * gradient
    second_next = 0.95 * second + 0.05 * gradient * gradient
    direction = (
        first_next / BIAS_FIRST / (jnp.sqrt(second_next / BIAS_SECOND) + 1e-08) + 0.1 * values
    )
    return (direction, first_next, second_next)


LANE = 128
GRANULE = 256


class Plan:
    def __init__(self, chips, cores, square_count, swiglu_count):
        planes = 4
        per = chips // planes
        side = max(1, int(round(math.sqrt(per))))

        def coords(i):
            return (i % side, (i // side) % max(1, per // side), i // per)

        def hops(a, b):
            return sum(abs(p - q) for p, q in zip(coords(a), coords(b)))

        low = [i for i in range(chips) if coords(i)[2] < planes // 2]
        low.sort(key=lambda i: (-(sum(coords(i)) % 2), -coords(i)[2], i))
        high = [i for i in range(chips) if coords(i)[2] >= planes // 2]
        high.sort(key=lambda i: (-(sum(coords(i)) % 2), coords(i)[2], i))
        order = [c for pair in zip(low, high) for c in pair]
        self.heavy = order[:swiglu_count]
        rest = order[swiglu_count:]
        near = lambda c: sum(hops(c, o) == 1 for o in self.heavy)
        half = lambda c: coords(c)[2] < planes // 2
        spare = len(rest) - square_count
        self.idle = []
        for want in (True, False):
            pool = sorted((c for c in rest if half(c) == want), key=lambda c: -near(c))
            self.idle += pool[: spare // 2 if want else spare - spare // 2]
        self.light = [c for c in rest if c not in self.idle]
        helpers = rest
        narrow = D // cores
        wide = FF // cores
        self.granules = (wide - narrow) // GRANULE
        self.passes = self.granules - 2
        count = len(helpers)
        cost = lambda k, h: hops(h, self.heavy[k]) ** 2
        places = [(p, k) for p in range(self.passes) for k in range(swiglu_count)]

        def search(room):
            take = [
                [helpers[(k + p * swiglu_count) % count] for k in range(swiglu_count)]
                for p in range(self.passes)
            ]
            better = True
            while better:
                better = False
                for p, k in places:
                    for h in helpers:
                        used = sum(row.count(h) for row in take)
                        if used < room(h) and h not in take[p] and cost(k, h) < cost(k, take[p][k]):
                            take[p][k] = h
                            better = True
                    for q, m in places:
                        a, b = take[p][k], take[q][m]
                        if a == b or (q != p and (b in take[p] or a in take[q])):
                            continue
                        if cost(k, b) + cost(m, a) < cost(k, a) + cost(m, b):
                            take[p][k], take[q][m] = b, a
                            better = True
            return take

        self.take = take = search(lambda h: 2)
        self.back = search(lambda h: 3 if h in self.idle else 2)
        self.column = {}
        self.choice = np.zeros((chips, 3), np.int32)
        for j, o in enumerate(self.heavy):
            self.column[(j, 0)], self.column[(j, 1)] = (o, narrow), (o, narrow + GRANULE)
        taken = {}
        for p, k in places:
            h = self.back[p][k]
            where = taken[h] = taken.get(h, -1) + 1
            self.choice[h, where] = 1 + p
            self.column[(k, 2 + p)] = (h, narrow + where * GRANULE if where < 2 else 0)
        self.held = {o: [(j, 0), (j, 1)] for j, o in enumerate(self.heavy)}
        self.place = {}
        for p in range(self.passes):
            for k in range(swiglu_count):
                h = take[p][k]
                self.held.setdefault(h, []).append((k, 2 + p))
        for chip, list_of in self.held.items():
            for where, item in enumerate(list_of):
                self.place[item] = (chip, where)
        self.is_heavy = np.array([c in self.heavy for c in range(chips)])
        self.slot_in_pass = np.zeros((max(1, self.passes), chips), np.bool_)
        for p in range(self.passes):
            for k in range(swiglu_count):
                self.slot_in_pass[p, take[p][k]] = self.place[(k, 2 + p)][1] == 1


def momentum_rows(grad, state, following, sent):
    def row(r, carry):
        after = MOMENTUM * state[r] + grad[r]
        following[r] = after
        sent[r] = grad[r] + MOMENTUM * after
        return carry

    lax.fori_loop(0, grad.shape[0], row, 0)


def wide_kernel(plan, cores, grad, state, following, first, second, sent):
    narrow_tiles = D // cores // LANE
    wide_tiles = FF // cores // LANE
    momentum_rows(grad, state, following, sent)
    for j, owner in enumerate(plan.heavy):
        for core in range(cores):
            for t in range(wide_tiles):
                value = sent[:, core * wide_tiles + t, j, :].astype(jnp.bfloat16)
                if t < narrow_tiles:
                    first[owner * cores + core, :, t * LANE : (t + 1) * LANE] = value
                else:
                    b, part = divmod(t - narrow_tiles, GRANULE // LANE)
                    chip, where = plan.place[(j, b)]
                    at = where * GRANULE + part * LANE
                    second[chip * cores + core, :, at : at + LANE] = value
    for chip in range(len(plan.is_heavy)):
        for core in range(cores):
            if chip in plan.idle:
                first[chip * cores + core] = jnp.zeros(first.shape[1:], first.dtype)
            for where in range(len(plan.held.get(chip, [])), 2):
                second[chip * cores + core, :, where * GRANULE : (where + 1) * GRANULE] = jnp.zeros(
                    (first.shape[1], GRANULE), first.dtype
                )


def narrow_kernel(plan, cores, grad, state, given, following, first, sent, stage, sems):
    narrow_tiles = D // cores // LANE
    momentum_rows(grad, state, following, sent)
    copies = []
    for j, owner in enumerate(plan.light):
        for core in range(cores):
            for t in range(narrow_tiles):
                value = sent[:, core * narrow_tiles + t, j, :].astype(jnp.bfloat16)
                stage[j * cores + core, :, t * LANE : (t + 1) * LANE] = value
        copies.append(
            pltpu.make_async_copy(
                stage.at[pl.ds(j * cores, cores)], first.at[pl.ds(owner * cores, cores)], sems.at[j]
            )
        )
        copies[-1].start()
    for copy in copies:
        copy.wait()


def tiles_of(x, rows, width):
    return x.reshape(x.shape[0], rows, width // LANE, LANE).transpose(1, 2, 0, 3)


def flat_of(x):
    return x.transpose(2, 0, 1, 3).reshape(x.shape[2], -1)


def prepare_wide(plan, chips, cores, grad, state):
    rows = D // (chips * cores)
    chunk = 16 if rows % 16 == 0 else rows
    count = grad.shape[0]
    narrow = D // cores
    devices = chips * cores
    block = (chunk, FF // LANE, count, LANE)
    spec = pl.BlockSpec(block, lambda i: (i, 0, 0, 0))
    following, first, second = pl.pallas_call(
        lambda *refs: wide_kernel(plan, cores, *refs),
        grid=(rows // chunk,),
        in_specs=[spec, spec],
        out_specs=[
            spec,
            pl.BlockSpec((devices, chunk, narrow), lambda i: (0, i, 0)),
            pl.BlockSpec((devices, chunk, 2 * GRANULE), lambda i: (0, i, 0)),
        ],
        out_shape=[
            jax.ShapeDtypeStruct((rows,) + block[1:], jnp.float32),
            jax.ShapeDtypeStruct((devices, rows, narrow), jnp.bfloat16),
            jax.ShapeDtypeStruct((devices, rows, 2 * GRANULE), jnp.bfloat16),
        ],
        scratch_shapes=[pltpu.VMEM(block, jnp.float32)],
        compiler_params=pltpu.CompilerParams(vmem_limit_bytes=48 * 1024 * 1024),
        name="prepare_wide",
    )(tiles_of(grad, rows, FF), tiles_of(state, rows, FF))
    return flat_of(following), first, second


def prepare_narrow(plan, chips, cores, grad, state, first):
    rows = D // (chips * cores)
    count = grad.shape[0]
    block = (rows, D // LANE, count, LANE)
    vmem = pl.BlockSpec(memory_space=pltpu.VMEM)
    anywhere = pl.BlockSpec(memory_space=pl.ANY)
    following, first = pl.pallas_call(
        lambda *refs: narrow_kernel(plan, cores, *refs),
        in_specs=[vmem, vmem, anywhere],
        out_specs=[vmem, anywhere],
        out_shape=[
            jax.ShapeDtypeStruct(block, jnp.float32),
            jax.ShapeDtypeStruct(first.shape, first.dtype),
        ],
        input_output_aliases={2: 1},
        scratch_shapes=[
            pltpu.VMEM(block, jnp.float32),
            pltpu.VMEM((count * cores, rows, D // cores), jnp.bfloat16),
            pltpu.SemaphoreType.DMA((count,)),
        ],
        compiler_params=pltpu.CompilerParams(vmem_limit_bytes=32 * 1024 * 1024),
        cost_estimate=pl.CostEstimate(
            flops=0, bytes_accessed=3 * grad.size * 4 + grad.size * 2, transcendentals=0
        ),
        name="prepare_narrow",
    )(tiles_of(grad, rows, D), tiles_of(state, rows, D), first)
    return flat_of(following), first


def other_core(x):
    return lax.ppermute(x, "tensor", [(0, 1), (1, 0)])


BLOCK = 256
EDGE = D // BLOCK
NEAR = EDGE // 2
PACKED = EDGE * NEAR + NEAR
GROUPS = EDGE + 1
MIB = 1024 * 1024


def each_pair(body, after=None):
    def row(i, carry):
        for d in range(NEAR):
            j = lax.rem(i + d, EDGE)
            body(i * NEAR + d, i, j, d == 0)
        if after is not None:
            after(i)
        return carry

    lax.fori_loop(0, EDGE, row, 0)
    for i in range(NEAR):
        body(EDGE * NEAR + i, i, i + NEAR, False)
    if after is not None:
        after(EDGE)


def span(i):
    if isinstance(i, int):
        return pl.ds(i * BLOCK, BLOCK)
    return pl.ds(pl.multiple_of(i * BLOCK, BLOCK), BLOCK)


def group(ref, g):
    return ref.at[pl.ds(g * NEAR, NEAR)]


def rows_of(ref, i):
    return ref.at[span(i), :]


def columns_of(ref, at, width):
    return ref.at[:, pl.ds(at, width)]


def gram_blocks(x, width, out, after):
    def body(slot, i, j, diagonal):
        out[slot] = lax.dot_general(
            x[span(i), :width],
            x[span(j), :width],
            (((1,), (1,)), ((), ())),
            preferred_element_type=jnp.float32,
        )

    each_pair(body, after)


def mirror(out, i, j, diagonal, value):
    rounded = value.astype(out.dtype)
    out[span(i), span(j)] = rounded
    if not diagonal:
        out[span(j), span(i)] = rounded.T


def polynomial_blocks(normed, out):
    def body(slot, i, j, diagonal):
        squared = jnp.dot(normed[span(i), :], normed[:, span(j)], preferred_element_type=jnp.float32)
        value = QUINTIC_CUBIC * normed[span(i), span(j)].astype(jnp.float32) + QUINTIC_FIFTH * squared
        mirror(out, i, j, diagonal, value)

    each_pair(body)


def mixed_rows(polynomial, x, width, scale, out, before=None, after=None):
    def row(i, carry):
        if before is not None:
            before(i)
        for c in range(0, width, BLOCK):
            product = jnp.dot(
                polynomial[span(i), :], x[:, c : c + BLOCK], preferred_element_type=jnp.float32
            )
            mixed = QUINTIC_LINEAR * x[span(i), c : c + BLOCK].astype(jnp.float32) + product
            out[span(i), c : c + BLOCK] = (mixed * scale).astype(out.dtype)
        if after is not None:
            after(i)
        return carry

    lax.fori_loop(0, EDGE, row, 0)


def column_copies(sources, x, sems):
    copies, at = [], 0
    for k, source in enumerate(sources):
        width = source.shape[1]
        copies.append(pltpu.make_async_copy(source, columns_of(x, at, width), sems.at[k]))
        at += width
    return copies


def start_all(copies):
    for copy in copies:
        copy.start()


def wait_all(copies):
    for copy in copies:
        copy.wait()


def by_kind(flag, narrow, wide, body):
    @pl.when(flag[0] > 0)
    def _():
        body(wide)

    @pl.when(flag[0] <= 0)
    def _():
        body(narrow)


def gram_kernel(flag, *refs):
    parts, (out, x, blocks, in_sems, out_sems) = refs[:-5], refs[-5:]
    copies = column_copies(parts, x, in_sems)

    def send(g):
        pltpu.make_async_copy(group(blocks, g), group(out, g), out_sems.at[g]).start()

    def run(width):
        used = copies[: 1 if width < x.shape[1] else len(copies)]
        start_all(used)
        wait_all(used)
        gram_blocks(x, width, blocks, send)

    by_kind(flag, parts[0].shape[1], x.shape[1], run)
    wait_all(
        [
            pltpu.make_async_copy(group(blocks, g), group(out, g), out_sems.at[g])
            for g in range(GROUPS)
        ]
    )


def group_copies(source, target, sems):
    return [
        pltpu.make_async_copy(group(source, g), group(target, g), sems.at[g]) for g in range(GROUPS)
    ]


def middle_kernel(flag, own_in, other_in, *refs):
    parts, refs = refs[:-15], refs[-15:]
    first_out, second_out, packed_out, scale_out = refs[:4]
    own, other, x, mixed, normed, polynomial = refs[4:10]
    own_sems, other_sems, x_sems, mixed_sems, packed_sems = refs[10:]
    narrow, wide = first_out.shape[1], x.shape[1]
    own_copies = group_copies(own_in, own, own_sems)
    other_copies = group_copies(other_in, other, other_sems)
    x_copies = column_copies(parts, x, x_sems)
    for a, b in zip(own_copies, other_copies):
        a.start()
        b.start()
    by_kind(flag, 1, len(x_copies), lambda used: start_all(x_copies[:used]))

    once = jnp.zeros((8, BLOCK), jnp.float32)
    twice = jnp.zeros((8, BLOCK), jnp.float32)
    for g in range(GROUPS):
        own_copies[g].wait()
        other_copies[g].wait()
        for d in range(NEAR):
            slot = g * NEAR + d
            gram = own[slot] + other[slot]
            own[slot] = gram
            squares = jnp.sum((gram * gram).reshape(BLOCK // 8, 8, BLOCK), axis=0)
            if d == 0 and g < EDGE:
                once += squares
            else:
                twice += squares
    total = jnp.full((8, LANE), jnp.sum(once + 2.0 * twice), jnp.float32)
    scale = jnp.sqrt(total) + 1e-06
    scale_out[...] = scale
    inverse = (1.0 / scale)[0:1, 0:1]
    root = (1.0 / jnp.sqrt(scale))[0:1, 0:1]
    each_pair(lambda slot, i, j, diagonal: mirror(normed, i, j, diagonal, own[slot] * inverse))
    polynomial_blocks(normed, polynomial)

    def send(g):
        pltpu.make_async_copy(group(other, g), group(packed_out, g), packed_sems.at[g]).start()

    def run(width):
        used = x_copies[: 1 if width < wide else len(x_copies)]
        wait_all(used)
        mixed_rows(polynomial, x, width, root, mixed)
        sends = [pltpu.make_async_copy(columns_of(mixed, 0, narrow), first_out, mixed_sems.at[0])]
        if width == wide:
            rest = columns_of(mixed, narrow, wide - narrow)
            sends.append(pltpu.make_async_copy(rest, second_out, mixed_sems.at[1]))
        start_all(sends)
        gram_blocks(mixed, width, other, send)
        wait_all(sends)

    by_kind(flag, narrow, wide, run)
    wait_all(group_copies(other, packed_out, packed_sems))


def last_kernel(flag, factor, own_in, other_in, x_in, *refs):
    count = len(refs) - 11
    polynomial_out, outs = refs[0], refs[1:count]
    own, other, x, mixed, normed, polynomial = refs[count : count + 6]
    own_sems, other_sems, x_sem, polynomial_sem, out_sems = refs[count + 6 :]
    own_copies = group_copies(own_in, own, own_sems)
    other_copies = group_copies(other_in, other, other_sems)
    for a, b in zip(own_copies, other_copies):
        a.start()
        b.start()
    x_copy = pltpu.make_async_copy(x_in, x, x_sem)
    heavy = flag[0] > 0

    @pl.when(heavy)
    def _():
        x_copy.start()

    for g in range(GROUPS):
        own_copies[g].wait()
        other_copies[g].wait()
        for d in range(NEAR):
            slot = g * NEAR + d
            i, j = (g, (g + d) % EDGE) if g < EDGE else (d, d + NEAR)
            mirror(normed, i, j, i == j, own[slot] + other[slot])
    polynomial_blocks(normed, polynomial)
    polynomial_copy = pltpu.make_async_copy(polynomial, polynomial_out, polynomial_sem)
    polynomial_copy.start()

    def out_copies(i):
        copies, at = [], 0
        for k, out in enumerate(outs):
            width = out.shape[1]
            source = mixed.at[span(i), pl.ds(at, width)]
            copies.append(pltpu.make_async_copy(source, rows_of(out, i), out_sems.at[k, i]))
            at += width
        return copies

    @pl.when(heavy)
    def _():
        x_copy.wait()
        mixed_rows(
            polynomial,
            x,
            x.shape[1],
            factor[0],
            mixed,
            after=lambda i: start_all(out_copies(i)),
        )
        for i in range(EDGE):
            wait_all(out_copies(i))

    polynomial_copy.wait()


def finish_kernel(factor, polynomial_in, x_in, out, x, mixed, polynomial, x_sem, in_sems, out_sems):
    x_copy = pltpu.make_async_copy(x_in, x, x_sem)
    x_copy.start()

    def in_copy(i):
        return pltpu.make_async_copy(rows_of(polynomial_in, i), rows_of(polynomial, i), in_sems.at[i])

    def out_copy(i):
        target = out.at[span(i), pl.ds(0, x.shape[1])]
        return pltpu.make_async_copy(rows_of(mixed, i), target, out_sems.at[i])

    start_all([in_copy(i) for i in range(EDGE)])
    x_copy.wait()
    mixed_rows(
        polynomial,
        x,
        x.shape[1],
        factor[0],
        mixed,
        before=lambda i: in_copy(i).wait(),
        after=lambda i: out_copy(i).start(),
    )
    wait_all([out_copy(i) for i in range(EDGE)])


def join_kernel(pick, own, *refs):
    handed, (given, out, stage, in_sems, out_sems) = refs[:-5], refs[-5:]
    narrow = out.shape[1] - 2 * GRANULE

    def incoming(where, source):
        target = columns_of(stage, where * GRANULE, GRANULE)
        return pltpu.make_async_copy(source, target, in_sems.at[where])

    def outgoing(where):
        at = narrow + where * GRANULE if where < 2 else 0
        source = columns_of(stage, where * GRANULE, GRANULE)
        return pltpu.make_async_copy(source, columns_of(out, at, GRANULE), out_sems.at[where])

    for where in range(3):
        for k in range(1 + len(handed)):
            if where == 2 and k == 0:
                continue
            source = columns_of(own, where * GRANULE, GRANULE) if k == 0 else handed[k - 1]

            @pl.when(pick[where] == k)
            def _():
                incoming(where, source).start()

    for where in range(2):
        incoming(where, columns_of(own, 0, GRANULE)).wait()
        outgoing(where).start()

    @pl.when(pick[2] > 0)
    def _():
        incoming(2, columns_of(own, 0, GRANULE)).wait()
        outgoing(2).start()
        outgoing(2).wait()

    for where in range(2):
        outgoing(where).wait()


def call(kernel, name, scalars, arrays, outs, scratch, limit, flops, small_outs=0, aliases=None):
    moved = sum(x.size * x.dtype.itemsize for x in arrays)
    moved += sum(math.prod(o.shape) * o.dtype.itemsize for o in outs)
    smem = pl.BlockSpec(memory_space=pltpu.SMEM)
    anywhere = pl.BlockSpec(memory_space=pl.ANY)
    vmem = pl.BlockSpec(memory_space=pltpu.VMEM)
    return pl.pallas_call(
        kernel,
        in_specs=[smem] * len(scalars) + [anywhere] * len(arrays),
        out_specs=[anywhere] * (len(outs) - small_outs) + [vmem] * small_outs,
        out_shape=list(outs),
        scratch_shapes=list(scratch),
        input_output_aliases=aliases or {},
        compiler_params=pltpu.CompilerParams(vmem_limit_bytes=limit * MIB),
        cost_estimate=pl.CostEstimate(flops=flops, bytes_accessed=moved, transcendentals=0),
        name=name,
    )(*scalars, *arrays)


def assemble(plan, square_order, swiglu_order, back):
    squares, wides = square_order.shape[0], swiglu_order.shape[0]
    rows, both = back.shape[1:]
    narrow = both - 2 * GRANULE
    wide = narrow + plan.granules * GRANULE
    parts = 1 + plan.passes

    def kernel(
        square_to, wide_to, source, square_out, wide_out, square_stage, wide_stage, *sems
    ):
        square_in, wide_in, square_sems, wide_sems = sems
        square_copies = [
            [
                pltpu.make_async_copy(
                    source.at[plan.light[j], :, pl.ds(0, narrow)], square_stage.at[j], square_in.at[j]
                )
            ]
            for j in range(squares)
        ]
        wide_copies = []
        for j in range(wides):
            moves = [(plan.heavy[j], 0, 0, both)]
            for b in range(2, plan.granules):
                chip, at = plan.column[(j, b)]
                moves.append((chip, at, narrow + b * GRANULE, GRANULE))
            wide_copies.append(
                [
                    pltpu.make_async_copy(
                        source.at[chip, :, pl.ds(at, width)],
                        wide_stage.at[j, :, pl.ds(to, width)],
                        wide_in.at[j * parts + n],
                    )
                    for n, (chip, at, to, width) in enumerate(moves)
                ]
            )
        for slot in square_copies + wide_copies:
            start_all(slot)
        outs = []
        for copies, stage, out, order, out_sems in (
            (square_copies, square_stage, square_out, square_to, square_sems),
            (wide_copies, wide_stage, wide_out, wide_to, wide_sems),
        ):
            for j, slot in enumerate(copies):
                wait_all(slot)
                outs.append(pltpu.make_async_copy(stage.at[j], out.at[order[j]], out_sems.at[j]))
                outs[-1].start()
        wait_all(outs)

    smem = pl.BlockSpec(memory_space=pltpu.SMEM)
    anywhere = pl.BlockSpec(memory_space=pl.ANY)
    shapes = [(squares, rows, narrow), (wides, rows, wide)]
    dma = pltpu.SemaphoreType.DMA
    return pl.pallas_call(
        kernel,
        in_specs=[smem, smem, anywhere],
        out_specs=[anywhere, anywhere],
        out_shape=[jax.ShapeDtypeStruct(shape, jnp.bfloat16) for shape in shapes],
        scratch_shapes=[pltpu.VMEM(shape, jnp.bfloat16) for shape in shapes]
        + [dma((squares,)), dma((wides * parts,)), dma((squares,)), dma((wides,))],
        compiler_params=pltpu.CompilerParams(vmem_limit_bytes=12 * MIB),
        name="assemble",
    )(square_order, swiglu_order, back)


def spread(value, chips, chip):
    known = jnp.where(jnp.arange(chips, dtype=jnp.int32) == chip, value, 0.0)
    step = 1
    while step < chips:
        known = known + lax.ppermute(known, "dp", [(s, s ^ step) for s in range(chips)])
        step *= 2
    return known


def lookup(table, positions):
    matches = positions[:, None] == jnp.arange(table.shape[0], dtype=jnp.int32)[None, :]
    return jnp.sum(jnp.where(matches, table[None, :], 0), axis=1)


def local(
    square_grad,
    square_state,
    swiglu_grad,
    swiglu_state,
    square_order,
    swiglu_order,
    owners,
    vector_values,
    vector_grad,
    vector_first,
    vector_second,
    embed_values,
    embed_grad,
    embed_first,
    embed_second,
    embed_ranges,
):
    chips = lax.axis_size("dp")
    cores = lax.axis_size("tensor")
    chip = lax.axis_index("dp")
    square_count = square_grad.shape[0]
    swiglu_count = swiglu_grad.shape[0]
    chip_rows = D // chips
    narrow = D // cores
    plan = Plan(chips, cores, square_count, swiglu_count)

    swiglu_next, first_send, second_send = prepare_wide(
        plan, chips, cores, swiglu_grad, swiglu_state
    )
    square_next, first_send = prepare_narrow(
        plan, chips, cores, square_grad, square_state, first_send
    )
    both = ("dp", "tensor")
    second_got = lax.all_to_all(
        second_send.reshape(D, 2 * GRANULE), both, split_axis=0, concat_axis=0, tiled=True
    )
    first_got = lax.all_to_all(
        first_send.reshape(D, narrow), both, split_axis=0, concat_axis=0, tiled=True
    )
    heavy_here = jnp.asarray(plan.is_heavy)[chip]
    pieces = [second_got[:, :GRANULE], second_got[:, GRANULE:]]
    relayed = []
    for p in range(plan.passes):
        pick = jnp.asarray(plan.slot_in_pass[p])[chip]
        pairs = [(plan.take[p][k], plan.heavy[k]) for k in range(swiglu_count)]
        relayed.append(lax.ppermute(jnp.where(pick, pieces[1], pieces[0]), "dp", pairs))
    flag = heavy_here.astype(jnp.int32).reshape(1)
    factor = jnp.where(heavy_here, jnp.float32(math.sqrt(FF)), jnp.float32(math.sqrt(D))).reshape(1)
    packed = jax.ShapeDtypeStruct((PACKED, BLOCK, BLOCK), jnp.float32)
    whole_square = jax.ShapeDtypeStruct((D, D), jnp.bfloat16)
    first_shape = jax.ShapeDtypeStruct((D, narrow), jnp.bfloat16)
    extra = plan.granules * GRANULE
    second_shape = jax.ShapeDtypeStruct((D, extra), jnp.bfloat16)
    square_buffer = pltpu.VMEM((D, D), jnp.bfloat16)
    packed_buffer = pltpu.VMEM(packed.shape, jnp.float32)
    matrix_buffer = pltpu.VMEM((D, narrow + extra), jnp.bfloat16)
    first_buffer = pltpu.VMEM((D, narrow), jnp.bfloat16)
    second_buffer = pltpu.VMEM((D, extra), jnp.bfloat16)
    sems = lambda *shape: pltpu.SemaphoreType.DMA(shape)
    half = D * D * (narrow + extra)
    parts = [first_got, second_got, *relayed]
    (own,) = call(
        gram_kernel,
        "gram",
        [flag],
        parts,
        [packed],
        [matrix_buffer, packed_buffer, sems(len(parts)), sems(GROUPS)],
        15,
        half,
    )
    first_mid, second_mid, own_mid, scale = call(
        middle_kernel,
        "middle",
        [flag],
        [own, other_core(own), *parts],
        [first_shape, second_shape, packed, jax.ShapeDtypeStruct((8, LANE), jnp.float32)],
        [packed_buffer] * 2
        + [matrix_buffer] * 2
        + [square_buffer] * 2
        + [sems(GROUPS), sems(GROUPS), sems(len(parts)), sems(2), sems(GROUPS)],
        37,
        3 * half + D * D * D,
        small_outs=1,
    )
    piece_shape = jax.ShapeDtypeStruct((D, GRANULE), jnp.bfloat16)
    pair_shape = jax.ShapeDtypeStruct((D, 2 * GRANULE), jnp.bfloat16)
    polynomial, kept, *rest = call(
        last_kernel,
        "last",
        [flag, factor],
        [own_mid, other_core(own_mid), second_mid],
        [whole_square, pair_shape] + [piece_shape] * plan.passes,
        [packed_buffer] * 2
        + [second_buffer] * 2
        + [square_buffer] * 2
        + [sems(GROUPS), sems(GROUPS), sems(), sems(), sems(1 + plan.passes, EDGE)],
        56,
        D * D * D + 2 * D * D * extra,
    )
    handed = []
    for p in range(plan.passes):
        pairs = [(plan.heavy[k], plan.back[p][k]) for k in range(swiglu_count)]
        handed.append(lax.ppermute(rest[p], "dp", pairs))
    back_shape = jax.ShapeDtypeStruct((D, narrow + 2 * GRANULE), jnp.bfloat16)
    (back_out,) = call(
        finish_kernel,
        "finish",
        [factor],
        [polynomial, first_mid],
        [back_shape],
        [first_buffer] * 2 + [square_buffer, sems(), sems(EDGE), sems(EDGE)],
        56,
        2 * D * D * narrow,
    )
    scale, _ = lax.optimization_barrier((scale, kept))
    logs = spread(0.5 * jnp.log(scale[0, 0]), chips, chip)
    (back_out,) = call(
        join_kernel,
        "join",
        [jnp.asarray(plan.choice)[chip]],
        [kept, *handed, back_out],
        [back_shape],
        [pltpu.VMEM((D, 3 * GRANULE), jnp.bfloat16), sems(3), sems(3)],
        56,
        0,
        aliases={2 + plan.passes: 0},
    )
    back_out, logs = lax.optimization_barrier((back_out, logs))
    back = lax.all_to_all(
        back_out.reshape(chips, chip_rows, -1), "dp", split_axis=0, concat_axis=0, tiled=True
    )
    square_update, swiglu_update = assemble(plan, square_order, swiglu_order, back)

    slot_chips = np.array(plan.light + plan.heavy, np.int32)
    slot_owner = jnp.concatenate(
        [lookup(owners[:square_count], square_order), lookup(owners[square_count:], swiglu_order)]
    )
    slot_logs = logs[slot_chips]
    owner_norms = jnp.sum(jnp.where(slot_owner == chip, slot_logs, 0.0)).reshape(1)

    vector_step, first_vector, second_vector = adamw_terms(
        vector_values, vector_grad, vector_first, vector_second
    )
    embed_rows = embed_values.shape[0]
    row_numbers = chip * embed_rows + jnp.arange(embed_rows, dtype=jnp.int32)
    inside = (row_numbers[:, None] >= embed_ranges[None, :, 0]) & (
        row_numbers[:, None] < embed_ranges[None, :, 1]
    )
    row_live = jnp.sum(inside.astype(jnp.int32), axis=1) > 0
    direction, first_next, second_next = adamw_terms(
        embed_values, embed_grad, embed_first, embed_second
    )
    embed_step = jnp.where(row_live[:, None], direction, 0.0)
    first_embed = jnp.where(row_live[:, None], first_next, embed_first)
    second_embed = jnp.where(row_live[:, None], second_next, embed_second)
    return (
        square_next,
        swiglu_next,
        square_update,
        swiglu_update,
        owner_norms,
        vector_step,
        first_vector,
        second_vector,
        embed_step,
        first_embed,
        second_embed,
    )


def solution(mesh):
    flat = P(None, ("dp", "tensor"))
    vector = P(("dp", "tensor"))
    tile = P("dp", "tensor")
    update = P(None, "dp", "tensor")
    return jax.shard_map(
        local,
        mesh=mesh,
        in_specs=(flat,) * 4 + (P(),) * 3 + (vector,) * 4 + (tile,) * 4 + (P(),),
        out_specs=(flat, flat, update, update, P("dp")) + (vector,) * 3 + (tile,) * 3,
        check_vma=False,
    )
```

```python
import math

import jax
import jax.numpy as jnp
import numpy as np
from jax import lax
from jax.experimental import pallas as pl
from jax.experimental.pallas import tpu as pltpu
from jax.sharding import PartitionSpec as P

D = 1536
FF = 4096
NS_STEPS = 2


QUINTIC_LINEAR = 3.4445
QUINTIC_CUBIC = -4.775
QUINTIC_FIFTH = 2.0315
MOMENTUM = 0.95
BIAS_FIRST = 1.0 - 0.9**10
BIAS_SECOND = 1.0 - 0.95**10


def momentum_terms(gradient, state):
    state_next = MOMENTUM * state + gradient
    return (state_next, (gradient + MOMENTUM * state_next).astype(jnp.bfloat16))


def adamw_terms(values, gradient, first, second):
    first_next = 0.9 * first + 0.1 * gradient
    second_next = 0.95 * second + 0.05 * gradient * gradient
    direction = (
        first_next / BIAS_FIRST / (jnp.sqrt(second_next / BIAS_SECOND) + 1e-08) + 0.1 * values
    )
    return (direction, first_next, second_next)


LANE = 128
GRANULE = 256


class Plan:
    def __init__(self, chips, cores, square_count, swiglu_count):
        planes = 4
        per = chips // planes
        side = max(1, int(round(math.sqrt(per))))

        def coords(i):
            return (i % side, (i // side) % max(1, per // side), i // per)

        def hops(a, b):
            return sum(abs(p - q) for p, q in zip(coords(a), coords(b)))

        low = [i for i in range(chips) if coords(i)[2] < planes // 2]
        low.sort(key=lambda i: (-(sum(coords(i)) % 2), -coords(i)[2], i))
        high = [i for i in range(chips) if coords(i)[2] >= planes // 2]
        high.sort(key=lambda i: (-(sum(coords(i)) % 2), coords(i)[2], i))
        order = [c for pair in zip(low, high) for c in pair]
        self.heavy = order[:swiglu_count]
        rest = order[swiglu_count:]
        near = lambda c: sum(hops(c, o) == 1 for o in self.heavy)
        half = lambda c: coords(c)[2] < planes // 2
        spare = len(rest) - square_count
        self.idle = []
        for want in (True, False):
            pool = sorted((c for c in rest if half(c) == want), key=lambda c: -near(c))
            self.idle += pool[: spare // 2 if want else spare - spare // 2]
        self.light = [c for c in rest if c not in self.idle]
        helpers = rest
        narrow = D // cores
        wide = FF // cores
        self.granules = (wide - narrow) // GRANULE
        self.passes = self.granules - 2
        count = len(helpers)
        cost = lambda k, h: hops(h, self.heavy[k]) ** 2
        places = [(p, k) for p in range(self.passes) for k in range(swiglu_count)]

        def search(room):
            take = [
                [helpers[(k + p * swiglu_count) % count] for k in range(swiglu_count)]
                for p in range(self.passes)
            ]
            better = True
            while better:
                better = False
                for p, k in places:
                    for h in helpers:
                        used = sum(row.count(h) for row in take)
                        if used < room(h) and h not in take[p] and cost(k, h) < cost(k, take[p][k]):
                            take[p][k] = h
                            better = True
                    for q, m in places:
                        a, b = take[p][k], take[q][m]
                        if a == b or (q != p and (b in take[p] or a in take[q])):
                            continue
                        if cost(k, b) + cost(m, a) < cost(k, a) + cost(m, b):
                            take[p][k], take[q][m] = b, a
                            better = True
            return take

        self.take = take = search(lambda h: 2)
        self.back = search(lambda h: 3 if h in self.idle else 2)
        self.column = {}
        self.choice = np.zeros((chips, 3), np.int32)
        for j, o in enumerate(self.heavy):
            self.column[(j, 0)], self.column[(j, 1)] = (o, narrow), (o, narrow + GRANULE)
        taken = {}
        for p, k in places:
            h = self.back[p][k]
            where = taken[h] = taken.get(h, -1) + 1
            self.choice[h, where] = 1 + p
            self.column[(k, 2 + p)] = (h, narrow + where * GRANULE if where < 2 else 0)
        self.held = {o: [(j, 0), (j, 1)] for j, o in enumerate(self.heavy)}
        self.place = {}
        for p in range(self.passes):
            for k in range(swiglu_count):
                h = take[p][k]
                self.held.setdefault(h, []).append((k, 2 + p))
        for chip, list_of in self.held.items():
            for where, item in enumerate(list_of):
                self.place[item] = (chip, where)
        self.is_heavy = np.array([c in self.heavy for c in range(chips)])
        self.slot_in_pass = np.zeros((max(1, self.passes), chips), np.bool_)
        for p in range(self.passes):
            for k in range(swiglu_count):
                self.slot_in_pass[p, take[p][k]] = self.place[(k, 2 + p)][1] == 1


def momentum_rows(grad, state, following, sent):
    def row(r, carry):
        after = MOMENTUM * state[r] + grad[r]
        following[r] = after
        sent[r] = grad[r] + MOMENTUM * after
        return carry

    lax.fori_loop(0, grad.shape[0], row, 0)


def wide_kernel(plan, cores, grad, state, following, first, second, sent):
    narrow_tiles = D // cores // LANE
    wide_tiles = FF // cores // LANE
    momentum_rows(grad, state, following, sent)
    for j, owner in enumerate(plan.heavy):
        for core in range(cores):
            for t in range(wide_tiles):
                value = sent[:, core * wide_tiles + t, j, :].astype(jnp.bfloat16)
                if t < narrow_tiles:
                    first[owner * cores + core, :, t * LANE : (t + 1) * LANE] = value
                else:
                    b, part = divmod(t - narrow_tiles, GRANULE // LANE)
                    chip, where = plan.place[(j, b)]
                    at = where * GRANULE + part * LANE
                    second[chip * cores + core, :, at : at + LANE] = value
    for chip in range(len(plan.is_heavy)):
        for core in range(cores):
            if chip in plan.idle:
                first[chip * cores + core] = jnp.zeros(first.shape[1:], first.dtype)
            for where in range(len(plan.held.get(chip, [])), 2):
                second[chip * cores + core, :, where * GRANULE : (where + 1) * GRANULE] = jnp.zeros(
                    (first.shape[1], GRANULE), first.dtype
                )


def narrow_kernel(plan, cores, grad, state, given, following, first, sent, stage, sems):
    narrow_tiles = D // cores // LANE
    momentum_rows(grad, state, following, sent)
    copies = []
    for j, owner in enumerate(plan.light):
        for core in range(cores):
            for t in range(narrow_tiles):
                value = sent[:, core * narrow_tiles + t, j, :].astype(jnp.bfloat16)
                stage[j * cores + core, :, t * LANE : (t + 1) * LANE] = value
        copies.append(
            pltpu.make_async_copy(
                stage.at[pl.ds(j * cores, cores)], first.at[pl.ds(owner * cores, cores)], sems.at[j]
            )
        )
        copies[-1].start()
    for copy in copies:
        copy.wait()


def tiles_of(x, rows, width):
    return x.reshape(x.shape[0], rows, width // LANE, LANE).transpose(1, 2, 0, 3)


def flat_of(x):
    return x.transpose(2, 0, 1, 3).reshape(x.shape[2], -1)


def prepare_wide(plan, chips, cores, grad, state):
    rows = D // (chips * cores)
    chunk = 16 if rows % 16 == 0 else rows
    count = grad.shape[0]
    narrow = D // cores
    devices = chips * cores
    block = (chunk, FF // LANE, count, LANE)
    spec = pl.BlockSpec(block, lambda i: (i, 0, 0, 0))
    following, first, second = pl.pallas_call(
        lambda *refs: wide_kernel(plan, cores, *refs),
        grid=(rows // chunk,),
        in_specs=[spec, spec],
        out_specs=[
            spec,
            pl.BlockSpec((devices, chunk, narrow), lambda i: (0, i, 0)),
            pl.BlockSpec((devices, chunk, 2 * GRANULE), lambda i: (0, i, 0)),
        ],
        out_shape=[
            jax.ShapeDtypeStruct((rows,) + block[1:], jnp.float32),
            jax.ShapeDtypeStruct((devices, rows, narrow), jnp.bfloat16),
            jax.ShapeDtypeStruct((devices, rows, 2 * GRANULE), jnp.bfloat16),
        ],
        scratch_shapes=[pltpu.VMEM(block, jnp.float32)],
        compiler_params=pltpu.CompilerParams(vmem_limit_bytes=48 * 1024 * 1024),
        name="prepare_wide",
    )(tiles_of(grad, rows, FF), tiles_of(state, rows, FF))
    return flat_of(following), first, second


def prepare_narrow(plan, chips, cores, grad, state, first):
    rows = D // (chips * cores)
    count = grad.shape[0]
    block = (rows, D // LANE, count, LANE)
    vmem = pl.BlockSpec(memory_space=pltpu.VMEM)
    anywhere = pl.BlockSpec(memory_space=pl.ANY)
    following, first = pl.pallas_call(
        lambda *refs: narrow_kernel(plan, cores, *refs),
        in_specs=[vmem, vmem, anywhere],
        out_specs=[vmem, anywhere],
        out_shape=[
            jax.ShapeDtypeStruct(block, jnp.float32),
            jax.ShapeDtypeStruct(first.shape, first.dtype),
        ],
        input_output_aliases={2: 1},
        scratch_shapes=[
            pltpu.VMEM(block, jnp.float32),
            pltpu.VMEM((count * cores, rows, D // cores), jnp.bfloat16),
            pltpu.SemaphoreType.DMA((count,)),
        ],
        compiler_params=pltpu.CompilerParams(vmem_limit_bytes=32 * 1024 * 1024),
        cost_estimate=pl.CostEstimate(
            flops=0, bytes_accessed=3 * grad.size * 4 + grad.size * 2, transcendentals=0
        ),
        name="prepare_narrow",
    )(tiles_of(grad, rows, D), tiles_of(state, rows, D), first)
    return flat_of(following), first


def other_core(x):
    return lax.ppermute(x, "tensor", [(0, 1), (1, 0)])


BLOCK = 256
EDGE = D // BLOCK
NEAR = EDGE // 2
PACKED = EDGE * NEAR + NEAR
GROUPS = EDGE + 1
MIB = 1024 * 1024


def each_pair(body, after=None):
    def row(i, carry):
        for d in range(NEAR):
            j = lax.rem(i + d, EDGE)
            body(i * NEAR + d, i, j, d == 0)
        if after is not None:
            after(i)
        return carry

    lax.fori_loop(0, EDGE, row, 0)
    for i in range(NEAR):
        body(EDGE * NEAR + i, i, i + NEAR, False)
    if after is not None:
        after(EDGE)


def span(i):
    if isinstance(i, int):
        return pl.ds(i * BLOCK, BLOCK)
    return pl.ds(pl.multiple_of(i * BLOCK, BLOCK), BLOCK)


def group(ref, g):
    return ref.at[pl.ds(g * NEAR, NEAR)]


def rows_of(ref, i):
    return ref.at[span(i), :]


def columns_of(ref, at, width):
    return ref.at[:, pl.ds(at, width)]


def gram_blocks(x, width, out, after):
    def body(slot, i, j, diagonal):
        out[slot] = lax.dot_general(
            x[span(i), :width],
            x[span(j), :width],
            (((1,), (1,)), ((), ())),
            preferred_element_type=jnp.float32,
        )

    each_pair(body, after)


def mirror(out, i, j, diagonal, value):
    rounded = value.astype(out.dtype)
    out[span(i), span(j)] = rounded
    if not diagonal:
        out[span(j), span(i)] = rounded.T


def polynomial_blocks(normed, out):
    def body(slot, i, j, diagonal):
        squared = jnp.dot(normed[span(i), :], normed[:, span(j)], preferred_element_type=jnp.float32)
        value = QUINTIC_CUBIC * normed[span(i), span(j)].astype(jnp.float32) + QUINTIC_FIFTH * squared
        mirror(out, i, j, diagonal, value)

    each_pair(body)


def mixed_rows(polynomial, x, width, scale, out, before=None, after=None):
    def row(i, carry):
        if before is not None:
            before(i)
        for c in range(0, width, BLOCK):
            product = jnp.dot(
                polynomial[span(i), :], x[:, c : c + BLOCK], preferred_element_type=jnp.float32
            )
            mixed = QUINTIC_LINEAR * x[span(i), c : c + BLOCK].astype(jnp.float32) + product
            out[span(i), c : c + BLOCK] = (mixed * scale).astype(out.dtype)
        if after is not None:
            after(i)
        return carry

    lax.fori_loop(0, EDGE, row, 0)


def column_copies(sources, x, sems):
    copies, at = [], 0
    for k, source in enumerate(sources):
        width = source.shape[1]
        copies.append(pltpu.make_async_copy(source, columns_of(x, at, width), sems.at[k]))
        at += width
    return copies


def start_all(copies):
    for copy in copies:
        copy.start()


def wait_all(copies):
    for copy in copies:
        copy.wait()


def by_kind(flag, narrow, wide, body):
    @pl.when(flag[0] > 0)
    def _():
        body(wide)

    @pl.when(flag[0] <= 0)
    def _():
        body(narrow)


def gram_kernel(flag, *refs):
    parts, (out, x, blocks, in_sems, out_sems) = refs[:-5], refs[-5:]
    copies = column_copies(parts, x, in_sems)

    def send(g):
        pltpu.make_async_copy(group(blocks, g), group(out, g), out_sems.at[g]).start()

    def run(width):
        used = copies[: 1 if width < x.shape[1] else len(copies)]
        start_all(used)
        wait_all(used)
        gram_blocks(x, width, blocks, send)

    by_kind(flag, parts[0].shape[1], x.shape[1], run)
    wait_all(
        [
            pltpu.make_async_copy(group(blocks, g), group(out, g), out_sems.at[g])
            for g in range(GROUPS)
        ]
    )


def group_copies(source, target, sems):
    return [
        pltpu.make_async_copy(group(source, g), group(target, g), sems.at[g]) for g in range(GROUPS)
    ]


def middle_kernel(flag, own_in, other_in, *refs):
    parts, refs = refs[:-15], refs[-15:]
    first_out, second_out, packed_out, scale_out = refs[:4]
    own, other, x, mixed, normed, polynomial = refs[4:10]
    own_sems, other_sems, x_sems, mixed_sems, packed_sems = refs[10:]
    narrow, wide = first_out.shape[1], x.shape[1]
    own_copies = group_copies(own_in, own, own_sems)
    other_copies = group_copies(other_in, other, other_sems)
    x_copies = column_copies(parts, x, x_sems)
    for a, b in zip(own_copies, other_copies):
        a.start()
        b.start()
    by_kind(flag, 1, len(x_copies), lambda used: start_all(x_copies[:used]))

    once = jnp.zeros((8, BLOCK), jnp.float32)
    twice = jnp.zeros((8, BLOCK), jnp.float32)
    for g in range(GROUPS):
        own_copies[g].wait()
        other_copies[g].wait()
        for d in range(NEAR):
            slot = g * NEAR + d
            gram = own[slot] + other[slot]
            own[slot] = gram
            squares = jnp.sum((gram * gram).reshape(BLOCK // 8, 8, BLOCK), axis=0)
            if d == 0 and g < EDGE:
                once += squares
            else:
                twice += squares
    total = jnp.full((8, LANE), jnp.sum(once + 2.0 * twice), jnp.float32)
    scale = jnp.sqrt(total) + 1e-06
    scale_out[...] = scale
    inverse = (1.0 / scale)[0:1, 0:1]
    root = (1.0 / jnp.sqrt(scale))[0:1, 0:1]
    each_pair(lambda slot, i, j, diagonal: mirror(normed, i, j, diagonal, own[slot] * inverse))
    polynomial_blocks(normed, polynomial)

    def send(g):
        pltpu.make_async_copy(group(other, g), group(packed_out, g), packed_sems.at[g]).start()

    def run(width):
        used = x_copies[: 1 if width < wide else len(x_copies)]
        wait_all(used)
        mixed_rows(polynomial, x, width, root, mixed)
        sends = [pltpu.make_async_copy(columns_of(mixed, 0, narrow), first_out, mixed_sems.at[0])]
        if width == wide:
            rest = columns_of(mixed, narrow, wide - narrow)
            sends.append(pltpu.make_async_copy(rest, second_out, mixed_sems.at[1]))
        start_all(sends)
        gram_blocks(mixed, width, other, send)
        wait_all(sends)

    by_kind(flag, narrow, wide, run)
    wait_all(group_copies(other, packed_out, packed_sems))


def last_kernel(flag, factor, own_in, other_in, x_in, *refs):
    count = len(refs) - 11
    polynomial_out, outs = refs[0], refs[1:count]
    own, other, x, mixed, normed, polynomial = refs[count : count + 6]
    own_sems, other_sems, x_sem, polynomial_sem, out_sems = refs[count + 6 :]
    own_copies = group_copies(own_in, own, own_sems)
    other_copies = group_copies(other_in, other, other_sems)
    for a, b in zip(own_copies, other_copies):
        a.start()
        b.start()
    x_copy = pltpu.make_async_copy(x_in, x, x_sem)
    heavy = flag[0] > 0

    @pl.when(heavy)
    def _():
        x_copy.start()

    for g in range(GROUPS):
        own_copies[g].wait()
        other_copies[g].wait()
        for d in range(NEAR):
            slot = g * NEAR + d
            i, j = (g, (g + d) % EDGE) if g < EDGE else (d, d + NEAR)
            mirror(normed, i, j, i == j, own[slot] + other[slot])
    polynomial_blocks(normed, polynomial)
    polynomial_copy = pltpu.make_async_copy(polynomial, polynomial_out, polynomial_sem)
    polynomial_copy.start()

    def out_copies(i):
        copies, at = [], 0
        for k, out in enumerate(outs):
            width = out.shape[1]
            source = mixed.at[span(i), pl.ds(at, width)]
            copies.append(pltpu.make_async_copy(source, rows_of(out, i), out_sems.at[k, i]))
            at += width
        return copies

    @pl.when(heavy)
    def _():
        x_copy.wait()
        mixed_rows(
            polynomial,
            x,
            x.shape[1],
            factor[0],
            mixed,
            after=lambda i: start_all(out_copies(i)),
        )
        for i in range(EDGE):
            wait_all(out_copies(i))

    polynomial_copy.wait()


def finish_kernel(factor, polynomial_in, x_in, out, x, mixed, polynomial, x_sem, in_sems, out_sems):
    x_copy = pltpu.make_async_copy(x_in, x, x_sem)
    x_copy.start()

    def in_copy(i):
        return pltpu.make_async_copy(rows_of(polynomial_in, i), rows_of(polynomial, i), in_sems.at[i])

    def out_copy(i):
        target = out.at[span(i), pl.ds(0, x.shape[1])]
        return pltpu.make_async_copy(rows_of(mixed, i), target, out_sems.at[i])

    start_all([in_copy(i) for i in range(EDGE)])
    x_copy.wait()
    mixed_rows(
        polynomial,
        x,
        x.shape[1],
        factor[0],
        mixed,
        before=lambda i: in_copy(i).wait(),
        after=lambda i: out_copy(i).start(),
    )
    wait_all([out_copy(i) for i in range(EDGE)])


def join_kernel(pick, own, *refs):
    handed, (given, out, stage, in_sems, out_sems) = refs[:-5], refs[-5:]
    narrow = out.shape[1] - 2 * GRANULE

    def incoming(where, source):
        target = columns_of(stage, where * GRANULE, GRANULE)
        return pltpu.make_async_copy(source, target, in_sems.at[where])

    def outgoing(where):
        at = narrow + where * GRANULE if where < 2 else 0
        source = columns_of(stage, where * GRANULE, GRANULE)
        return pltpu.make_async_copy(source, columns_of(out, at, GRANULE), out_sems.at[where])

    for where in range(3):
        for k in range(1 + len(handed)):
            if where == 2 and k == 0:
                continue
            source = columns_of(own, where * GRANULE, GRANULE) if k == 0 else handed[k - 1]

            @pl.when(pick[where] == k)
            def _():
                incoming(where, source).start()

    for where in range(2):
        incoming(where, columns_of(own, 0, GRANULE)).wait()
        outgoing(where).start()

    @pl.when(pick[2] > 0)
    def _():
        incoming(2, columns_of(own, 0, GRANULE)).wait()
        outgoing(2).start()
        outgoing(2).wait()

    for where in range(2):
        outgoing(where).wait()


def call(kernel, name, scalars, arrays, outs, scratch, limit, flops, small_outs=0, aliases=None):
    moved = sum(x.size * x.dtype.itemsize for x in arrays)
    moved += sum(math.prod(o.shape) * o.dtype.itemsize for o in outs)
    smem = pl.BlockSpec(memory_space=pltpu.SMEM)
    anywhere = pl.BlockSpec(memory_space=pl.ANY)
    vmem = pl.BlockSpec(memory_space=pltpu.VMEM)
    return pl.pallas_call(
        kernel,
        in_specs=[smem] * len(scalars) + [anywhere] * len(arrays),
        out_specs=[anywhere] * (len(outs) - small_outs) + [vmem] * small_outs,
        out_shape=list(outs),
        scratch_shapes=list(scratch),
        input_output_aliases=aliases or {},
        compiler_params=pltpu.CompilerParams(vmem_limit_bytes=limit * MIB),
        cost_estimate=pl.CostEstimate(flops=flops, bytes_accessed=moved, transcendentals=0),
        name=name,
    )(*scalars, *arrays)


def assemble(plan, square_order, swiglu_order, back):
    squares, wides = square_order.shape[0], swiglu_order.shape[0]
    rows, both = back.shape[1:]
    narrow = both - 2 * GRANULE
    wide = narrow + plan.granules * GRANULE
    parts = 1 + plan.passes

    def kernel(
        square_to, wide_to, source, square_out, wide_out, square_stage, wide_stage, *sems
    ):
        square_in, wide_in, square_sems, wide_sems = sems
        square_copies = [
            [
                pltpu.make_async_copy(
                    source.at[plan.light[j], :, pl.ds(0, narrow)], square_stage.at[j], square_in.at[j]
                )
            ]
            for j in range(squares)
        ]
        wide_copies = []
        for j in range(wides):
            moves = [(plan.heavy[j], 0, 0, both)]
            for b in range(2, plan.granules):
                chip, at = plan.column[(j, b)]
                moves.append((chip, at, narrow + b * GRANULE, GRANULE))
            wide_copies.append(
                [
                    pltpu.make_async_copy(
                        source.at[chip, :, pl.ds(at, width)],
                        wide_stage.at[j, :, pl.ds(to, width)],
                        wide_in.at[j * parts + n],
                    )
                    for n, (chip, at, to, width) in enumerate(moves)
                ]
            )
        for slot in square_copies + wide_copies:
            start_all(slot)
        outs = []
        for copies, stage, out, order, out_sems in (
            (square_copies, square_stage, square_out, square_to, square_sems),
            (wide_copies, wide_stage, wide_out, wide_to, wide_sems),
        ):
            for j, slot in enumerate(copies):
                wait_all(slot)
                outs.append(pltpu.make_async_copy(stage.at[j], out.at[order[j]], out_sems.at[j]))
                outs[-1].start()
        wait_all(outs)

    smem = pl.BlockSpec(memory_space=pltpu.SMEM)
    anywhere = pl.BlockSpec(memory_space=pl.ANY)
    shapes = [(squares, rows, narrow), (wides, rows, wide)]
    dma = pltpu.SemaphoreType.DMA
    return pl.pallas_call(
        kernel,
        in_specs=[smem, smem, anywhere],
        out_specs=[anywhere, anywhere],
        out_shape=[jax.ShapeDtypeStruct(shape, jnp.bfloat16) for shape in shapes],
        scratch_shapes=[pltpu.VMEM(shape, jnp.bfloat16) for shape in shapes]
        + [dma((squares,)), dma((wides * parts,)), dma((squares,)), dma((wides,))],
        compiler_params=pltpu.CompilerParams(vmem_limit_bytes=12 * MIB),
        name="assemble",
    )(square_order, swiglu_order, back)


def spread(known, chips, steps):
    for step in steps:
        known = known + lax.ppermute(known, "dp", [(s, s ^ step) for s in range(chips)])
    return known


def lookup(table, positions):
    matches = positions[:, None] == jnp.arange(table.shape[0], dtype=jnp.int32)[None, :]
    return jnp.sum(jnp.where(matches, table[None, :], 0), axis=1)


def local(
    square_grad,
    square_state,
    swiglu_grad,
    swiglu_state,
    square_order,
    swiglu_order,
    owners,
    vector_values,
    vector_grad,
    vector_first,
    vector_second,
    embed_values,
    embed_grad,
    embed_first,
    embed_second,
    embed_ranges,
):
    chips = lax.axis_size("dp")
    cores = lax.axis_size("tensor")
    chip = lax.axis_index("dp")
    square_count = square_grad.shape[0]
    swiglu_count = swiglu_grad.shape[0]
    chip_rows = D // chips
    narrow = D // cores
    plan = Plan(chips, cores, square_count, swiglu_count)

    swiglu_next, first_send, second_send = prepare_wide(
        plan, chips, cores, swiglu_grad, swiglu_state
    )
    square_next, first_send = prepare_narrow(
        plan, chips, cores, square_grad, square_state, first_send
    )
    both = ("dp", "tensor")
    second_got = lax.all_to_all(
        second_send.reshape(D, 2 * GRANULE), both, split_axis=0, concat_axis=0, tiled=True
    )
    first_got = lax.all_to_all(
        first_send.reshape(D, narrow), both, split_axis=0, concat_axis=0, tiled=True
    )
    heavy_here = jnp.asarray(plan.is_heavy)[chip]
    pieces = [second_got[:, :GRANULE], second_got[:, GRANULE:]]
    relayed = []
    for p in range(plan.passes):
        pick = jnp.asarray(plan.slot_in_pass[p])[chip]
        pairs = [(plan.take[p][k], plan.heavy[k]) for k in range(swiglu_count)]
        relayed.append(lax.ppermute(jnp.where(pick, pieces[1], pieces[0]), "dp", pairs))
    flag = heavy_here.astype(jnp.int32).reshape(1)
    factor = jnp.where(heavy_here, jnp.float32(math.sqrt(FF)), jnp.float32(math.sqrt(D))).reshape(1)
    packed = jax.ShapeDtypeStruct((PACKED, BLOCK, BLOCK), jnp.float32)
    whole_square = jax.ShapeDtypeStruct((D, D), jnp.bfloat16)
    first_shape = jax.ShapeDtypeStruct((D, narrow), jnp.bfloat16)
    extra = plan.granules * GRANULE
    second_shape = jax.ShapeDtypeStruct((D, extra), jnp.bfloat16)
    square_buffer = pltpu.VMEM((D, D), jnp.bfloat16)
    packed_buffer = pltpu.VMEM(packed.shape, jnp.float32)
    matrix_buffer = pltpu.VMEM((D, narrow + extra), jnp.bfloat16)
    first_buffer = pltpu.VMEM((D, narrow), jnp.bfloat16)
    second_buffer = pltpu.VMEM((D, extra), jnp.bfloat16)
    sems = lambda *shape: pltpu.SemaphoreType.DMA(shape)
    half = D * D * (narrow + extra)
    parts = [first_got, second_got, *relayed]
    (own,) = call(
        gram_kernel,
        "gram",
        [flag],
        parts,
        [packed],
        [matrix_buffer, packed_buffer, sems(len(parts)), sems(GROUPS)],
        15,
        half,
    )
    first_mid, second_mid, own_mid, scale = call(
        middle_kernel,
        "middle",
        [flag],
        [own, other_core(own), *parts],
        [first_shape, second_shape, packed, jax.ShapeDtypeStruct((8, LANE), jnp.float32)],
        [packed_buffer] * 2
        + [matrix_buffer] * 2
        + [square_buffer] * 2
        + [sems(GROUPS), sems(GROUPS), sems(len(parts)), sems(2), sems(GROUPS)],
        37,
        3 * half + D * D * D,
        small_outs=1,
    )
    steps = [1 << n for n in range(chips.bit_length() - 1)]
    logs = jnp.where(
        jnp.arange(chips, dtype=jnp.int32) == chip, 0.5 * jnp.log(scale[0, 0]), 0.0
    )
    logs = spread(logs, chips, steps[len(steps) // 2 :])
    other_mid, logs = lax.optimization_barrier((other_core(own_mid), logs))
    piece_shape = jax.ShapeDtypeStruct((D, GRANULE), jnp.bfloat16)
    pair_shape = jax.ShapeDtypeStruct((D, 2 * GRANULE), jnp.bfloat16)
    polynomial, kept, *rest = call(
        last_kernel,
        "last",
        [flag, factor],
        [own_mid, other_mid, second_mid],
        [whole_square, pair_shape] + [piece_shape] * plan.passes,
        [packed_buffer] * 2
        + [second_buffer] * 2
        + [square_buffer] * 2
        + [sems(GROUPS), sems(GROUPS), sems(), sems(), sems(1 + plan.passes, EDGE)],
        56,
        D * D * D + 2 * D * D * extra,
    )
    handed = []
    for p in range(plan.passes):
        pairs = [(plan.heavy[k], plan.back[p][k]) for k in range(swiglu_count)]
        handed.append(lax.ppermute(rest[p], "dp", pairs))
    back_shape = jax.ShapeDtypeStruct((D, narrow + 2 * GRANULE), jnp.bfloat16)
    (back_out,) = call(
        finish_kernel,
        "finish",
        [factor],
        [polynomial, first_mid],
        [back_shape],
        [first_buffer] * 2 + [square_buffer, sems(), sems(EDGE), sems(EDGE)],
        56,
        2 * D * D * narrow,
    )
    logs, back_out = lax.optimization_barrier((logs, back_out))
    logs = spread(logs, chips, steps[: len(steps) // 2])
    (back_out,) = call(
        join_kernel,
        "join",
        [jnp.asarray(plan.choice)[chip]],
        [kept, *handed, back_out],
        [back_shape],
        [pltpu.VMEM((D, 3 * GRANULE), jnp.bfloat16), sems(3), sems(3)],
        56,
        0,
        aliases={2 + plan.passes: 0},
    )
    back_out, logs = lax.optimization_barrier((back_out, logs))
    back = lax.all_to_all(
        back_out.reshape(chips, chip_rows, -1), "dp", split_axis=0, concat_axis=0, tiled=True
    )
    square_update, swiglu_update = assemble(plan, square_order, swiglu_order, back)

    slot_chips = np.array(plan.light + plan.heavy, np.int32)
    slot_owner = jnp.concatenate(
        [lookup(owners[:square_count], square_order), lookup(owners[square_count:], swiglu_order)]
    )
    slot_logs = logs[slot_chips]
    owner_norms = jnp.sum(jnp.where(slot_owner == chip, slot_logs, 0.0)).reshape(1)

    vector_step, first_vector, second_vector = adamw_terms(
        vector_values, vector_grad, vector_first, vector_second
    )
    embed_rows = embed_values.shape[0]
    row_numbers = chip * embed_rows + jnp.arange(embed_rows, dtype=jnp.int32)
    inside = (row_numbers[:, None] >= embed_ranges[None, :, 0]) & (
        row_numbers[:, None] < embed_ranges[None, :, 1]
    )
    row_live = jnp.sum(inside.astype(jnp.int32), axis=1) > 0
    direction, first_next, second_next = adamw_terms(
        embed_values, embed_grad, embed_first, embed_second
    )
    embed_step = jnp.where(row_live[:, None], direction, 0.0)
    first_embed = jnp.where(row_live[:, None], first_next, embed_first)
    second_embed = jnp.where(row_live[:, None], second_next, embed_second)
    return (
        square_next,
        swiglu_next,
        square_update,
        swiglu_update,
        owner_norms,
        vector_step,
        first_vector,
        second_vector,
        embed_step,
        first_embed,
        second_embed,
    )


def solution(mesh):
    flat = P(None, ("dp", "tensor"))
    vector = P(("dp", "tensor"))
    tile = P("dp", "tensor")
    update = P(None, "dp", "tensor")
    return jax.shard_map(
        local,
        mesh=mesh,
        in_specs=(flat,) * 4 + (P(),) * 3 + (vector,) * 4 + (tile,) * 4 + (P(),),
        out_specs=(flat, flat, update, update, P("dp")) + (vector,) * 3 + (tile,) * 3,
        check_vma=False,
    )
```

```python
import math

import jax
import jax.numpy as jnp
import numpy as np
from jax import lax
from jax.experimental import pallas as pl
from jax.experimental.pallas import tpu as pltpu
from jax.sharding import PartitionSpec as P

D = 1536
FF = 4096
NS_STEPS = 2


QUINTIC_LINEAR = 3.4445
QUINTIC_CUBIC = -4.775
QUINTIC_FIFTH = 2.0315
MOMENTUM = 0.95
BIAS_FIRST = 1.0 - 0.9**10
BIAS_SECOND = 1.0 - 0.95**10


def momentum_terms(gradient, state):
    state_next = MOMENTUM * state + gradient
    return (state_next, (gradient + MOMENTUM * state_next).astype(jnp.bfloat16))


def adamw_terms(values, gradient, first, second):
    first_next = 0.9 * first + 0.1 * gradient
    second_next = 0.95 * second + 0.05 * gradient * gradient
    direction = (
        first_next / BIAS_FIRST / (jnp.sqrt(second_next / BIAS_SECOND) + 1e-08) + 0.1 * values
    )
    return (direction, first_next, second_next)


LANE = 128
GRANULE = 256


class Plan:
    def __init__(self, chips, cores, square_count, swiglu_count):
        planes = 4
        per = chips // planes
        side = max(1, int(round(math.sqrt(per))))

        def coords(i):
            return (i % side, (i // side) % max(1, per // side), i // per)

        def hops(a, b):
            return sum(abs(p - q) for p, q in zip(coords(a), coords(b)))

        low = [i for i in range(chips) if coords(i)[2] < planes // 2]
        low.sort(key=lambda i: (-(sum(coords(i)) % 2), -coords(i)[2], i))
        high = [i for i in range(chips) if coords(i)[2] >= planes // 2]
        high.sort(key=lambda i: (-(sum(coords(i)) % 2), coords(i)[2], i))
        order = [c for pair in zip(low, high) for c in pair]
        self.heavy = order[:swiglu_count]
        rest = order[swiglu_count:]
        near = lambda c: sum(hops(c, o) == 1 for o in self.heavy)
        half = lambda c: coords(c)[2] < planes // 2
        spare = len(rest) - square_count
        self.idle = []
        for want in (True, False):
            pool = sorted((c for c in rest if half(c) == want), key=lambda c: -near(c))
            self.idle += pool[: spare // 2 if want else spare - spare // 2]
        self.light = [c for c in rest if c not in self.idle]
        helpers = rest
        narrow = D // cores
        wide = FF // cores
        self.granules = (wide - narrow) // GRANULE
        self.passes = self.granules - 2
        count = len(helpers)
        cost = lambda k, h: hops(h, self.heavy[k]) ** 2
        places = [(p, k) for p in range(self.passes) for k in range(swiglu_count)]

        def search(room):
            take = [
                [helpers[(k + p * swiglu_count) % count] for k in range(swiglu_count)]
                for p in range(self.passes)
            ]
            better = True
            while better:
                better = False
                for p, k in places:
                    for h in helpers:
                        used = sum(row.count(h) for row in take)
                        if used < room(h) and h not in take[p] and cost(k, h) < cost(k, take[p][k]):
                            take[p][k] = h
                            better = True
                    for q, m in places:
                        a, b = take[p][k], take[q][m]
                        if a == b or (q != p and (b in take[p] or a in take[q])):
                            continue
                        if cost(k, b) + cost(m, a) < cost(k, a) + cost(m, b):
                            take[p][k], take[q][m] = b, a
                            better = True
            return take

        self.take = take = search(lambda h: 2)
        self.back = search(lambda h: 3 if h in self.idle else 2)
        self.column = {}
        self.choice = np.zeros((chips, 3), np.int32)
        for j, o in enumerate(self.heavy):
            self.column[(j, 0)], self.column[(j, 1)] = (o, narrow), (o, narrow + GRANULE)
        taken = {}
        for p, k in places:
            h = self.back[p][k]
            where = taken[h] = taken.get(h, -1) + 1
            self.choice[h, where] = 1 + p
            self.column[(k, 2 + p)] = (h, narrow + where * GRANULE if where < 2 else 0)
        self.held = {o: [(j, 0), (j, 1)] for j, o in enumerate(self.heavy)}
        self.place = {}
        for p in range(self.passes):
            for k in range(swiglu_count):
                h = take[p][k]
                self.held.setdefault(h, []).append((k, 2 + p))
        for chip, list_of in self.held.items():
            for where, item in enumerate(list_of):
                self.place[item] = (chip, where)
        self.is_heavy = np.array([c in self.heavy for c in range(chips)])
        self.slot_in_pass = np.zeros((max(1, self.passes), chips), np.bool_)
        for p in range(self.passes):
            for k in range(swiglu_count):
                self.slot_in_pass[p, take[p][k]] = self.place[(k, 2 + p)][1] == 1


def momentum_rows(grad, state, following, sent):
    def row(r, carry):
        after = MOMENTUM * state[r] + grad[r]
        following[r] = after
        sent[r] = grad[r] + MOMENTUM * after
        return carry

    lax.fori_loop(0, grad.shape[0], row, 0)


def wide_kernel(plan, cores, grad, state, following, first, second, sent):
    narrow_tiles = D // cores // LANE
    wide_tiles = FF // cores // LANE
    momentum_rows(grad, state, following, sent)
    for j, owner in enumerate(plan.heavy):
        for core in range(cores):
            for t in range(wide_tiles):
                value = sent[:, core * wide_tiles + t, j, :].astype(jnp.bfloat16)
                if t < narrow_tiles:
                    first[owner * cores + core, :, t * LANE : (t + 1) * LANE] = value
                else:
                    b, part = divmod(t - narrow_tiles, GRANULE // LANE)
                    chip, where = plan.place[(j, b)]
                    at = where * GRANULE + part * LANE
                    second[chip * cores + core, :, at : at + LANE] = value
    for chip in range(len(plan.is_heavy)):
        for core in range(cores):
            if chip in plan.idle:
                first[chip * cores + core] = jnp.zeros(first.shape[1:], first.dtype)
            for where in range(len(plan.held.get(chip, [])), 2):
                second[chip * cores + core, :, where * GRANULE : (where + 1) * GRANULE] = jnp.zeros(
                    (first.shape[1], GRANULE), first.dtype
                )


def narrow_kernel(plan, cores, grad, state, given, following, first, sent, stage, sems):
    narrow_tiles = D // cores // LANE
    momentum_rows(grad, state, following, sent)
    copies = []
    for j, owner in enumerate(plan.light):
        for core in range(cores):
            for t in range(narrow_tiles):
                value = sent[:, core * narrow_tiles + t, j, :].astype(jnp.bfloat16)
                stage[j * cores + core, :, t * LANE : (t + 1) * LANE] = value
        copies.append(
            pltpu.make_async_copy(
                stage.at[pl.ds(j * cores, cores)], first.at[pl.ds(owner * cores, cores)], sems.at[j]
            )
        )
        copies[-1].start()
    for copy in copies:
        copy.wait()


def tiles_of(x, rows, width):
    return x.reshape(x.shape[0], rows, width // LANE, LANE).transpose(1, 2, 0, 3)


def flat_of(x):
    return x.transpose(2, 0, 1, 3).reshape(x.shape[2], -1)


def prepare_wide(plan, chips, cores, grad, state):
    rows = D // (chips * cores)
    chunk = 16 if rows % 16 == 0 else rows
    count = grad.shape[0]
    narrow = D // cores
    devices = chips * cores
    block = (chunk, FF // LANE, count, LANE)
    spec = pl.BlockSpec(block, lambda i: (i, 0, 0, 0))
    following, first, second = pl.pallas_call(
        lambda *refs: wide_kernel(plan, cores, *refs),
        grid=(rows // chunk,),
        in_specs=[spec, spec],
        out_specs=[
            spec,
            pl.BlockSpec((devices, chunk, narrow), lambda i: (0, i, 0)),
            pl.BlockSpec((devices, chunk, 2 * GRANULE), lambda i: (0, i, 0)),
        ],
        out_shape=[
            jax.ShapeDtypeStruct((rows,) + block[1:], jnp.float32),
            jax.ShapeDtypeStruct((devices, rows, narrow), jnp.bfloat16),
            jax.ShapeDtypeStruct((devices, rows, 2 * GRANULE), jnp.bfloat16),
        ],
        scratch_shapes=[pltpu.VMEM(block, jnp.float32)],
        compiler_params=pltpu.CompilerParams(vmem_limit_bytes=48 * 1024 * 1024),
        name="prepare_wide",
    )(tiles_of(grad, rows, FF), tiles_of(state, rows, FF))
    return flat_of(following), first, second


def prepare_narrow(plan, chips, cores, grad, state, first):
    rows = D // (chips * cores)
    count = grad.shape[0]
    block = (rows, D // LANE, count, LANE)
    vmem = pl.BlockSpec(memory_space=pltpu.VMEM)
    anywhere = pl.BlockSpec(memory_space=pl.ANY)
    following, first = pl.pallas_call(
        lambda *refs: narrow_kernel(plan, cores, *refs),
        in_specs=[vmem, vmem, anywhere],
        out_specs=[vmem, anywhere],
        out_shape=[
            jax.ShapeDtypeStruct(block, jnp.float32),
            jax.ShapeDtypeStruct(first.shape, first.dtype),
        ],
        input_output_aliases={2: 1},
        scratch_shapes=[
            pltpu.VMEM(block, jnp.float32),
            pltpu.VMEM((count * cores, rows, D // cores), jnp.bfloat16),
            pltpu.SemaphoreType.DMA((count,)),
        ],
        compiler_params=pltpu.CompilerParams(vmem_limit_bytes=32 * 1024 * 1024),
        cost_estimate=pl.CostEstimate(
            flops=0, bytes_accessed=3 * grad.size * 4 + grad.size * 2, transcendentals=0
        ),
        name="prepare_narrow",
    )(tiles_of(grad, rows, D), tiles_of(state, rows, D), first)
    return flat_of(following), first


def other_core(x):
    return lax.ppermute(x, "tensor", [(0, 1), (1, 0)])


BLOCK = 256
EDGE = D // BLOCK
NEAR = EDGE // 2
PACKED = EDGE * NEAR + NEAR
GROUPS = EDGE + 1
MIB = 1024 * 1024


def each_pair(body, after=None):
    for i in range(EDGE):
        for d in range(NEAR):
            body(i * NEAR + d, i, (i + d) % EDGE, d == 0)
        if after is not None:
            after(i)
    for i in range(NEAR):
        body(EDGE * NEAR + i, i, i + NEAR, False)
    if after is not None:
        after(EDGE)


def span(i):
    return pl.ds(i * BLOCK, BLOCK)


def group(ref, g):
    return ref.at[pl.ds(g * NEAR, NEAR)]


def rows_of(ref, i):
    return ref.at[span(i), :]


def columns_of(ref, at, width):
    return ref.at[:, pl.ds(at, width)]


def gram_blocks(x, width, out, after):
    def body(slot, i, j, diagonal):
        out[slot] = lax.dot_general(
            x[span(i), :width],
            x[span(j), :width],
            (((1,), (1,)), ((), ())),
            preferred_element_type=jnp.float32,
        )

    each_pair(body, after)


def mirror(out, i, j, diagonal, value):
    rounded = value.astype(out.dtype)
    out[span(i), span(j)] = rounded
    if not diagonal:
        out[span(j), span(i)] = rounded.T


def polynomial_blocks(normed, out):
    def body(slot, i, j, diagonal):
        squared = jnp.dot(normed[span(i), :], normed[:, span(j)], preferred_element_type=jnp.float32)
        value = QUINTIC_CUBIC * normed[span(i), span(j)].astype(jnp.float32) + QUINTIC_FIFTH * squared
        mirror(out, i, j, diagonal, value)

    each_pair(body)


def mixed_rows(polynomial, x, width, scale, out, before=None, after=None):
    for i in range(EDGE):
        if before is not None:
            before(i)
        for c in range(0, width, BLOCK):
            product = jnp.dot(
                polynomial[span(i), :], x[:, c : c + BLOCK], preferred_element_type=jnp.float32
            )
            mixed = QUINTIC_LINEAR * x[span(i), c : c + BLOCK].astype(jnp.float32) + product
            out[span(i), c : c + BLOCK] = (mixed * scale).astype(out.dtype)
        if after is not None:
            after(i)


def column_copies(sources, x, sems):
    copies, at = [], 0
    for k, source in enumerate(sources):
        width = source.shape[1]
        copies.append(pltpu.make_async_copy(source, columns_of(x, at, width), sems.at[k]))
        at += width
    return copies


def start_all(copies):
    for copy in copies:
        copy.start()


def wait_all(copies):
    for copy in copies:
        copy.wait()


def by_kind(flag, narrow, wide, body):
    @pl.when(flag[0] > 0)
    def _():
        body(wide)

    @pl.when(flag[0] <= 0)
    def _():
        body(narrow)


def gram_kernel(flag, *refs):
    parts, (out, x, blocks, in_sems, out_sems) = refs[:-5], refs[-5:]
    copies = column_copies(parts, x, in_sems)

    def send(g):
        pltpu.make_async_copy(group(blocks, g), group(out, g), out_sems.at[g]).start()

    def run(width):
        used = copies[: 1 if width < x.shape[1] else len(copies)]
        start_all(used)
        wait_all(used)
        gram_blocks(x, width, blocks, send)

    by_kind(flag, parts[0].shape[1], x.shape[1], run)
    wait_all(
        [
            pltpu.make_async_copy(group(blocks, g), group(out, g), out_sems.at[g])
            for g in range(GROUPS)
        ]
    )


def group_copies(source, target, sems):
    return [
        pltpu.make_async_copy(group(source, g), group(target, g), sems.at[g]) for g in range(GROUPS)
    ]


def middle_kernel(flag, own_in, other_in, *refs):
    parts, refs = refs[:-15], refs[-15:]
    first_out, second_out, packed_out, scale_out = refs[:4]
    own, other, x, mixed, normed, polynomial = refs[4:10]
    own_sems, other_sems, x_sems, mixed_sems, packed_sems = refs[10:]
    narrow, wide = first_out.shape[1], x.shape[1]
    own_copies = group_copies(own_in, own, own_sems)
    other_copies = group_copies(other_in, other, other_sems)
    x_copies = column_copies(parts, x, x_sems)
    for a, b in zip(own_copies, other_copies):
        a.start()
        b.start()
    by_kind(flag, 1, len(x_copies), lambda used: start_all(x_copies[:used]))

    once = jnp.zeros((8, BLOCK), jnp.float32)
    twice = jnp.zeros((8, BLOCK), jnp.float32)
    for g in range(GROUPS):
        own_copies[g].wait()
        other_copies[g].wait()
        for d in range(NEAR):
            slot = g * NEAR + d
            gram = own[slot] + other[slot]
            own[slot] = gram
            squares = jnp.sum((gram * gram).reshape(BLOCK // 8, 8, BLOCK), axis=0)
            if d == 0 and g < EDGE:
                once += squares
            else:
                twice += squares
    total = jnp.full((8, LANE), jnp.sum(once + 2.0 * twice), jnp.float32)
    scale = jnp.sqrt(total) + 1e-06
    scale_out[...] = scale
    inverse = (1.0 / scale)[0:1, 0:1]
    root = (1.0 / jnp.sqrt(scale))[0:1, 0:1]
    each_pair(lambda slot, i, j, diagonal: mirror(normed, i, j, diagonal, own[slot] * inverse))
    polynomial_blocks(normed, polynomial)

    def send(g):
        pltpu.make_async_copy(group(other, g), group(packed_out, g), packed_sems.at[g]).start()

    def run(width):
        used = x_copies[: 1 if width < wide else len(x_copies)]
        wait_all(used)
        mixed_rows(polynomial, x, width, root, mixed)
        sends = [pltpu.make_async_copy(columns_of(mixed, 0, narrow), first_out, mixed_sems.at[0])]
        if width == wide:
            rest = columns_of(mixed, narrow, wide - narrow)
            sends.append(pltpu.make_async_copy(rest, second_out, mixed_sems.at[1]))
        start_all(sends)
        gram_blocks(mixed, width, other, send)
        wait_all(sends)

    by_kind(flag, narrow, wide, run)
    wait_all(group_copies(other, packed_out, packed_sems))


def last_kernel(flag, factor, own_in, other_in, x_in, *refs):
    count = len(refs) - 11
    polynomial_out, outs = refs[0], refs[1:count]
    own, other, x, mixed, normed, polynomial = refs[count : count + 6]
    own_sems, other_sems, x_sem, polynomial_sem, out_sems = refs[count + 6 :]
    own_copies = group_copies(own_in, own, own_sems)
    other_copies = group_copies(other_in, other, other_sems)
    for a, b in zip(own_copies, other_copies):
        a.start()
        b.start()
    x_copy = pltpu.make_async_copy(x_in, x, x_sem)
    heavy = flag[0] > 0

    @pl.when(heavy)
    def _():
        x_copy.start()

    for g in range(GROUPS):
        own_copies[g].wait()
        other_copies[g].wait()
        for d in range(NEAR):
            slot = g * NEAR + d
            i, j = (g, (g + d) % EDGE) if g < EDGE else (d, d + NEAR)
            mirror(normed, i, j, i == j, own[slot] + other[slot])
    polynomial_blocks(normed, polynomial)
    polynomial_copy = pltpu.make_async_copy(polynomial, polynomial_out, polynomial_sem)
    polynomial_copy.start()

    def out_copies(i):
        copies, at = [], 0
        for k, out in enumerate(outs):
            width = out.shape[1]
            source = mixed.at[span(i), pl.ds(at, width)]
            copies.append(pltpu.make_async_copy(source, rows_of(out, i), out_sems.at[k, i]))
            at += width
        return copies

    @pl.when(heavy)
    def _():
        x_copy.wait()
        mixed_rows(
            polynomial,
            x,
            x.shape[1],
            factor[0],
            mixed,
            after=lambda i: start_all(out_copies(i)),
        )
        for i in range(EDGE):
            wait_all(out_copies(i))

    polynomial_copy.wait()


def finish_kernel(factor, polynomial_in, x_in, out, x, mixed, polynomial, x_sem, in_sems, out_sems):
    x_copy = pltpu.make_async_copy(x_in, x, x_sem)
    x_copy.start()

    def in_copy(i):
        return pltpu.make_async_copy(rows_of(polynomial_in, i), rows_of(polynomial, i), in_sems.at[i])

    def out_copy(i):
        target = out.at[span(i), pl.ds(0, x.shape[1])]
        return pltpu.make_async_copy(rows_of(mixed, i), target, out_sems.at[i])

    start_all([in_copy(i) for i in range(EDGE)])
    x_copy.wait()
    mixed_rows(
        polynomial,
        x,
        x.shape[1],
        factor[0],
        mixed,
        before=lambda i: in_copy(i).wait(),
        after=lambda i: out_copy(i).start(),
    )
    wait_all([out_copy(i) for i in range(EDGE)])


def join_kernel(table, me, own, *refs):
    pick = [table[me[0] * 3 + where] for where in range(3)]
    handed, (given, out, stage, in_sems, out_sems) = refs[:-5], refs[-5:]
    narrow = out.shape[1] - 2 * GRANULE

    def incoming(where, source):
        target = columns_of(stage, where * GRANULE, GRANULE)
        return pltpu.make_async_copy(source, target, in_sems.at[where])

    def outgoing(where):
        at = narrow + where * GRANULE if where < 2 else 0
        source = columns_of(stage, where * GRANULE, GRANULE)
        return pltpu.make_async_copy(source, columns_of(out, at, GRANULE), out_sems.at[where])

    for where in range(3):
        for k in range(1 + len(handed)):
            if where == 2 and k == 0:
                continue
            source = columns_of(own, where * GRANULE, GRANULE) if k == 0 else handed[k - 1]

            @pl.when(pick[where] == k)
            def _():
                incoming(where, source).start()

    for where in range(2):
        incoming(where, columns_of(own, 0, GRANULE)).wait()
        outgoing(where).start()

    @pl.when(pick[2] > 0)
    def _():
        incoming(2, columns_of(own, 0, GRANULE)).wait()
        outgoing(2).start()
        outgoing(2).wait()

    for where in range(2):
        outgoing(where).wait()


def call(kernel, name, scalars, arrays, outs, scratch, limit, flops, small_outs=0, aliases=None):
    moved = sum(x.size * x.dtype.itemsize for x in arrays)
    moved += sum(math.prod(o.shape) * o.dtype.itemsize for o in outs)
    smem = pl.BlockSpec(memory_space=pltpu.SMEM)
    anywhere = pl.BlockSpec(memory_space=pl.ANY)
    vmem = pl.BlockSpec(memory_space=pltpu.VMEM)
    return pl.pallas_call(
        kernel,
        in_specs=[smem] * len(scalars) + [anywhere] * len(arrays),
        out_specs=[anywhere] * (len(outs) - small_outs) + [vmem] * small_outs,
        out_shape=list(outs),
        scratch_shapes=list(scratch),
        input_output_aliases=aliases or {},
        compiler_params=pltpu.CompilerParams(vmem_limit_bytes=limit * MIB),
        cost_estimate=pl.CostEstimate(flops=flops, bytes_accessed=moved, transcendentals=0),
        name=name,
    )(*scalars, *arrays)


def assemble(plan, square_order, swiglu_order, back):
    squares, wides = square_order.shape[0], swiglu_order.shape[0]
    rows, both = back.shape[1:]
    narrow = both - 2 * GRANULE
    wide = narrow + plan.granules * GRANULE
    parts = 1 + plan.passes

    def kernel(
        square_to, wide_to, source, square_out, wide_out, square_stage, wide_stage, *sems
    ):
        square_in, wide_in, square_sems, wide_sems = sems
        square_copies = [
            [
                pltpu.make_async_copy(
                    source.at[plan.light[j], :, pl.ds(0, narrow)], square_stage.at[j], square_in.at[j]
                )
            ]
            for j in range(squares)
        ]
        wide_copies = []
        for j in range(wides):
            moves = [(plan.heavy[j], 0, 0, both)]
            for b in range(2, plan.granules):
                chip, at = plan.column[(j, b)]
                moves.append((chip, at, narrow + b * GRANULE, GRANULE))
            wide_copies.append(
                [
                    pltpu.make_async_copy(
                        source.at[chip, :, pl.ds(at, width)],
                        wide_stage.at[j, :, pl.ds(to, width)],
                        wide_in.at[j * parts + n],
                    )
                    for n, (chip, at, to, width) in enumerate(moves)
                ]
            )
        for slot in square_copies + wide_copies:
            start_all(slot)
        outs = []
        for copies, stage, out, order, out_sems in (
            (square_copies, square_stage, square_out, square_to, square_sems),
            (wide_copies, wide_stage, wide_out, wide_to, wide_sems),
        ):
            for j, slot in enumerate(copies):
                wait_all(slot)
                outs.append(pltpu.make_async_copy(stage.at[j], out.at[order[j]], out_sems.at[j]))
                outs[-1].start()
        wait_all(outs)

    smem = pl.BlockSpec(memory_space=pltpu.SMEM)
    anywhere = pl.BlockSpec(memory_space=pl.ANY)
    shapes = [(squares, rows, narrow), (wides, rows, wide)]
    dma = pltpu.SemaphoreType.DMA
    return pl.pallas_call(
        kernel,
        in_specs=[smem, smem, anywhere],
        out_specs=[anywhere, anywhere],
        out_shape=[jax.ShapeDtypeStruct(shape, jnp.bfloat16) for shape in shapes],
        scratch_shapes=[pltpu.VMEM(shape, jnp.bfloat16) for shape in shapes]
        + [dma((squares,)), dma((wides * parts,)), dma((squares,)), dma((wides,))],
        compiler_params=pltpu.CompilerParams(vmem_limit_bytes=12 * MIB),
        name="assemble",
    )(square_order, swiglu_order, back)


def spread(known, chips, steps):
    for step in steps:
        known = known + lax.ppermute(known, "dp", [(s, s ^ step) for s in range(chips)])
    return known


def lookup(table, positions):
    matches = positions[:, None] == jnp.arange(table.shape[0], dtype=jnp.int32)[None, :]
    return jnp.sum(jnp.where(matches, table[None, :], 0), axis=1)


def local(
    square_grad,
    square_state,
    swiglu_grad,
    swiglu_state,
    square_order,
    swiglu_order,
    owners,
    vector_values,
    vector_grad,
    vector_first,
    vector_second,
    embed_values,
    embed_grad,
    embed_first,
    embed_second,
    embed_ranges,
):
    chips = lax.axis_size("dp")
    cores = lax.axis_size("tensor")
    chip = lax.axis_index("dp")
    square_count = square_grad.shape[0]
    swiglu_count = swiglu_grad.shape[0]
    chip_rows = D // chips
    narrow = D // cores
    plan = Plan(chips, cores, square_count, swiglu_count)

    swiglu_next, first_send, second_send = prepare_wide(
        plan, chips, cores, swiglu_grad, swiglu_state
    )
    square_next, first_send = prepare_narrow(
        plan, chips, cores, square_grad, square_state, first_send
    )
    both = ("dp", "tensor")
    second_got = lax.all_to_all(
        second_send.reshape(D, 2 * GRANULE), both, split_axis=0, concat_axis=0, tiled=True
    )
    first_got = lax.all_to_all(
        first_send.reshape(D, narrow), both, split_axis=0, concat_axis=0, tiled=True
    )
    heavy_here = jnp.asarray(plan.is_heavy)[chip]
    pieces = [second_got[:, :GRANULE], second_got[:, GRANULE:]]
    relayed = []
    for p in range(plan.passes):
        pick = jnp.asarray(plan.slot_in_pass[p])[chip]
        pairs = [(plan.take[p][k], plan.heavy[k]) for k in range(swiglu_count)]
        relayed.append(lax.ppermute(jnp.where(pick, pieces[1], pieces[0]), "dp", pairs))
    flag = heavy_here.astype(jnp.int32).reshape(1)
    factor = jnp.where(heavy_here, jnp.float32(math.sqrt(FF)), jnp.float32(math.sqrt(D))).reshape(1)
    packed = jax.ShapeDtypeStruct((PACKED, BLOCK, BLOCK), jnp.float32)
    whole_square = jax.ShapeDtypeStruct((D, D), jnp.bfloat16)
    first_shape = jax.ShapeDtypeStruct((D, narrow), jnp.bfloat16)
    extra = plan.granules * GRANULE
    second_shape = jax.ShapeDtypeStruct((D, extra), jnp.bfloat16)
    square_buffer = pltpu.VMEM((D, D), jnp.bfloat16)
    packed_buffer = pltpu.VMEM(packed.shape, jnp.float32)
    matrix_buffer = pltpu.VMEM((D, narrow + extra), jnp.bfloat16)
    first_buffer = pltpu.VMEM((D, narrow), jnp.bfloat16)
    second_buffer = pltpu.VMEM((D, extra), jnp.bfloat16)
    sems = lambda *shape: pltpu.SemaphoreType.DMA(shape)
    half = D * D * (narrow + extra)
    parts = [first_got, second_got, *relayed]
    (own,) = call(
        gram_kernel,
        "gram",
        [flag],
        parts,
        [packed],
        [matrix_buffer, packed_buffer, sems(len(parts)), sems(GROUPS)],
        15,
        half,
    )
    first_mid, second_mid, own_mid, scale = call(
        middle_kernel,
        "middle",
        [flag],
        [own, other_core(own), *parts],
        [first_shape, second_shape, packed, jax.ShapeDtypeStruct((8, LANE), jnp.float32)],
        [packed_buffer] * 2
        + [matrix_buffer] * 2
        + [square_buffer] * 2
        + [sems(GROUPS), sems(GROUPS), sems(len(parts)), sems(2), sems(GROUPS)],
        37,
        3 * half + D * D * D,
        small_outs=1,
    )
    steps = [1 << n for n in range(chips.bit_length() - 1)]
    logs = jnp.where(
        jnp.arange(chips, dtype=jnp.int32) == chip, 0.5 * jnp.log(scale[0, 0]), 0.0
    )
    logs = spread(logs, chips, steps[len(steps) // 2 :])
    other_mid, logs = lax.optimization_barrier((other_core(own_mid), logs))
    piece_shape = jax.ShapeDtypeStruct((D, GRANULE), jnp.bfloat16)
    pair_shape = jax.ShapeDtypeStruct((D, 2 * GRANULE), jnp.bfloat16)
    polynomial, kept, *rest = call(
        last_kernel,
        "last",
        [flag, factor],
        [own_mid, other_mid, second_mid],
        [whole_square, pair_shape] + [piece_shape] * plan.passes,
        [packed_buffer] * 2
        + [second_buffer] * 2
        + [square_buffer] * 2
        + [sems(GROUPS), sems(GROUPS), sems(), sems(), sems(1 + plan.passes, EDGE)],
        56,
        D * D * D + 2 * D * D * extra,
    )
    handed = []
    for p in range(plan.passes):
        pairs = [(plan.heavy[k], plan.back[p][k]) for k in range(swiglu_count)]
        handed.append(lax.ppermute(rest[p], "dp", pairs))
    back_shape = jax.ShapeDtypeStruct((D, narrow + 2 * GRANULE), jnp.bfloat16)
    (back_out,) = call(
        finish_kernel,
        "finish",
        [factor],
        [polynomial, first_mid],
        [back_shape],
        [first_buffer] * 2 + [square_buffer, sems(), sems(EDGE), sems(EDGE)],
        56,
        2 * D * D * narrow,
    )
    logs, back_out = lax.optimization_barrier((logs, back_out))
    logs = spread(logs, chips, steps[: len(steps) // 2])
    (back_out,) = call(
        join_kernel,
        "join",
        [jnp.asarray(plan.choice.reshape(-1)), chip.reshape(1)],
        [kept, *handed, back_out],
        [back_shape],
        [pltpu.VMEM((D, 3 * GRANULE), jnp.bfloat16), sems(3), sems(3)],
        56,
        0,
        aliases={3 + plan.passes: 0},
    )
    back_out, logs = lax.optimization_barrier((back_out, logs))
    back = lax.all_to_all(
        back_out.reshape(chips, chip_rows, -1), "dp", split_axis=0, concat_axis=0, tiled=True
    )
    square_update, swiglu_update = assemble(plan, square_order, swiglu_order, back)

    slot_chips = np.array(plan.light + plan.heavy, np.int32)
    slot_owner = jnp.concatenate(
        [lookup(owners[:square_count], square_order), lookup(owners[square_count:], swiglu_order)]
    )
    slot_logs = logs[slot_chips]
    owner_norms = jnp.sum(jnp.where(slot_owner == chip, slot_logs, 0.0)).reshape(1)

    vector_step, first_vector, second_vector = adamw_terms(
        vector_values, vector_grad, vector_first, vector_second
    )
    embed_rows = embed_values.shape[0]
    row_numbers = chip * embed_rows + jnp.arange(embed_rows, dtype=jnp.int32)
    inside = (row_numbers[:, None] >= embed_ranges[None, :, 0]) & (
        row_numbers[:, None] < embed_ranges[None, :, 1]
    )
    row_live = jnp.sum(inside.astype(jnp.int32), axis=1) > 0
    direction, first_next, second_next = adamw_terms(
        embed_values, embed_grad, embed_first, embed_second
    )
    embed_step = jnp.where(row_live[:, None], direction, 0.0)
    first_embed = jnp.where(row_live[:, None], first_next, embed_first)
    second_embed = jnp.where(row_live[:, None], second_next, embed_second)
    return (
        square_next,
        swiglu_next,
        square_update,
        swiglu_update,
        owner_norms,
        vector_step,
        first_vector,
        second_vector,
        embed_step,
        first_embed,
        second_embed,
    )


def solution(mesh):
    flat = P(None, ("dp", "tensor"))
    vector = P(("dp", "tensor"))
    tile = P("dp", "tensor")
    update = P(None, "dp", "tensor")
    return jax.shard_map(
        local,
        mesh=mesh,
        in_specs=(flat,) * 4 + (P(),) * 3 + (vector,) * 4 + (tile,) * 4 + (P(),),
        out_specs=(flat, flat, update, update, P("dp")) + (vector,) * 3 + (tile,) * 3,
        check_vma=False,
    )
```

```python
import math

import jax
import jax.numpy as jnp
import numpy as np
from jax import lax
from jax.experimental import pallas as pl
from jax.experimental.pallas import tpu as pltpu
from jax.sharding import PartitionSpec as P

D = 1536
FF = 4096
NS_STEPS = 2


QUINTIC_LINEAR = 3.4445
QUINTIC_CUBIC = -4.775
QUINTIC_FIFTH = 2.0315
MOMENTUM = 0.95
BIAS_FIRST = 1.0 - 0.9**10
BIAS_SECOND = 1.0 - 0.95**10


def momentum_terms(gradient, state):
    state_next = MOMENTUM * state + gradient
    return (state_next, (gradient + MOMENTUM * state_next).astype(jnp.bfloat16))


def adamw_terms(values, gradient, first, second):
    first_next = 0.9 * first + 0.1 * gradient
    second_next = 0.95 * second + 0.05 * gradient * gradient
    direction = (
        first_next / BIAS_FIRST / (jnp.sqrt(second_next / BIAS_SECOND) + 1e-08) + 0.1 * values
    )
    return (direction, first_next, second_next)


LANE = 128
GRANULE = 256


class Plan:
    def __init__(self, chips, cores, square_count, swiglu_count):
        planes = 4
        per = chips // planes
        side = max(1, int(round(math.sqrt(per))))

        def coords(i):
            return (i % side, (i // side) % max(1, per // side), i // per)

        def hops(a, b):
            return sum(abs(p - q) for p, q in zip(coords(a), coords(b)))

        low = [i for i in range(chips) if coords(i)[2] < planes // 2]
        low.sort(key=lambda i: (-(sum(coords(i)) % 2), -coords(i)[2], i))
        high = [i for i in range(chips) if coords(i)[2] >= planes // 2]
        high.sort(key=lambda i: (-(sum(coords(i)) % 2), coords(i)[2], i))
        order = [c for pair in zip(low, high) for c in pair]
        self.heavy = order[:swiglu_count]
        rest = order[swiglu_count:]
        near = lambda c: sum(hops(c, o) == 1 for o in self.heavy)
        half = lambda c: coords(c)[2] < planes // 2
        spare = len(rest) - square_count
        self.idle = []
        for want in (True, False):
            pool = sorted((c for c in rest if half(c) == want), key=lambda c: -near(c))
            self.idle += pool[: spare // 2 if want else spare - spare // 2]
        self.light = [c for c in rest if c not in self.idle]
        helpers = rest
        narrow = D // cores
        wide = FF // cores
        self.granules = (wide - narrow) // GRANULE
        self.passes = self.granules - 2
        count = len(helpers)
        cost = lambda k, h: hops(h, self.heavy[k]) ** 2
        places = [(p, k) for p in range(self.passes) for k in range(swiglu_count)]

        def search(room):
            take = [
                [helpers[(k + p * swiglu_count) % count] for k in range(swiglu_count)]
                for p in range(self.passes)
            ]
            better = True
            while better:
                better = False
                for p, k in places:
                    for h in helpers:
                        used = sum(row.count(h) for row in take)
                        if used < room(h) and h not in take[p] and cost(k, h) < cost(k, take[p][k]):
                            take[p][k] = h
                            better = True
                    for q, m in places:
                        a, b = take[p][k], take[q][m]
                        if a == b or (q != p and (b in take[p] or a in take[q])):
                            continue
                        if cost(k, b) + cost(m, a) < cost(k, a) + cost(m, b):
                            take[p][k], take[q][m] = b, a
                            better = True
            return take

        self.take = take = search(lambda h: 2)
        self.back = search(lambda h: 3 if h in self.idle else 2)
        self.column = {}
        self.choice = np.zeros((chips, 3), np.int32)
        for j, o in enumerate(self.heavy):
            self.column[(j, 0)], self.column[(j, 1)] = (o, narrow), (o, narrow + GRANULE)
        taken = {}
        for p, k in places:
            h = self.back[p][k]
            where = taken[h] = taken.get(h, -1) + 1
            self.choice[h, where] = 1 + p
            self.column[(k, 2 + p)] = (h, narrow + where * GRANULE if where < 2 else 0)
        self.held = {o: [(j, 0), (j, 1)] for j, o in enumerate(self.heavy)}
        self.place = {}
        for p in range(self.passes):
            for k in range(swiglu_count):
                h = take[p][k]
                self.held.setdefault(h, []).append((k, 2 + p))
        for chip, list_of in self.held.items():
            for where, item in enumerate(list_of):
                self.place[item] = (chip, where)
        self.is_heavy = np.array([c in self.heavy for c in range(chips)])
        self.slot_in_pass = np.zeros((max(1, self.passes), chips), np.bool_)
        for p in range(self.passes):
            for k in range(swiglu_count):
                self.slot_in_pass[p, take[p][k]] = self.place[(k, 2 + p)][1] == 1


def momentum_rows(grad, state, following, sent):
    def row(r, carry):
        after = MOMENTUM * state[r] + grad[r]
        following[r] = after
        sent[r] = grad[r] + MOMENTUM * after
        return carry

    lax.fori_loop(0, grad.shape[0], row, 0)


def wide_kernel(plan, cores, grad, state, following, first, second, sent):
    narrow_tiles = D // cores // LANE
    wide_tiles = FF // cores // LANE
    momentum_rows(grad, state, following, sent)
    for j, owner in enumerate(plan.heavy):
        for core in range(cores):
            for t in range(wide_tiles):
                value = sent[:, core * wide_tiles + t, j, :].astype(jnp.bfloat16)
                if t < narrow_tiles:
                    first[owner * cores + core, :, t * LANE : (t + 1) * LANE] = value
                else:
                    b, part = divmod(t - narrow_tiles, GRANULE // LANE)
                    chip, where = plan.place[(j, b)]
                    at = where * GRANULE + part * LANE
                    second[chip * cores + core, :, at : at + LANE] = value
    for chip in range(len(plan.is_heavy)):
        for core in range(cores):
            if chip in plan.idle:
                first[chip * cores + core] = jnp.zeros(first.shape[1:], first.dtype)
            for where in range(len(plan.held.get(chip, [])), 2):
                second[chip * cores + core, :, where * GRANULE : (where + 1) * GRANULE] = jnp.zeros(
                    (first.shape[1], GRANULE), first.dtype
                )


def narrow_kernel(plan, cores, grad, state, given, following, first, sent, stage, sems):
    narrow_tiles = D // cores // LANE
    momentum_rows(grad, state, following, sent)
    copies = []
    for j, owner in enumerate(plan.light):
        for core in range(cores):
            for t in range(narrow_tiles):
                value = sent[:, core * narrow_tiles + t, j, :].astype(jnp.bfloat16)
                stage[j * cores + core, :, t * LANE : (t + 1) * LANE] = value
        copies.append(
            pltpu.make_async_copy(
                stage.at[pl.ds(j * cores, cores)], first.at[pl.ds(owner * cores, cores)], sems.at[j]
            )
        )
        copies[-1].start()
    for copy in copies:
        copy.wait()


def tiles_of(x, rows, width):
    return x.reshape(x.shape[0], rows, width // LANE, LANE).transpose(1, 2, 0, 3)


def flat_of(x):
    return x.transpose(2, 0, 1, 3).reshape(x.shape[2], -1)


def prepare_wide(plan, chips, cores, grad, state):
    rows = D // (chips * cores)
    chunk = 16 if rows % 16 == 0 else rows
    count = grad.shape[0]
    narrow = D // cores
    devices = chips * cores
    block = (chunk, FF // LANE, count, LANE)
    spec = pl.BlockSpec(block, lambda i: (i, 0, 0, 0))
    following, first, second = pl.pallas_call(
        lambda *refs: wide_kernel(plan, cores, *refs),
        grid=(rows // chunk,),
        in_specs=[spec, spec],
        out_specs=[
            spec,
            pl.BlockSpec((devices, chunk, narrow), lambda i: (0, i, 0)),
            pl.BlockSpec((devices, chunk, 2 * GRANULE), lambda i: (0, i, 0)),
        ],
        out_shape=[
            jax.ShapeDtypeStruct((rows,) + block[1:], jnp.float32),
            jax.ShapeDtypeStruct((devices, rows, narrow), jnp.bfloat16),
            jax.ShapeDtypeStruct((devices, rows, 2 * GRANULE), jnp.bfloat16),
        ],
        scratch_shapes=[pltpu.VMEM(block, jnp.float32)],
        compiler_params=pltpu.CompilerParams(vmem_limit_bytes=48 * 1024 * 1024),
        name="prepare_wide",
    )(tiles_of(grad, rows, FF), tiles_of(state, rows, FF))
    return flat_of(following), first, second


def prepare_narrow(plan, chips, cores, grad, state, first):
    rows = D // (chips * cores)
    count = grad.shape[0]
    block = (rows, D // LANE, count, LANE)
    vmem = pl.BlockSpec(memory_space=pltpu.VMEM)
    anywhere = pl.BlockSpec(memory_space=pl.ANY)
    following, first = pl.pallas_call(
        lambda *refs: narrow_kernel(plan, cores, *refs),
        in_specs=[vmem, vmem, anywhere],
        out_specs=[vmem, anywhere],
        out_shape=[
            jax.ShapeDtypeStruct(block, jnp.float32),
            jax.ShapeDtypeStruct(first.shape, first.dtype),
        ],
        input_output_aliases={2: 1},
        scratch_shapes=[
            pltpu.VMEM(block, jnp.float32),
            pltpu.VMEM((count * cores, rows, D // cores), jnp.bfloat16),
            pltpu.SemaphoreType.DMA((count,)),
        ],
        compiler_params=pltpu.CompilerParams(vmem_limit_bytes=32 * 1024 * 1024),
        cost_estimate=pl.CostEstimate(
            flops=0, bytes_accessed=3 * grad.size * 4 + grad.size * 2, transcendentals=0
        ),
        name="prepare_narrow",
    )(tiles_of(grad, rows, D), tiles_of(state, rows, D), first)
    return flat_of(following), first


def other_core(x):
    return lax.ppermute(x, "tensor", [(0, 1), (1, 0)])


BLOCK = 256
EDGE = D // BLOCK
NEAR = EDGE // 2
PACKED = EDGE * NEAR + NEAR
GROUPS = EDGE + 1
MIB = 1024 * 1024


def repeat(count, body, looped):
    if looped:

        def step(i, carry):
            body(i)
            return carry

        lax.fori_loop(0, count, step, 0)
    else:
        for i in range(count):
            body(i)


def each_pair(body, after=None, looped=False):
    def row(i):
        for d in range(NEAR):
            body(i * NEAR + d, i, lax.rem(i + d, EDGE) if looped else (i + d) % EDGE, d == 0)
        if after is not None:
            after(i)

    repeat(EDGE, row, looped)
    for i in range(NEAR):
        body(EDGE * NEAR + i, i, i + NEAR, False)
    if after is not None:
        after(EDGE)


def span(i):
    if isinstance(i, int):
        return pl.ds(i * BLOCK, BLOCK)
    return pl.ds(pl.multiple_of(i * BLOCK, BLOCK), BLOCK)


def group(ref, g):
    return ref.at[pl.ds(g * NEAR, NEAR)]


def rows_of(ref, i):
    return ref.at[span(i), :]


def columns_of(ref, at, width):
    return ref.at[:, pl.ds(at, width)]


def gram_blocks(x, width, out, after, looped=False):
    def body(slot, i, j, diagonal):
        out[slot] = lax.dot_general(
            x[span(i), :width],
            x[span(j), :width],
            (((1,), (1,)), ((), ())),
            preferred_element_type=jnp.float32,
        )

    each_pair(body, after, looped)


def mirror(out, i, j, diagonal, value):
    rounded = value.astype(out.dtype)
    out[span(i), span(j)] = rounded
    if not diagonal:
        out[span(j), span(i)] = rounded.T


def polynomial_blocks(normed, out):
    def body(slot, i, j, diagonal):
        squared = jnp.dot(normed[span(i), :], normed[:, span(j)], preferred_element_type=jnp.float32)
        value = QUINTIC_CUBIC * normed[span(i), span(j)].astype(jnp.float32) + QUINTIC_FIFTH * squared
        mirror(out, i, j, diagonal, value)

    each_pair(body)


def mixed_rows(polynomial, x, width, scale, out, before=None, after=None, looped=False):
    def row(i):
        if before is not None:
            before(i)
        for c in range(0, width, BLOCK):
            product = jnp.dot(
                polynomial[span(i), :], x[:, c : c + BLOCK], preferred_element_type=jnp.float32
            )
            mixed = QUINTIC_LINEAR * x[span(i), c : c + BLOCK].astype(jnp.float32) + product
            out[span(i), c : c + BLOCK] = (mixed * scale).astype(out.dtype)
        if after is not None:
            after(i)

    repeat(EDGE, row, looped)


def column_copies(sources, x, sems):
    copies, at = [], 0
    for k, source in enumerate(sources):
        width = source.shape[1]
        copies.append(pltpu.make_async_copy(source, columns_of(x, at, width), sems.at[k]))
        at += width
    return copies


def start_all(copies):
    for copy in copies:
        copy.start()


def wait_all(copies):
    for copy in copies:
        copy.wait()


def by_kind(flag, narrow, wide, body):
    @pl.when(flag[0] > 0)
    def _():
        body(wide)

    @pl.when(flag[0] <= 0)
    def _():
        body(narrow)


def gram_kernel(flag, *refs):
    parts, (out, x, blocks, in_sems, out_sems) = refs[:-5], refs[-5:]
    copies = column_copies(parts, x, in_sems)

    def send(g):
        pltpu.make_async_copy(group(blocks, g), group(out, g), out_sems.at[g]).start()

    def run(width):
        used = copies[: 1 if width < x.shape[1] else len(copies)]
        start_all(used)
        wait_all(used)
        gram_blocks(x, width, blocks, send, looped=True)

    by_kind(flag, parts[0].shape[1], x.shape[1], run)
    wait_all(
        [
            pltpu.make_async_copy(group(blocks, g), group(out, g), out_sems.at[g])
            for g in range(GROUPS)
        ]
    )


def group_copies(source, target, sems):
    return [
        pltpu.make_async_copy(group(source, g), group(target, g), sems.at[g]) for g in range(GROUPS)
    ]


def middle_kernel(flag, own_in, other_in, *refs):
    parts, refs = refs[:-15], refs[-15:]
    first_out, second_out, packed_out, scale_out = refs[:4]
    own, other, x, mixed, normed, polynomial = refs[4:10]
    own_sems, other_sems, x_sems, mixed_sems, packed_sems = refs[10:]
    narrow, wide = first_out.shape[1], x.shape[1]
    own_copies = group_copies(own_in, own, own_sems)
    other_copies = group_copies(other_in, other, other_sems)
    x_copies = column_copies(parts, x, x_sems)
    for a, b in zip(own_copies, other_copies):
        a.start()
        b.start()
    by_kind(flag, 1, len(x_copies), lambda used: start_all(x_copies[:used]))

    once = jnp.zeros((8, BLOCK), jnp.float32)
    twice = jnp.zeros((8, BLOCK), jnp.float32)
    for g in range(GROUPS):
        own_copies[g].wait()
        other_copies[g].wait()
        for d in range(NEAR):
            slot = g * NEAR + d
            gram = own[slot] + other[slot]
            own[slot] = gram
            squares = jnp.sum((gram * gram).reshape(BLOCK // 8, 8, BLOCK), axis=0)
            if d == 0 and g < EDGE:
                once += squares
            else:
                twice += squares
    total = jnp.full((8, LANE), jnp.sum(once + 2.0 * twice), jnp.float32)
    scale = jnp.sqrt(total) + 1e-06
    scale_out[...] = scale
    inverse = (1.0 / scale)[0:1, 0:1]
    root = (1.0 / jnp.sqrt(scale))[0:1, 0:1]
    each_pair(lambda slot, i, j, diagonal: mirror(normed, i, j, diagonal, own[slot] * inverse))
    polynomial_blocks(normed, polynomial)

    def send(g):
        pltpu.make_async_copy(group(other, g), group(packed_out, g), packed_sems.at[g]).start()

    def run(width):
        used = x_copies[: 1 if width < wide else len(x_copies)]
        wait_all(used)
        mixed_rows(polynomial, x, width, root, mixed)
        sends = [pltpu.make_async_copy(columns_of(mixed, 0, narrow), first_out, mixed_sems.at[0])]
        if width == wide:
            rest = columns_of(mixed, narrow, wide - narrow)
            sends.append(pltpu.make_async_copy(rest, second_out, mixed_sems.at[1]))
        start_all(sends)
        gram_blocks(mixed, width, other, send)
        wait_all(sends)

    by_kind(flag, narrow, wide, run)
    wait_all(group_copies(other, packed_out, packed_sems))


def last_kernel(flag, factor, own_in, other_in, x_in, *refs):
    count = len(refs) - 11
    polynomial_out, outs = refs[0], refs[1:count]
    own, other, x, mixed, normed, polynomial = refs[count : count + 6]
    own_sems, other_sems, x_sem, polynomial_sem, out_sems = refs[count + 6 :]
    own_copies = group_copies(own_in, own, own_sems)
    other_copies = group_copies(other_in, other, other_sems)
    for a, b in zip(own_copies, other_copies):
        a.start()
        b.start()
    x_copy = pltpu.make_async_copy(x_in, x, x_sem)
    heavy = flag[0] > 0

    @pl.when(heavy)
    def _():
        x_copy.start()

    for g in range(GROUPS):
        own_copies[g].wait()
        other_copies[g].wait()
        for d in range(NEAR):
            slot = g * NEAR + d
            i, j = (g, (g + d) % EDGE) if g < EDGE else (d, d + NEAR)
            mirror(normed, i, j, i == j, own[slot] + other[slot])
    polynomial_blocks(normed, polynomial)
    polynomial_copy = pltpu.make_async_copy(polynomial, polynomial_out, polynomial_sem)
    polynomial_copy.start()

    def out_copies(i):
        copies, at = [], 0
        for k, out in enumerate(outs):
            width = out.shape[1]
            source = mixed.at[span(i), pl.ds(at, width)]
            copies.append(pltpu.make_async_copy(source, rows_of(out, i), out_sems.at[k, i]))
            at += width
        return copies

    @pl.when(heavy)
    def _():
        x_copy.wait()
        mixed_rows(
            polynomial,
            x,
            x.shape[1],
            factor[0],
            mixed,
            after=lambda i: start_all(out_copies(i)),
        )
        for i in range(EDGE):
            wait_all(out_copies(i))

    polynomial_copy.wait()


def finish_kernel(factor, polynomial_in, x_in, out, x, mixed, polynomial, x_sem, in_sems, out_sems):
    x_copy = pltpu.make_async_copy(x_in, x, x_sem)
    x_copy.start()

    def in_copy(i):
        return pltpu.make_async_copy(rows_of(polynomial_in, i), rows_of(polynomial, i), in_sems.at[i])

    def out_copy(i):
        target = out.at[span(i), pl.ds(0, x.shape[1])]
        return pltpu.make_async_copy(rows_of(mixed, i), target, out_sems.at[i])

    start_all([in_copy(i) for i in range(EDGE)])
    x_copy.wait()
    mixed_rows(
        polynomial,
        x,
        x.shape[1],
        factor[0],
        mixed,
        before=lambda i: in_copy(i).wait(),
        after=lambda i: out_copy(i).start(),
        looped=True,
    )
    wait_all([out_copy(i) for i in range(EDGE)])


def join_kernel(table, me, own, *refs):
    pick = [table[me[0] * 3 + where] for where in range(3)]
    handed, (given, out, stage, in_sems, out_sems) = refs[:-5], refs[-5:]
    narrow = out.shape[1] - 2 * GRANULE

    def incoming(where, source):
        target = columns_of(stage, where * GRANULE, GRANULE)
        return pltpu.make_async_copy(source, target, in_sems.at[where])

    def outgoing(where):
        at = narrow + where * GRANULE if where < 2 else 0
        source = columns_of(stage, where * GRANULE, GRANULE)
        return pltpu.make_async_copy(source, columns_of(out, at, GRANULE), out_sems.at[where])

    for where in range(3):
        for k in range(1 + len(handed)):
            if where == 2 and k == 0:
                continue
            source = columns_of(own, where * GRANULE, GRANULE) if k == 0 else handed[k - 1]

            @pl.when(pick[where] == k)
            def _():
                incoming(where, source).start()

    for where in range(2):
        incoming(where, columns_of(own, 0, GRANULE)).wait()
        outgoing(where).start()

    @pl.when(pick[2] > 0)
    def _():
        incoming(2, columns_of(own, 0, GRANULE)).wait()
        outgoing(2).start()
        outgoing(2).wait()

    for where in range(2):
        outgoing(where).wait()


def call(kernel, name, scalars, arrays, outs, scratch, limit, flops, small_outs=0, aliases=None):
    moved = sum(x.size * x.dtype.itemsize for x in arrays)
    moved += sum(math.prod(o.shape) * o.dtype.itemsize for o in outs)
    smem = pl.BlockSpec(memory_space=pltpu.SMEM)
    anywhere = pl.BlockSpec(memory_space=pl.ANY)
    vmem = pl.BlockSpec(memory_space=pltpu.VMEM)
    return pl.pallas_call(
        kernel,
        in_specs=[smem] * len(scalars) + [anywhere] * len(arrays),
        out_specs=[anywhere] * (len(outs) - small_outs) + [vmem] * small_outs,
        out_shape=list(outs),
        scratch_shapes=list(scratch),
        input_output_aliases=aliases or {},
        compiler_params=pltpu.CompilerParams(vmem_limit_bytes=limit * MIB),
        cost_estimate=pl.CostEstimate(flops=flops, bytes_accessed=moved, transcendentals=0),
        name=name,
    )(*scalars, *arrays)


def assemble(plan, square_order, swiglu_order, back):
    squares, wides = square_order.shape[0], swiglu_order.shape[0]
    rows, both = back.shape[1:]
    narrow = both - 2 * GRANULE
    wide = narrow + plan.granules * GRANULE
    parts = 1 + plan.passes

    def kernel(
        square_to, wide_to, source, square_out, wide_out, square_stage, wide_stage, *sems
    ):
        square_in, wide_in, square_sems, wide_sems = sems
        square_copies = [
            [
                pltpu.make_async_copy(
                    source.at[plan.light[j], :, pl.ds(0, narrow)], square_stage.at[j], square_in.at[j]
                )
            ]
            for j in range(squares)
        ]
        wide_copies = []
        for j in range(wides):
            moves = [(plan.heavy[j], 0, 0, both)]
            for b in range(2, plan.granules):
                chip, at = plan.column[(j, b)]
                moves.append((chip, at, narrow + b * GRANULE, GRANULE))
            wide_copies.append(
                [
                    pltpu.make_async_copy(
                        source.at[chip, :, pl.ds(at, width)],
                        wide_stage.at[j, :, pl.ds(to, width)],
                        wide_in.at[j * parts + n],
                    )
                    for n, (chip, at, to, width) in enumerate(moves)
                ]
            )
        for slot in square_copies + wide_copies:
            start_all(slot)
        outs = []
        for copies, stage, out, order, out_sems in (
            (square_copies, square_stage, square_out, square_to, square_sems),
            (wide_copies, wide_stage, wide_out, wide_to, wide_sems),
        ):
            for j, slot in enumerate(copies):
                wait_all(slot)
                outs.append(pltpu.make_async_copy(stage.at[j], out.at[order[j]], out_sems.at[j]))
                outs[-1].start()
        wait_all(outs)

    smem = pl.BlockSpec(memory_space=pltpu.SMEM)
    anywhere = pl.BlockSpec(memory_space=pl.ANY)
    shapes = [(squares, rows, narrow), (wides, rows, wide)]
    dma = pltpu.SemaphoreType.DMA
    return pl.pallas_call(
        kernel,
        in_specs=[smem, smem, anywhere],
        out_specs=[anywhere, anywhere],
        out_shape=[jax.ShapeDtypeStruct(shape, jnp.bfloat16) for shape in shapes],
        scratch_shapes=[pltpu.VMEM(shape, jnp.bfloat16) for shape in shapes]
        + [dma((squares,)), dma((wides * parts,)), dma((squares,)), dma((wides,))],
        compiler_params=pltpu.CompilerParams(vmem_limit_bytes=12 * MIB),
        name="assemble",
    )(square_order, swiglu_order, back)


def spread(known, chips, steps):
    for step in steps:
        known = known + lax.ppermute(known, "dp", [(s, s ^ step) for s in range(chips)])
    return known


def lookup(table, positions):
    matches = positions[:, None] == jnp.arange(table.shape[0], dtype=jnp.int32)[None, :]
    return jnp.sum(jnp.where(matches, table[None, :], 0), axis=1)


def local(
    square_grad,
    square_state,
    swiglu_grad,
    swiglu_state,
    square_order,
    swiglu_order,
    owners,
    vector_values,
    vector_grad,
    vector_first,
    vector_second,
    embed_values,
    embed_grad,
    embed_first,
    embed_second,
    embed_ranges,
):
    chips = lax.axis_size("dp")
    cores = lax.axis_size("tensor")
    chip = lax.axis_index("dp")
    square_count = square_grad.shape[0]
    swiglu_count = swiglu_grad.shape[0]
    chip_rows = D // chips
    narrow = D // cores
    plan = Plan(chips, cores, square_count, swiglu_count)

    swiglu_next, first_send, second_send = prepare_wide(
        plan, chips, cores, swiglu_grad, swiglu_state
    )
    square_next, first_send = prepare_narrow(
        plan, chips, cores, square_grad, square_state, first_send
    )
    both = ("dp", "tensor")
    second_got = lax.all_to_all(
        second_send.reshape(D, 2 * GRANULE), both, split_axis=0, concat_axis=0, tiled=True
    )
    first_got = lax.all_to_all(
        first_send.reshape(D, narrow), both, split_axis=0, concat_axis=0, tiled=True
    )
    heavy_here = jnp.asarray(plan.is_heavy)[chip]
    pieces = [second_got[:, :GRANULE], second_got[:, GRANULE:]]
    relayed = []
    for p in range(plan.passes):
        pick = jnp.asarray(plan.slot_in_pass[p])[chip]
        pairs = [(plan.take[p][k], plan.heavy[k]) for k in range(swiglu_count)]
        relayed.append(lax.ppermute(jnp.where(pick, pieces[1], pieces[0]), "dp", pairs))
    flag = heavy_here.astype(jnp.int32).reshape(1)
    factor = jnp.where(heavy_here, jnp.float32(math.sqrt(FF)), jnp.float32(math.sqrt(D))).reshape(1)
    packed = jax.ShapeDtypeStruct((PACKED, BLOCK, BLOCK), jnp.float32)
    whole_square = jax.ShapeDtypeStruct((D, D), jnp.bfloat16)
    first_shape = jax.ShapeDtypeStruct((D, narrow), jnp.bfloat16)
    extra = plan.granules * GRANULE
    second_shape = jax.ShapeDtypeStruct((D, extra), jnp.bfloat16)
    square_buffer = pltpu.VMEM((D, D), jnp.bfloat16)
    packed_buffer = pltpu.VMEM(packed.shape, jnp.float32)
    matrix_buffer = pltpu.VMEM((D, narrow + extra), jnp.bfloat16)
    first_buffer = pltpu.VMEM((D, narrow), jnp.bfloat16)
    second_buffer = pltpu.VMEM((D, extra), jnp.bfloat16)
    sems = lambda *shape: pltpu.SemaphoreType.DMA(shape)
    half = D * D * (narrow + extra)
    parts = [first_got, second_got, *relayed]
    (own,) = call(
        gram_kernel,
        "gram",
        [flag],
        parts,
        [packed],
        [matrix_buffer, packed_buffer, sems(len(parts)), sems(GROUPS)],
        15,
        half,
    )
    first_mid, second_mid, own_mid, scale = call(
        middle_kernel,
        "middle",
        [flag],
        [own, other_core(own), *parts],
        [first_shape, second_shape, packed, jax.ShapeDtypeStruct((8, LANE), jnp.float32)],
        [packed_buffer] * 2
        + [matrix_buffer] * 2
        + [square_buffer] * 2
        + [sems(GROUPS), sems(GROUPS), sems(len(parts)), sems(2), sems(GROUPS)],
        37,
        3 * half + D * D * D,
        small_outs=1,
    )
    steps = [1 << n for n in range(chips.bit_length() - 1)]
    logs = jnp.where(
        jnp.arange(chips, dtype=jnp.int32) == chip, 0.5 * jnp.log(scale[0, 0]), 0.0
    )
    logs = spread(logs, chips, steps[len(steps) // 2 :])
    other_mid, logs = lax.optimization_barrier((other_core(own_mid), logs))
    piece_shape = jax.ShapeDtypeStruct((D, GRANULE), jnp.bfloat16)
    pair_shape = jax.ShapeDtypeStruct((D, 2 * GRANULE), jnp.bfloat16)
    polynomial, kept, *rest = call(
        last_kernel,
        "last",
        [flag, factor],
        [own_mid, other_mid, second_mid],
        [whole_square, pair_shape] + [piece_shape] * plan.passes,
        [packed_buffer] * 2
        + [second_buffer] * 2
        + [square_buffer] * 2
        + [sems(GROUPS), sems(GROUPS), sems(), sems(), sems(1 + plan.passes, EDGE)],
        56,
        D * D * D + 2 * D * D * extra,
    )
    handed = []
    for p in range(plan.passes):
        pairs = [(plan.heavy[k], plan.back[p][k]) for k in range(swiglu_count)]
        handed.append(lax.ppermute(rest[p], "dp", pairs))
    back_shape = jax.ShapeDtypeStruct((D, narrow + 2 * GRANULE), jnp.bfloat16)
    (back_out,) = call(
        finish_kernel,
        "finish",
        [factor],
        [polynomial, first_mid],
        [back_shape],
        [first_buffer] * 2 + [square_buffer, sems(), sems(EDGE), sems(EDGE)],
        56,
        2 * D * D * narrow,
    )
    logs, back_out = lax.optimization_barrier((logs, back_out))
    logs = spread(logs, chips, steps[: len(steps) // 2])
    (back_out,) = call(
        join_kernel,
        "join",
        [jnp.asarray(plan.choice.reshape(-1)), chip.reshape(1)],
        [kept, *handed, back_out],
        [back_shape],
        [pltpu.VMEM((D, 3 * GRANULE), jnp.bfloat16), sems(3), sems(3)],
        56,
        0,
        aliases={3 + plan.passes: 0},
    )
    back_out, logs = lax.optimization_barrier((back_out, logs))
    back = lax.all_to_all(
        back_out.reshape(chips, chip_rows, -1), "dp", split_axis=0, concat_axis=0, tiled=True
    )
    square_update, swiglu_update = assemble(plan, square_order, swiglu_order, back)

    slot_chips = np.array(plan.light + plan.heavy, np.int32)
    slot_owner = jnp.concatenate(
        [lookup(owners[:square_count], square_order), lookup(owners[square_count:], swiglu_order)]
    )
    slot_logs = logs[slot_chips]
    owner_norms = jnp.sum(jnp.where(slot_owner == chip, slot_logs, 0.0)).reshape(1)

    vector_step, first_vector, second_vector = adamw_terms(
        vector_values, vector_grad, vector_first, vector_second
    )
    embed_rows = embed_values.shape[0]
    row_numbers = chip * embed_rows + jnp.arange(embed_rows, dtype=jnp.int32)
    inside = (row_numbers[:, None] >= embed_ranges[None, :, 0]) & (
        row_numbers[:, None] < embed_ranges[None, :, 1]
    )
    row_live = jnp.sum(inside.astype(jnp.int32), axis=1) > 0
    direction, first_next, second_next = adamw_terms(
        embed_values, embed_grad, embed_first, embed_second
    )
    embed_step = jnp.where(row_live[:, None], direction, 0.0)
    first_embed = jnp.where(row_live[:, None], first_next, embed_first)
    second_embed = jnp.where(row_live[:, None], second_next, embed_second)
    return (
        square_next,
        swiglu_next,
        square_update,
        swiglu_update,
        owner_norms,
        vector_step,
        first_vector,
        second_vector,
        embed_step,
        first_embed,
        second_embed,
    )


def solution(mesh):
    flat = P(None, ("dp", "tensor"))
    vector = P(("dp", "tensor"))
    tile = P("dp", "tensor")
    update = P(None, "dp", "tensor")
    return jax.shard_map(
        local,
        mesh=mesh,
        in_specs=(flat,) * 4 + (P(),) * 3 + (vector,) * 4 + (tile,) * 4 + (P(),),
        out_specs=(flat, flat, update, update, P("dp")) + (vector,) * 3 + (tile,) * 3,
        check_vma=False,
    )
```
